128 devices in a mesh: clu: 128 (over x, z, y, core).
Axes of the slice: x: 4, y: 4, z: 4, core: 2. Of those that a mesh axis runs over, the one named last changes fastest.
Arguments:
- charges: bfloat16 [1024, 32, 256], P('clu'), may hold values from -6 to 6
- basis: bfloat16 [1024, 96, 256], P('clu'), may hold values from -0.375 to 0.375
- transfer: bfloat16 [1024, 96, 96], P('clu'), may hold values from -0.4375 to 0.4375
- near_field: bfloat16 [1024, 3, 256, 256], P('clu'), may hold values from -0.21875 to 0.21875
- coupling: bfloat16 [16384, 96, 96], P('clu'), may hold values from -0.625 to 0.625
- ranks: int32 [1536], P('clu'), may hold values from 32 to 96, as said below
- block_source: int32 [16384], P('clu'), may hold values from 0 to 1535, as said below
- block_target: int32 [16384], P('clu'), may hold values from 0 to 1535, as said below
Outputs:
- first: bfloat16 [1024, 32, 256], P('clu')
- second: bfloat16 [1024, 32, 256], P('clu')
The draws below stay inside these ranges and needn't reach their ends.
Inputs may be any that keep to these rules, and one draw needn't show every extreme that they name: `ranks`: each cluster's rank; 96 and 32 are both taken. `block_source`: global cluster numbers; a block's source and target are both leaves or both parents. Among the blocks of one device, at most 2 have their source on any one device, and exactly 2 for some device. `block_target`: global cluster numbers of the same level as the block's source. Among the blocks of one device, at most 2 have their target on any one device, and exactly 2 for some device.
All inputs are finite; a program needn't handle non-finite values.
Results may differ from the reference program's by a relative error of at most 0.025.
Values may be sent and summed in bfloat16 or wider, within the bound.
A program may use at most 128 MiB of HBM per device.

```python
import jax
import jax.numpy as jnp
from jax import lax

LEAF = 256
RMAX = 96
RHS = 32
LEAF_DEV = 8
BLK_DEV = 128
DEVS = 128
CL_DEV = 12
CAP = 2
LEAVES = 1024
CLUSTERS = 1536
BLOCKS = 16384


def peer_lists(key):
    keys = jax.random.split(key, DEVS)

    def one_device(subkey):
        key_a, key_b, key_c = jax.random.split(subkey, 3)
        leading = jax.random.randint(key_a, (), 0, DEVS)
        others = (leading + 1 + jnp.arange((DEVS - 1) * CAP) // CAP) % DEVS
        picked = others[jax.random.permutation(key_b, (DEVS - 1) * CAP)[:BLK_DEV - CAP]]
        joined = jnp.concatenate([jnp.full((CAP,), leading, jnp.int32), picked.astype(jnp.int32)])
        return joined[jax.random.permutation(key_c, BLK_DEV)]
    return jax.vmap(one_device)(keys)


def first_match(devices, wanted):
    return jnp.argmax((devices.ravel() == wanted).astype(jnp.int32)).astype(jnp.int32)


def routing(key):
    keys = jax.random.split(key, 7)
    source_dev = peer_lists(keys[0])
    target_dev = peer_lists(keys[1])
    low_src = first_match(source_dev, 0)
    high_src = first_match(source_dev, DEVS - 1)
    low_tgt = first_match(target_dev, 0)
    high_tgt = first_match(target_dev, DEVS - 1)
    level = jax.random.randint(keys[2], (DEVS * BLK_DEV,), 0, 2)
    level = level.at[low_src].set(0).at[low_tgt].set(0).at[high_src].set(1).at[high_tgt].set(1)
    source_loc = jnp.where(level == 0, jax.random.randint(keys[3], (DEVS * BLK_DEV,), 0, LEAF_DEV), LEAF_DEV + jax.random.randint(keys[4], (DEVS * BLK_DEV,), 0, LEAF_DEV // 2))
    target_loc = jnp.where(level == 0, jax.random.randint(keys[5], (DEVS * BLK_DEV,), 0, LEAF_DEV), LEAF_DEV + jax.random.randint(keys[6], (DEVS * BLK_DEV,), 0, LEAF_DEV // 2))
    source_loc = source_loc.at[low_src].set(0).at[high_src].set(CL_DEV - 1)
    target_loc = target_loc.at[low_tgt].set(0).at[high_tgt].set(CL_DEV - 1)
    source_loc = source_loc.reshape(DEVS, BLK_DEV).astype(jnp.int32)
    target_loc = target_loc.reshape(DEVS, BLK_DEV).astype(jnp.int32)
    return (source_dev, source_loc, target_dev, target_loc)


def draw_ranks(key, part):
    key = jax.random.fold_in(key, 11)
    values = jax.random.randint(key, (CLUSTERS,), RMAX // 3, RMAX + 1)
    return values.at[0].set(RMAX).at[1].set(RMAX // 3).astype(jnp.int32)


def draw_block_source(key, part):
    source_dev, source_loc, target_dev, target_loc = routing(key)
    return (source_dev * CL_DEV + source_loc).ravel().astype(jnp.int32)


def draw_block_target(key, part):
    source_dev, source_loc, target_dev, target_loc = routing(key)
    return (target_dev * CL_DEV + target_loc).ravel().astype(jnp.int32)


def shard_levels(stream_key, dims, cuts, least, high):
    def one(position, parts):
        draws = jax.random.uniform(jax.random.fold_in(jax.random.fold_in(stream_key, 6), position), (parts,), jnp.float32, least / len(cuts), high / len(cuts))
        return jnp.repeat(jnp.exp(draws), dims[position] // parts).reshape((-1,) + (1,) * (len(dims) - position - 1))

    level = one(*cuts[0])
    for cut in cuts[1:]:
        level = level * one(*cut)
    return level


def noise(own_key, shape, spread, most, cuts=(), dtype=jnp.bfloat16):
    entries = jax.random.normal(own_key, shape, jnp.float32) * spread
    if len(cuts) > 0:
        entries = shard_levels(own_key, shape, cuts, -0.22, 0.18) * entries
    return jnp.clip(entries, min=-most, max=most).astype(dtype)


def setup_inputs(seed: int = 0) -> dict:
    key_list = jax.random.split(jax.random.key(seed), 9)
    charges = noise(key_list[0], (LEAVES, RHS, LEAF), 1.0, 6.0, ((0, 128),))
    basis = noise(key_list[1], (LEAVES, RMAX, LEAF), LEAF ** -0.5, 0.375, ((0, 128),))
    transfer = noise(key_list[2], (LEAVES, RMAX, RMAX), (2 * RMAX) ** -0.5, 0.4375, ((0, 128),))
    near_field = noise(key_list[3], (LEAVES, 3, LEAF, LEAF), (3 * LEAF) ** -0.5, 0.21875, ((0, 128),))
    coupling = noise(key_list[4], (BLOCKS, RMAX, RMAX), RMAX ** -0.5, 0.625, ((0, 128),))
    ranks = draw_ranks(jax.random.fold_in(key_list[8], 71), 0)
    block_source = draw_block_source(jax.random.fold_in(key_list[8], 71), 0)
    block_target = draw_block_target(jax.random.fold_in(key_list[8], 71), 0)
    return dict(charges=charges, basis=basis, transfer=transfer, near_field=near_field, coupling=coupling, ranks=ranks, block_source=block_source, block_target=block_target)


def rank_table(ranks):
    return (jnp.arange(RMAX)[None, :] < ranks[:, None]).astype(jnp.float32)


def apply_matrix(field_in, basis, transfer, near_field, coupling, masks, block_source, block_target):
    highest = lax.Precision.HIGHEST
    grouped = masks.reshape(DEVS, CL_DEV, RMAX)
    leaf_mask = grouped[:, :LEAF_DEV].reshape(LEAVES, RMAX)
    parent_mask = grouped[:, LEAF_DEV:].reshape(LEAVES // 2, RMAX)
    basis_wide = basis.astype(jnp.float32)
    leaf_coeff = jnp.einsum('irb,ikb->irk', field_in.astype(jnp.float32), basis_wide, precision=highest)
    leaf_coeff = (leaf_coeff * leaf_mask[:, None, :]).astype(jnp.bfloat16)
    kids = leaf_coeff.reshape(LEAVES // 2, 2, RHS, RMAX).astype(jnp.float32)
    pairs = transfer.reshape(LEAVES // 2, 2, RMAX, RMAX).astype(jnp.float32)
    parent_coeff = jnp.einsum('qcrk,qckp->qrp', kids, pairs, precision=highest)
    parent_coeff = (parent_coeff * parent_mask[:, None, :]).astype(jnp.bfloat16)
    coeffs = jnp.concatenate([leaf_coeff.reshape(DEVS, LEAF_DEV, RHS, RMAX),
                              parent_coeff.reshape(DEVS, LEAF_DEV // 2, RHS, RMAX)], axis=1)
    coeffs = coeffs.reshape(CLUSTERS, RHS, RMAX)

    def add_blocks(index, total):
        start = (index * BLK_DEV).astype(jnp.int32)
        sources = lax.dynamic_slice_in_dim(block_source, start, BLK_DEV)
        targets = lax.dynamic_slice_in_dim(block_target, start, BLK_DEV)
        mats = lax.dynamic_slice_in_dim(coupling, start, BLK_DEV).astype(jnp.float32)
        terms = jnp.einsum('jrk,jkp->jrp', coeffs[sources].astype(jnp.float32), mats, precision=highest)
        return total.at[targets].add(terms)

    field = lax.fori_loop(0, DEVS, add_blocks, jnp.zeros((CLUSTERS, RHS, RMAX), jnp.float32))
    field = (field * masks[:, None, :]).astype(jnp.bfloat16).reshape(DEVS, CL_DEV, RHS, RMAX)
    leaf_field = field[:, :LEAF_DEV].reshape(LEAVES, RHS, RMAX).astype(jnp.float32)
    parent_field = field[:, LEAF_DEV:].reshape(LEAVES // 2, RHS, RMAX).astype(jnp.float32)
    downward = jnp.einsum('qrp,qckp->qcrk', parent_field, pairs, precision=highest).reshape(LEAVES, RHS, RMAX)
    leaf_total = ((leaf_field + downward) * leaf_mask[:, None, :]).astype(jnp.bfloat16)
    result = jnp.einsum('irk,ikb->irb', leaf_total.astype(jnp.float32), basis_wide, precision=highest)
    padded = jnp.pad(field_in.astype(jnp.float32), ((1, 1), (0, 0), (0, 0)))
    for offset in range(3):
        result = result + jnp.einsum('irb,iba->ira', padded[offset:offset + LEAVES],
                                     near_field[:, offset].astype(jnp.float32), precision=highest)
    return result.astype(jnp.bfloat16)


def reference(charges, basis, transfer, near_field, coupling, ranks, block_source, block_target):
    masks = rank_table(ranks)
    first = apply_matrix(charges, basis, transfer, near_field, coupling, masks, block_source, block_target)
    second = apply_matrix(first, basis, transfer, near_field, coupling, masks, block_source, block_target)
    return (first, second)
```

```python
import jax
import jax.numpy as jnp
from jax import lax
from jax.experimental import pallas as pl
from jax.experimental.pallas import tpu as pltpu
from jax.sharding import PartitionSpec as P

MESH = pl.DeviceIdType.MESH
F32 = jnp.float32
BF16 = jnp.bfloat16
RMAX = 96
RHS = 32
LEAF = 256
STRIDE = {"x": 32, "z": 8, "y": 2}
ROUTES = (("y", "x", "z"), ("z", "y", "x"), ("x", "z", "y"))
WIDE = 1024
HALF = WIDE // 2
GROUPS = 8
SLOTS = 32
BLOCKS = 128

G1, G2, EX0, EX1, R2, R1 = 0, 4, 8, 17, 26, 30
PER_ROUTE = 34
HALO = 3 * PER_ROUTE
COPIES = HALO + 2


def dot(a, b):
    return jnp.dot(a, b, preferred_element_type=F32)


def dot_nt(a, b):
    return lax.dot_general(a, b, (((1,), (1,)), ((), ())), preferred_element_type=F32)


def kernel(
    charges, basis, transfer, near_hbm, coupling_hbm, mask, lists, source_slot, target_slot,
    out,
    near, coupling, v, near_sum, lists_in, pick, scatter, unpick, place,
    small, big_in, big_out, products, gathered, outbox, inbox, passing,
    total, partial, half_out, half_in, full_out, full_in,
    half1_out, half1_in, full1_out, full1_in,
    send_sem, recv_sem, list_send, list_recv, load_sem,
):
    me = lax.axis_index("clu")
    devices = 128
    core = lax.rem(me, 2)
    pos = {a: lax.rem(lax.div(me, s), 4) for a, s in STRIDE.items()}

    def at(axis, step):
        return lax.rem(pos[axis] + (step + 4), 4)

    def near_by(axis, step, other=0):
        base = me + (at(axis, step) - pos[axis]) * STRIDE[axis]
        return base + (1 - 2 * core) if other else base

    sibling = me + (1 - 2 * core)
    before = lax.rem(me + devices - 1, devices)
    after = lax.rem(me + 1, devices)

    barrier = pltpu.get_barrier_semaphore()
    peers = [sibling, before, after]
    for axis in STRIDE:
        for step in (1, -1, 2):
            for other in (0, 1):
                peers.append(near_by(axis, step, other))
    for peer in peers:
        pl.semaphore_signal(barrier, inc=1, device_id=(peer,), device_id_type=MESH)

    load_near = pltpu.make_async_copy(near_hbm, near, load_sem.at[0])
    load_coupling = pltpu.make_async_copy(coupling_hbm, coupling, load_sem.at[1])
    load_near.start()
    load_coupling.start()
    v[0, 1:9] = charges[...]
    small[...] = jnp.zeros_like(small)

    lane = lax.broadcasted_iota(jnp.int32, (16, 128), 1)

    def merge(row, extra, u, width):
        lanes = lax.broadcasted_iota(jnp.int32, (width, 128), 1)
        return jnp.where(lanes < RMAX, row, pltpu.roll(extra, RMAX - 32 * u, 1))

    def fourth(parts, width):
        lanes = lax.broadcasted_iota(jnp.int32, (width, 128), 1)
        rolled = [pltpu.roll(part, 32 + 32 * u, 1) for u, part in enumerate(parts)]
        return jnp.where(lanes < 32, rolled[0], jnp.where(lanes < 64, rolled[1], rolled[2]))

    def coefficients(p):
        for q in range(4):
            total_q = jnp.zeros((RHS, RMAX), F32)
            for i in (2 * q, 2 * q + 1):
                c = dot_nt(v[p, 1 + i], basis[i]) * mask[i : i + 1, :RMAX]
                c = c.astype(BF16)
                small[pl.ds(i, RHS, stride=16), 0:RMAX] = c.astype(F32)
                total_q = total_q + dot(c, transfer[i])
            c = (total_q * mask[8 + q : 9 + q, :RMAX]).astype(BF16)
            small[pl.ds(8 + q, RHS, stride=16), 0:RMAX] = c.astype(F32)
        for u, (first, second, _) in enumerate(ROUTES):
            where = pos[second] * 4 + pos[first]
            for g in range(8):
                row = small[(4 * g + u) * 16 : (4 * g + u + 1) * 16, :]
                extra = small[(4 * g + 3) * 16 : (4 * g + 4) * 16, :]
                gathered[p, u, where, :, g * 128 : (g + 1) * 128] = merge(row, extra, u, 16).astype(BF16)

    def near_part(p, lo, hi):
        def body(i, carry):
            s = dot(v[p, i], near[i, 0])
            s = s + dot(v[p, i + 1], near[i, 1])
            s = s + dot(v[p, i + 2], near[i, 2])
            near_sum[i] = s
            return carry

        lax.fori_loop(lo, hi, body, 0)

    list_copies = []
    for u, (_, _, axis) in enumerate(ROUTES):
        mine = pos[axis] * 2 + core
        targets = [(near_by(axis, s, o), at(axis, s) * 2 + (1 - core if o else core))
                   for s in (1, -1, 2) for o in (0, 1)]
        targets.append((sibling, pos[axis] * 2 + 1 - core))
        for k, (device, group) in enumerate(targets):
            list_copies.append(pltpu.make_async_remote_copy(
                src_ref=lists.at[u, group], dst_ref=lists_in.at[u, mine],
                send_sem=list_send.at[u * 7 + k], recv_sem=list_recv.at[u * 7 + k],
                device_id=(device,), device_id_type=MESH))

    def make_selectors():
        rows = lax.broadcasted_iota(jnp.int32, (256, 256), 0)
        for u, (_, _, axis) in enumerate(ROUTES):
            mine = pos[axis] * 2 + core
            lists_in[u, mine] = lists[u, mine]
            both = lists_in[u, 0]
            for q in range(1, 8):
                both = jnp.maximum(both, lists_in[u, q])
            hit = jnp.where(rows == both[0:1, :], 1.0, 0.0).astype(F32)
            pick[u] = jnp.transpose(hit, (1, 0)).astype(BF16)
            scatter[u] = jnp.where(rows == both[1:2, :], 1.0, 0.0).astype(BF16)
            lanes = lax.broadcasted_iota(jnp.int32, (128, 256), 1)
            unpick[u] = jnp.where(lanes == source_slot[:, u : u + 1], 1.0, 0.0).astype(BF16)
            slots = lax.broadcasted_iota(jnp.int32, (256, 128), 0)
            place[u] = jnp.where(slots == target_slot[u : u + 1, :], 1.0, 0.0).astype(BF16)

    coefficients(0)
    pl.semaphore_wait(barrier, len(peers))

    def product(p, carry):
        started = []

        def remote(k, src, dst, device):
            copy = pltpu.make_async_remote_copy(
                src_ref=src, dst_ref=dst, send_sem=send_sem.at[p, k], recv_sem=recv_sem.at[p, k],
                device_id=(device,), device_id_type=MESH)
            started.append(copy)
            copy.start()
            return copy

        halo = [
            remote(HALO, v.at[p, 1], v.at[p, 9], before),
            remote(HALO + 1, v.at[p, 8], v.at[p, 0], after),
        ]

        ring = []
        for u, (axis, second, _) in enumerate(ROUTES):
            base = u * PER_ROUTE + G1
            own = gathered.at[p, u, pos[second] * 4 + pos[axis]]
            ring.append((remote(base, own, own, near_by(axis, 1)), remote(base + 1, own, own, near_by(axis, -1))))

        @pl.when(p == 0)
        def _():
            for copy in list_copies:
                copy.start()

        later = []
        for u, (axis, second, _) in enumerate(ROUTES):
            base = u * PER_ROUTE + G1
            ring[u][0].wait_recv()
            left = gathered.at[p, u, pos[second] * 4 + at(axis, -1), :, pl.ds(0, HALF)]
            a = remote(base + 2, left, left, near_by(axis, 1))
            ring[u][1].wait_recv()
            right = gathered.at[p, u, pos[second] * 4 + at(axis, 1), :, pl.ds(HALF, HALF)]
            later.append((a, remote(base + 3, right, right, near_by(axis, -1))))

        ring = []
        for u, (_, axis, _) in enumerate(ROUTES):
            base = u * PER_ROUTE + G2
            later[u][0].wait_recv()
            later[u][1].wait_recv()
            own = gathered.at[p, u, pl.ds(pos[axis] * 4, 4)]
            ring.append((remote(base, own, own, near_by(axis, 1)), remote(base + 1, own, own, near_by(axis, -1))))

        @pl.when(p == 0)
        def _():
            for copy in list_copies:
                copy.wait()
            make_selectors()
            load_near.wait()
            load_coupling.wait()

        later = []
        for u, (_, axis, _) in enumerate(ROUTES):
            base = u * PER_ROUTE + G2
            ring[u][0].wait_recv()
            left = gathered.at[p, u, pl.ds(at(axis, -1) * 4, 2)]
            a = remote(base + 2, left, left, near_by(axis, 1))
            ring[u][1].wait_recv()
            right = gathered.at[p, u, pl.ds(at(axis, 1) * 4 + 2, 2)]
            later.append((a, remote(base + 3, right, right, near_by(axis, -1))))

        def exchange_start(way, u):
            axis = ROUTES[u][2]
            base = u * PER_ROUTE + (EX1 if way else EX0)
            box, to, via = outbox.at[p, way, u], inbox.at[p, way, u], passing.at[p, way, u]
            mine = to.at[pos[axis] * 2 + core]
            fwd = [remote(base + 4, box.at[at(axis, 2) * 2 + core], via.at[0], near_by(axis, 1)),
                   remote(base + 5, box.at[at(axis, 2) * 2 + 1 - core], via.at[1], near_by(axis, -1))]
            direct = []
            for s, step in enumerate((1, -1)):
                for o in (0, 1):
                    group = at(axis, step) * 2 + (1 - core if o else core)
                    direct.append(remote(base + 2 * s + o, box.at[group], mine, near_by(axis, step, o)))
            direct.append(remote(base + 8, box.at[pos[axis] * 2 + 1 - core], mine, sibling))
            inbox[p, way, u, pos[axis] * 2 + core] = outbox[p, way, u, pos[axis] * 2 + core]
            return fwd, direct

        def exchange_pass(way, u, fwd, direct):
            axis = ROUTES[u][2]
            base = u * PER_ROUTE + (EX1 if way else EX0)
            to, via = inbox.at[p, way, u], passing.at[p, way, u]
            fwd[0].wait_recv()
            direct.append(remote(base + 6, via.at[0], to.at[at(axis, -1) * 2 + core], near_by(axis, 1)))
            fwd[1].wait_recv()
            direct.append(remote(base + 7, via.at[1], to.at[at(axis, 1) * 2 + core], near_by(axis, -1, 1)))

        flight = []
        for u in range(3):
            later[u][0].wait_recv()
            later[u][1].wait_recv()

            def picks(n, carry, u=u):
                cols = pl.ds(pl.multiple_of(n * 256, 256), 256)
                rows = gathered[p, u, :, :, cols].reshape(256, 256)
                outbox[p, 0, u, :, :, cols] = dot(pick[u], rows).astype(BF16).reshape(GROUPS, SLOTS, 256)
                return carry

            lax.fori_loop(0, 4, picks, 0)
            flight.append(exchange_start(0, u))

        halo[0].wait_recv()
        halo[1].wait_recv()
        v[p, 0] = (v[p, 0].astype(F32) * (me > 0).astype(F32)).astype(BF16)
        v[p, 9] = (v[p, 9].astype(F32) * (me < devices - 1).astype(F32)).astype(BF16)
        near_part(p, 0, 2)
        for u in range(3):
            exchange_pass(0, u, *flight[u])
        near_part(p, 2, 6)
        for u in range(3):
            for copy in flight[u][1]:
                copy.wait_recv()

        def unpicks(n, carry):
            cols = pl.ds(pl.multiple_of(n * 256, 256), 256)
            parts = [dot(unpick[u], inbox[p, 0, u, :, :, cols].reshape(256, 256)) for u in range(3)]
            for k in range(2):
                g = 2 * n + k
                sides = [part[:, k * 128 : (k + 1) * 128] for part in parts]
                for u in range(3):
                    big_in[pl.ds(pl.multiple_of((4 * g + u) * 128, 128), 128), :] = sides[u]
                big_in[pl.ds(pl.multiple_of((4 * g + 3) * 128, 128), 128), :] = fourth(sides, 128)
            return carry

        lax.fori_loop(0, 4, unpicks, 0)

        def blocks(b, carry):
            for k in range(8):
                j = b * 8 + k
                x = big_in[pl.ds(j, RHS, stride=BLOCKS), 0:RMAX].astype(BF16)
                big_out[pl.ds(j, RHS, stride=BLOCKS), 0:RMAX] = dot(x, coupling[j])
            return carry

        lax.fori_loop(0, BLOCKS // 8, blocks, 0)

        def packs(g, carry):
            cols = pl.ds(pl.multiple_of(g * 128, 128), 128)
            extra = big_out[pl.ds(pl.multiple_of((4 * g + 3) * 128, 128), 128), :]
            for u in range(3):
                row = big_out[pl.ds(pl.multiple_of((4 * g + u) * 128, 128), 128), :]
                products[u, :, cols] = merge(row, extra, u, 128).astype(BF16)
            return carry

        lax.fori_loop(0, 8, packs, 0)

        flight = []
        for u in range(3):
            def places(n, carry, u=u):
                cols = pl.ds(pl.multiple_of(n * 256, 256), 256)
                sent = dot(place[u], products[u, :, cols]).astype(BF16)
                outbox[p, 1, u, :, :, cols] = sent.reshape(GROUPS, SLOTS, 256)
                return carry

            lax.fori_loop(0, 4, places, 0)
            flight.append(exchange_start(1, u))
        for u in range(3):
            exchange_pass(1, u, *flight[u])
        near_part(p, 6, 8)

        first_half = []
        for u, (_, axis, _) in enumerate(ROUTES):
            base = u * PER_ROUTE + R2
            for copy in flight[u][1]:
                copy.wait_recv()

            def sums(n, carry, u=u):
                cols = pl.ds(pl.multiple_of(n * 256, 256), 256)
                rows = inbox[p, 1, u, :, :, cols].reshape(256, 256)
                total[u, :, :, cols] = dot(scatter[u], rows).reshape(4, 64, 256)
                return carry

            lax.fori_loop(0, 4, sums, 0)
            far = at(axis, 2)
            half_out[p, u, 0] = total[u, far, :, 0:HALF].astype(BF16)
            half_out[p, u, 1] = total[u, far, :, HALF:WIDE].astype(BF16)
            first_half.append((
                remote(base, half_out.at[p, u, 0], half_in.at[p, u, 0], near_by(axis, 1)),
                remote(base + 1, half_out.at[p, u, 1], half_in.at[p, u, 1], near_by(axis, -1))))
        second_half = []
        for u, (_, axis, _) in enumerate(ROUTES):
            base = u * PER_ROUTE + R2
            up, down = at(axis, 1), at(axis, -1)
            first_half[u][0].wait_recv()
            full_out[p, u, 0, :, 0:HALF] = (total[u, up, :, 0:HALF] + half_in[p, u, 0].astype(F32)).astype(BF16)
            full_out[p, u, 0, :, HALF:WIDE] = total[u, up, :, HALF:WIDE].astype(BF16)
            a = remote(base + 2, full_out.at[p, u, 0], full_in.at[p, u, 0], near_by(axis, 1))
            first_half[u][1].wait_recv()
            full_out[p, u, 1, :, 0:HALF] = total[u, down, :, 0:HALF].astype(BF16)
            full_out[p, u, 1, :, HALF:WIDE] = (
                total[u, down, :, HALF:WIDE] + half_in[p, u, 1].astype(F32)).astype(BF16)
            second_half.append((a, remote(base + 3, full_out.at[p, u, 1], full_in.at[p, u, 1], near_by(axis, -1))))

        first_half = []
        for u, (axis, second, _) in enumerate(ROUTES):
            base = u * PER_ROUTE + R1
            second_half[u][0].wait_recv()
            second_half[u][1].wait_recv()
            for k in range(4):
                rows = slice(16 * k, 16 * k + 16)
                partial[u, k] = (total[u, pos[second], rows] + full_in[p, u, 0, rows].astype(F32)
                                 + full_in[p, u, 1, rows].astype(F32))
            far = at(axis, 2)
            half1_out[p, u, 0] = partial[u, far, :, 0:HALF].astype(BF16)
            half1_out[p, u, 1] = partial[u, far, :, HALF:WIDE].astype(BF16)
            first_half.append((
                remote(base, half1_out.at[p, u, 0], half1_in.at[p, u, 0], near_by(axis, 1)),
                remote(base + 1, half1_out.at[p, u, 1], half1_in.at[p, u, 1], near_by(axis, -1))))
        second_half = []
        for u, (axis, _, _) in enumerate(ROUTES):
            base = u * PER_ROUTE + R1
            up, down = at(axis, 1), at(axis, -1)
            first_half[u][0].wait_recv()
            full1_out[p, u, 0, :, 0:HALF] = (partial[u, up, :, 0:HALF] + half1_in[p, u, 0].astype(F32)).astype(BF16)
            full1_out[p, u, 0, :, HALF:WIDE] = partial[u, up, :, HALF:WIDE].astype(BF16)
            a = remote(base + 2, full1_out.at[p, u, 0], full1_in.at[p, u, 0], near_by(axis, 1))
            first_half[u][1].wait_recv()
            full1_out[p, u, 1, :, 0:HALF] = partial[u, down, :, 0:HALF].astype(BF16)
            full1_out[p, u, 1, :, HALF:WIDE] = (
                partial[u, down, :, HALF:WIDE] + half1_in[p, u, 1].astype(F32)).astype(BF16)
            second_half.append((a, remote(base + 3, full1_out.at[p, u, 1], full1_in.at[p, u, 1], near_by(axis, -1))))
        for u, (axis, _, _) in enumerate(ROUTES):
            second_half[u][0].wait_recv()
            second_half[u][1].wait_recv()
            partial[u, pos[axis]] = (partial[u, pos[axis]] + full1_in[p, u, 0].astype(F32)
                                     + full1_in[p, u, 1].astype(F32))
        for g in range(8):
            sides = [partial[u, pos[ROUTES[u][0]], :, g * 128 : (g + 1) * 128] for u in range(3)]
            for u in range(3):
                small[(4 * g + u) * 16 : (4 * g + u + 1) * 16, :] = sides[u]
            small[(4 * g + 3) * 16 : (4 * g + 4) * 16, :] = fourth(sides, 16)

        for q in range(4):
            above = (small[pl.ds(8 + q, RHS, stride=16), 0:RMAX] * mask[8 + q : 9 + q, :RMAX]).astype(BF16)
            for i in (2 * q, 2 * q + 1):
                own = mask[i : i + 1, :RMAX]
                here = (small[pl.ds(i, RHS, stride=16), 0:RMAX] * own).astype(BF16)
                leaf = ((here.astype(F32) + dot_nt(above, transfer[i])) * own).astype(BF16)
                result = (near_sum[i] + dot(leaf, basis[i])).astype(BF16)
                out[p, i] = result
                v[p + 1, 1 + i] = result

        @pl.when(p == 0)
        def _():
            small[...] = jnp.zeros_like(small)
            coefficients(p + 1)

        for copy in started:
            copy.wait_send()
        return carry

    lax.fori_loop(0, 2, product, 0)


def routing(clusters_of):
    device, local = clusters_of // 12, clusters_of % 12
    where = {a: (device // s) % 4 for a, s in STRIDE.items()}
    groups = jnp.stack([where[a] * 2 + device % 2 for _, _, a in ROUTES])
    rows = jnp.stack([where[b] * 64 + where[a] * 16 + local for a, b, _ in ROUTES])
    order = jnp.arange(BLOCKS)
    same = (groups[:, :, None] == groups[:, None, :]) & (order[None, None, :] < order[None, :, None])
    slot = groups * SLOTS + jnp.sum(same.astype(jnp.int32), axis=2)
    hit = slot[:, None, :] == jnp.arange(GROUPS * SLOTS)[None, :, None]
    wanted = jnp.max(jnp.where(hit, rows[:, None, :], -1), axis=2)
    return slot, wanted.reshape(3, GROUPS, SLOTS)


def local(charges, basis, transfer, near_field, coupling, ranks, block_source, block_target):
    me = lax.axis_index("clu")
    mask = (jnp.arange(128)[None, :] < jnp.pad(ranks, (0, 4))[:, None]).astype(F32)
    source_slot, source_rows = routing(block_source)
    target_slot, target_rows = routing(block_target)
    both = jnp.stack([source_rows, target_rows], axis=2)
    mine = jnp.stack([(me // STRIDE[a]) % 4 * 2 + me % 2 for _, _, a in ROUTES])
    spread = jnp.tile(both, (1, 1, 1, GROUPS))
    shown = (jnp.arange(GROUPS * SLOTS) // SLOTS)[None, :] == mine[:, None]
    lists = jnp.where(shown[:, None, None, :], spread, -1)
    lists = jnp.pad(lists, ((0, 0), (0, 0), (0, 6), (0, 0)), constant_values=-1)
    columns = jnp.pad(source_slot.T, ((0, 0), (0, 5)))
    lines = jnp.pad(target_slot, ((0, 5), (0, 0)))
    vmem = pl.BlockSpec(memory_space=pltpu.VMEM)
    hbm = pl.BlockSpec(memory_space=pl.ANY)
    both_out = pl.pallas_call(
        kernel,
        out_shape=jax.ShapeDtypeStruct((2, 8, RHS, LEAF), BF16),
        in_specs=[vmem, vmem, vmem, hbm, hbm, vmem, vmem, vmem, vmem],
        out_specs=vmem,
        scratch_shapes=[
            pltpu.VMEM((8, 3, LEAF, LEAF), BF16),
            pltpu.VMEM((BLOCKS, RMAX, RMAX), BF16),
            pltpu.VMEM((3, 10, RHS, LEAF), BF16),
            pltpu.VMEM((8, RHS, LEAF), F32),
            pltpu.VMEM((3, 8, 8, 256), jnp.int32),
            pltpu.VMEM((3, 256, 256), BF16),
            pltpu.VMEM((3, 256, 256), BF16),
            pltpu.VMEM((3, 128, 256), BF16),
            pltpu.VMEM((3, 256, 128), BF16),
            pltpu.VMEM((RHS * 16, 128), F32),
            pltpu.VMEM((RHS * BLOCKS, 128), F32),
            pltpu.VMEM((RHS * BLOCKS, 128), F32),
            pltpu.VMEM((3, BLOCKS, WIDE), BF16),
            pltpu.VMEM((2, 3, 16, 16, WIDE), BF16),
            pltpu.VMEM((2, 2, 3, GROUPS, SLOTS, WIDE), BF16),
            pltpu.VMEM((2, 2, 3, GROUPS, SLOTS, WIDE), BF16),
            pltpu.VMEM((2, 2, 3, 2, SLOTS, WIDE), BF16),
            pltpu.VMEM((3, 4, 64, WIDE), F32),
            pltpu.VMEM((3, 4, 16, WIDE), F32),
            pltpu.VMEM((2, 3, 2, 64, HALF), BF16),
            pltpu.VMEM((2, 3, 2, 64, HALF), BF16),
            pltpu.VMEM((2, 3, 2, 64, WIDE), BF16),
            pltpu.VMEM((2, 3, 2, 64, WIDE), BF16),
            pltpu.VMEM((2, 3, 2, 16, HALF), BF16),
            pltpu.VMEM((2, 3, 2, 16, HALF), BF16),
            pltpu.VMEM((2, 3, 2, 16, WIDE), BF16),
            pltpu.VMEM((2, 3, 2, 16, WIDE), BF16),
            pltpu.SemaphoreType.DMA((2, COPIES)),
            pltpu.SemaphoreType.DMA((2, COPIES)),
            pltpu.SemaphoreType.DMA((21,)),
            pltpu.SemaphoreType.DMA((21,)),
            pltpu.SemaphoreType.DMA((2,)),
        ],
        compiler_params=pltpu.CompilerParams(
            collective_id=0, has_side_effects=True, vmem_limit_bytes=56 * 1024 * 1024
        ),
    )(charges, basis, transfer, near_field, coupling, mask, lists, columns, lines)
    return both_out[0], both_out[1]


def solution(mesh):
    in_specs = (
        P("clu", None, None),
        P("clu", None, None),
        P("clu", None, None),
        P("clu", None, None, None),
        P("clu", None, None),
        P("clu"),
        P("clu"),
        P("clu"),
    )
    out_specs = (P("clu", None, None), P("clu", None, None))
    return jax.shard_map(local, mesh=mesh, in_specs=in_specs, out_specs=out_specs, check_vma=False)
```

```python
import jax
import jax.numpy as jnp
from jax import lax
from jax.experimental import pallas as pl
from jax.experimental.pallas import tpu as pltpu
from jax.sharding import PartitionSpec as P

MESH = pl.DeviceIdType.MESH
F32 = jnp.float32
BF16 = jnp.bfloat16
RMAX = 96
RHS = 32
PART = 16
LEAF = 256
STRIDE = {"x": 32, "z": 8, "y": 2}
ROUTES = (("y", "x", "z"), ("z", "y", "x"), ("x", "z", "y"))
STEPS = (2, 1, -1)
WIDE = 512
GROUPS = 8
SLOTS = 32
BLOCKS = 128

G1, G2, EX, R2, R1, HALO = 0, 9, 45, 87, 96, 105
COPIES = 107


def dot(a, b):
    return jnp.dot(a, b, preferred_element_type=F32)


def dot_nt(a, b):
    return lax.dot_general(a, b, (((1,), (1,)), ((), ())), preferred_element_type=F32)


def iota(shape, dim):
    return lax.broadcasted_iota(jnp.int32, shape, dim)


def ones_where(hit):
    return jnp.where(hit, 1.0, 0.0).astype(F32)


def merge(row, extra, u):
    return jnp.where(iota(row.shape, 1) < RMAX, row, pltpu.roll(extra, RMAX - 32 * u, 1))


def fourth(parts):
    rolled = [pltpu.roll(part, 32 + 32 * u, 1) for u, part in enumerate(parts)]
    lanes = iota(parts[0].shape, 1)
    return jnp.where(lanes < 32, rolled[0], jnp.where(lanes < 64, rolled[1], rolled[2]))


def kernel(
    charges, basis, transfer, near_hbm, coupling_hbm, ranks, block_source, block_target,
    first_out, second_out,
    near, turned, wide_coupling, coupling, v, near_sum, mask, raw, raw_in, meta, pick, scatter, unpick, place,
    small, big_in, big_out, products, gathered, outbox, inbox, sums_out, sums_in, ends_out, ends_in,
    send_sem, recv_sem, list_send, list_recv, load_sem,
):
    me = lax.axis_index("clu")
    devices = 128
    core = lax.rem(me, 2)
    pos = {a: lax.rem(lax.div(me, s), 4) for a, s in STRIDE.items()}

    def at(axis, step):
        return lax.rem(pos[axis] + (step + 4), 4)

    def near_by(axis, step, other=0):
        base = me + (at(axis, step) - pos[axis]) * STRIDE[axis]
        return base + (1 - 2 * core) if other else base

    sibling = me + (1 - 2 * core)
    before = lax.rem(me + devices - 1, devices)
    after = lax.rem(me + 1, devices)

    barrier = pltpu.get_barrier_semaphore()
    peers = [sibling, before, after]
    for axis in STRIDE:
        for step in STEPS:
            for other in (0, 1):
                peers.append(near_by(axis, step, other))
    for peer in peers:
        pl.semaphore_signal(barrier, inc=1, device_id=(peer,), device_id_type=MESH)

    load_near = pltpu.make_async_copy(near_hbm, near, load_sem.at[0])
    load_coupling = pltpu.make_async_copy(coupling_hbm, turned, load_sem.at[1])
    load_coupling.start()
    load_near.start()
    v[0, 1:9] = charges[...]
    small[...] = jnp.zeros_like(small)
    raw[...] = jnp.zeros_like(raw)
    raw[0:1, :] = block_source[...]
    raw[1:2, :] = block_target[...]
    for i in range(12):
        mask[i : i + 1, :] = ones_where(iota((1, 128), 1) < ranks[0:1, i : i + 1])

    def copy_of(p, h, k, src, dst, device):
        return pltpu.make_async_remote_copy(
            src_ref=src, dst_ref=dst, send_sem=send_sem.at[p, h, k], recv_sem=recv_sem.at[p, h, k],
            device_id=(device,), device_id_type=MESH)

    def coefficients(p, h):
        rows = pl.ds(PART * h, PART)
        for q in range(4):
            above = jnp.zeros((PART, RMAX), F32)
            for i in (2 * q, 2 * q + 1):
                c = dot_nt(v[p, 1 + i, rows], basis[i]) * mask[i : i + 1, :RMAX]
                c = c.astype(BF16)
                small[h, pl.ds(i, PART, stride=16), 0:RMAX] = c.astype(F32)
                above = above + dot(c, transfer[i])
            c = (above * mask[8 + q : 9 + q, :RMAX]).astype(BF16)
            small[h, pl.ds(8 + q, PART, stride=16), 0:RMAX] = c.astype(F32)
        for u, (first, second, _) in enumerate(ROUTES):
            where = pos[second] * 4 + pos[first]
            for g in range(4):
                row = small[h, (4 * g + u) * 16 : (4 * g + u + 1) * 16, :]
                extra = small[h, (4 * g + 3) * 16 : (4 * g + 4) * 16, :]
                gathered[p, h, u, where, :, g * 128 : (g + 1) * 128] = merge(row, extra, u).astype(BF16)

    def halo_copies(p, h):
        rows = pl.ds(PART * h, PART)
        return [
            copy_of(p, h, HALO, v.at[p, 1, rows], v.at[p, 9, rows], before),
            copy_of(p, h, HALO + 1, v.at[p, 8, rows], v.at[p, 0, rows], after),
        ]

    def first_gather(p, h):
        copies = []
        for u, (first, second, _) in enumerate(ROUTES):
            own = gathered.at[p, h, u, pos[second] * 4 + pos[first]]
            copies.append([copy_of(p, h, G1 + 3 * u + s, own, own, near_by(first, step))
                           for s, step in enumerate(STEPS)])
        return copies

    def second_gather(p, h, u, piece):
        first, second, _ = ROUTES[u]
        block = gathered.at[p, h, u, pos[second] * 4 + at(first, (0, -2, -1, 1)[piece])]
        return [copy_of(p, h, G2 + (4 * u + piece) * 3 + s, block, block, near_by(second, step))
                for s, step in enumerate(STEPS)]

    def begin(p, h):
        coefficients(p, h)
        for copies in first_gather(p, h):
            for copy in copies:
                copy.start()
        for u in range(3):
            for copy in second_gather(p, h, u, 0):
                copy.start()
        for copy in halo_copies(p, h):
            copy.start()

    def near_part(p, lo, hi):
        def body(i, carry):
            s = dot(v[p, i], near[i, 0])
            s = s + dot(v[p, i + 1], near[i, 1])
            near_sum[i] = s + dot(v[p, i + 2], near[i, 2])
            return carry

        lax.fori_loop(lo, hi, body, 0)

    list_copies = []
    for u, (_, _, axis) in enumerate(ROUTES):
        mine = pos[axis] * 2 + core
        targets = [near_by(axis, s, o) for s in STEPS for o in (0, 1)] + [sibling]
        for k, device in enumerate(targets):
            list_copies.append(pltpu.make_async_remote_copy(
                src_ref=raw, dst_ref=raw_in.at[u, pl.ds(pl.multiple_of(mine * 8, 8), 8)],
                send_sem=list_send.at[u * 7 + k], recv_sem=list_recv.at[u * 7 + k],
                device_id=(device,), device_id_type=MESH))

    def place_of(ids, route):
        first, second, axis = route
        device = lax.shift_right_logical(ids * 43691, 19)
        where = {a: lax.shift_right_logical(device, n) & 3 for a, n in (("x", 5), ("z", 3), ("y", 1))}
        group = where[axis] * 2 + (device & 1)
        return group, where[second] * 64 + where[first] * 16 + (ids - 12 * device)

    def make_selectors():
        ahead = ones_where(iota((128, 128), 0) < iota((128, 128), 1)).astype(BF16)
        for u, route in enumerate(ROUTES):
            axis = route[2]
            mine = pos[axis] * 2 + core
            group, _ = place_of(raw[...], route)
            slots = []
            for k in range(2):
                hit = ones_where(iota((8, 128), 0) == group[k : k + 1, :])
                rank = jnp.sum(hit * dot(hit.astype(BF16), ahead), axis=0, keepdims=True)
                slots.append(group[k : k + 1, :].astype(F32) * SLOTS + rank)
            number = iota((256, 128), 0).astype(F32)
            unpick[u] = jnp.transpose(ones_where(number == slots[0]), (1, 0)).astype(BF16)
            place[u] = ones_where(number == slots[1]).astype(BF16)
            raw_in[u, pl.ds(pl.multiple_of(mine * 8, 8), 8), :] = raw[...]
            for k in range(2):
                group, row = place_of(raw_in[u, pl.ds(k, 8, stride=8), :], route)
                hit = ones_where(group == mine)
                rank = dot(hit.astype(BF16), ahead)
                meta[k, 0] = jnp.where(group == mine, rank, -1.0)
                meta[k, 1] = row.astype(F32)

            def fill(q, carry, u=u):
                for k in range(2):
                    slot = ones_where(iota((SLOTS, 128), 0).astype(F32) == meta[k, 0, pl.ds(q, 1), :])
                    row = ones_where(iota((256, 128), 0).astype(F32) == meta[k, 1, pl.ds(q, 1), :])
                    lines = dot_nt(slot.astype(BF16), row.astype(BF16))
                    here = pl.ds(pl.multiple_of(q * SLOTS, SLOTS), SLOTS)
                    if k == 0:
                        pick[u, here, :] = lines.astype(BF16)
                    else:
                        big_in[0, here, :] = lines[:, 0:128]
                        big_in[1, here, :] = lines[:, 128:256]
                return carry

            lax.fori_loop(0, GROUPS, fill, 0)
            scatter[u, 0:128, :] = jnp.transpose(big_in[0, 0:256, :], (1, 0)).astype(BF16)
            scatter[u, 128:256, :] = jnp.transpose(big_in[1, 0:256, :], (1, 0)).astype(BF16)

    def turn(lo, hi):
        same = ones_where(iota((128, 128), 0) == iota((128, 128), 1)).astype(BF16)

        def body(n, carry):
            for k in range(4):
                row = 4 * n + k
                wide_coupling[pl.ds(row, BLOCKS, stride=RMAX), 0:RMAX] = dot_nt(same, turned[row])
            return carry

        lax.fori_loop(lo // 4, hi // 4, body, 0)

    def narrow():
        def body(n, carry):
            for k in range(4):
                j = 4 * n + k
                rows = pl.ds(pl.multiple_of(j * RMAX, RMAX), RMAX)
                coupling[j] = wide_coupling[rows, 0:RMAX].astype(BF16)
            return carry

        lax.fori_loop(0, BLOCKS // 4, body, 0)

    def exchange(p, h, way, u):
        axis = ROUTES[u][2]
        base = EX + 21 * way + 7 * u
        box = outbox.at[p, h, way, u]
        mine = inbox.at[p, h, way, u, pos[axis] * 2 + core]
        copies = []
        for s, step in enumerate(STEPS):
            for o in (0, 1):
                group = at(axis, step) * 2 + (1 - core if o else core)
                copies.append(copy_of(p, h, base + 2 * s + o, box.at[group], mine, near_by(axis, step, o)))
        copies.append(copy_of(p, h, base + 6, box.at[pos[axis] * 2 + 1 - core], mine, sibling))
        for copy in copies:
            copy.start()
        inbox[p, h, way, u, pos[axis] * 2 + core] = outbox[p, h, way, u, pos[axis] * 2 + core]
        return copies

    def tiles(body):
        lax.fori_loop(0, WIDE // 256, lambda n, carry: body(pl.ds(pl.multiple_of(n * 256, 256), 256), n), 0)

    def stream(p, h):
        started = []
        ring = first_gather(p, h)
        waits = []
        for u in range(3):
            waits.append(second_gather(p, h, u, 0))
        for s in range(3):
            for u in range(3):
                ring[u][s].wait_recv()
                copies = second_gather(p, h, u, 1 + s)
                for copy in copies:
                    copy.start()
                waits[u] += copies
        for u in range(3):
            started += ring[u] + waits[u]
        yield
        flight = []
        for u in range(3):
            for copy in waits[u]:
                copy.wait_recv()

            def picks(cols, n, u=u):
                rows = gathered[p, h, u, :, :, cols].reshape(256, 256)
                outbox[p, h, 0, u, :, :, cols] = dot(pick[u], rows).astype(BF16).reshape(GROUPS, SLOTS, 256)
                return 0

            tiles(picks)
            flight.append(exchange(p, h, 0, u))
        yield
        for u in range(3):
            started += flight[u]
            for copy in flight[u]:
                copy.wait_recv()

        def unpicks(cols, n):
            parts = [dot(unpick[u], inbox[p, h, 0, u, :, :, cols].reshape(256, 256)) for u in range(3)]
            for k in range(2):
                g = 2 * n + k
                sides = [part[:, k * 128 : (k + 1) * 128] for part in parts]
                for u in range(3):
                    big_in[h, pl.ds(pl.multiple_of((4 * g + u) * 128, 128), 128), :] = sides[u]
                big_in[h, pl.ds(pl.multiple_of((4 * g + 3) * 128, 128), 128), :] = fourth(sides)
            return 0

        tiles(unpicks)

        def blocks(b, carry):
            for k in range(16):
                j = b * 16 + k
                x = big_in[h, pl.ds(j, PART, stride=BLOCKS), 0:RMAX].astype(BF16)
                big_out[h, pl.ds(j, PART, stride=BLOCKS), 0:RMAX] = dot(x, coupling[j])
            return carry

        lax.fori_loop(0, BLOCKS // 16, blocks, 0)

        def packs(g, carry):
            cols = pl.ds(pl.multiple_of(g * 128, 128), 128)
            extra = big_out[h, pl.ds(pl.multiple_of((4 * g + 3) * 128, 128), 128), :]
            for u in range(3):
                row = big_out[h, pl.ds(pl.multiple_of((4 * g + u) * 128, 128), 128), :]
                products[h, u, :, cols] = merge(row, extra, u).astype(BF16)
            return carry

        lax.fori_loop(0, 4, packs, 0)
        flight = []
        for u in range(3):
            def places(cols, n, u=u):
                sent = dot(place[u], products[h, u, :, cols]).astype(BF16)
                outbox[p, h, 1, u, :, :, cols] = sent.reshape(GROUPS, SLOTS, 256)
                return 0

            tiles(places)
            flight.append(exchange(p, h, 1, u))
        yield
        parts = []
        for u, (_, axis, _) in enumerate(ROUTES):
            started += flight[u]
            for copy in flight[u]:
                copy.wait_recv()

            def sums(cols, n, u=u):
                rows = inbox[p, h, 1, u, :, :, cols].reshape(256, 256)
                sums_out[p, h, u, :, :, cols] = dot(scatter[u], rows).astype(BF16).reshape(4, 64, 256)
                return 0

            tiles(sums)
            copies = [copy_of(p, h, R2 + 3 * u + s, sums_out.at[p, h, u, at(axis, step)], sums_in.at[p, h, u, s],
                              near_by(axis, step)) for s, step in enumerate(STEPS)]
            for copy in copies:
                copy.start()
            parts.append(copies)
        yield
        ends = []
        for u, (axis, second, _) in enumerate(ROUTES):
            started += parts[u]
            for copy in parts[u]:
                copy.wait_recv()
            for k in range(4):
                rows = slice(16 * k, 16 * k + 16)
                s = sums_out[p, h, u, pos[second], rows].astype(F32)
                for n in range(3):
                    s = s + sums_in[p, h, u, n, rows].astype(F32)
                ends_out[p, h, u, k] = s.astype(BF16)
            copies = [copy_of(p, h, R1 + 3 * u + s, ends_out.at[p, h, u, at(axis, step)], ends_in.at[p, h, u, s],
                              near_by(axis, step)) for s, step in enumerate(STEPS)]
            for copy in copies:
                copy.start()
            ends.append(copies)
        yield
        sides = []
        for u, (axis, _, _) in enumerate(ROUTES):
            started += ends[u]
            for copy in ends[u]:
                copy.wait_recv()
            s = ends_out[p, h, u, pos[axis]].astype(F32)
            for n in range(3):
                s = s + ends_in[p, h, u, n].astype(F32)
            sides.append(s)
        for g in range(4):
            here = [s[:, g * 128 : (g + 1) * 128] for s in sides]
            for u in range(3):
                small[h, (4 * g + u) * 16 : (4 * g + u + 1) * 16, :] = here[u]
            small[h, (4 * g + 3) * 16 : (4 * g + 4) * 16, :] = fourth(here)
        lines = pl.ds(PART * h, PART)
        for q in range(4):
            above = (small[h, pl.ds(8 + q, PART, stride=16), 0:RMAX] * mask[8 + q : 9 + q, :RMAX]).astype(BF16)
            for i in (2 * q, 2 * q + 1):
                own = mask[i : i + 1, :RMAX]
                here = (small[h, pl.ds(i, PART, stride=16), 0:RMAX] * own).astype(BF16)
                leaf = ((here.astype(F32) + dot_nt(above, transfer[i])) * own).astype(BF16)
                v[p + 1, 1 + i, lines] = (near_sum[i, lines] + dot(leaf, basis[i])).astype(BF16)

        @pl.when(p == 0)
        def _():
            small[h] = jnp.zeros_like(small[h])
            begin(p + 1, h)

        for copy in started + halo_copies(p, h):
            copy.wait_send()
        yield

    pl.semaphore_wait(barrier, len(peers))
    begin(0, 0)
    begin(0, 1)
    for copy in list_copies:
        copy.start()

    def product(p, carry):
        streams = [stream(p, h) for h in (0, 1)]

        def both():
            for s in streams:
                next(s)

        both()

        @pl.when(p == 0)
        def _():
            for copy in list_copies:
                copy.wait()
            make_selectors()
            load_coupling.wait()
            turn(0, 32)
            load_near.wait()

        for h in (0, 1):
            for copy in halo_copies(p, h):
                copy.wait_recv()
        v[p, 0] = (v[p, 0].astype(F32) * (me > 0).astype(F32)).astype(BF16)
        v[p, 9] = (v[p, 9].astype(F32) * (me < devices - 1).astype(F32)).astype(BF16)
        near_part(p, 0, 4)
        both()

        @pl.when(p == 0)
        def _():
            turn(32, 96)
            narrow()

        near_part(p, 4, 8)
        both()
        both()
        both()
        both()
        return carry

    lax.fori_loop(0, 2, product, 0)
    first_out[...] = v[1, 1:9]
    second_out[...] = v[2, 1:9]


def local(charges, basis, transfer, near_field, coupling, ranks, block_source, block_target):
    vmem = pl.BlockSpec(memory_space=pltpu.VMEM)
    hbm = pl.BlockSpec(memory_space=pl.ANY)
    result = jax.ShapeDtypeStruct((8, RHS, LEAF), BF16)
    return pl.pallas_call(
        kernel,
        out_shape=(result, result),
        in_specs=[vmem, vmem, vmem, hbm, hbm, vmem, vmem, vmem],
        out_specs=(vmem, vmem),
        scratch_shapes=[
            pltpu.VMEM((8, 3, LEAF, LEAF), BF16),
            pltpu.VMEM((RMAX, RMAX, BLOCKS), BF16),
            pltpu.VMEM((BLOCKS * RMAX, 128), F32),
            pltpu.VMEM((BLOCKS, RMAX, RMAX), BF16),
            pltpu.VMEM((3, 10, RHS, LEAF), BF16),
            pltpu.VMEM((8, RHS, LEAF), F32),
            pltpu.VMEM((16, 128), F32),
            pltpu.VMEM((8, 128), jnp.int32),
            pltpu.VMEM((3, 64, 128), jnp.int32),
            pltpu.VMEM((2, 2, 8, 128), F32),
            pltpu.VMEM((3, 256, 256), BF16),
            pltpu.VMEM((3, 256, 256), BF16),
            pltpu.VMEM((3, 128, 256), BF16),
            pltpu.VMEM((3, 256, 128), BF16),
            pltpu.VMEM((2, PART * 16, 128), F32),
            pltpu.VMEM((2, PART * BLOCKS, 128), F32),
            pltpu.VMEM((2, PART * BLOCKS, 128), F32),
            pltpu.VMEM((2, 3, BLOCKS, WIDE), BF16),
            pltpu.VMEM((2, 2, 3, 16, 16, WIDE), BF16),
            pltpu.VMEM((2, 2, 2, 3, GROUPS, SLOTS, WIDE), BF16),
            pltpu.VMEM((2, 2, 2, 3, GROUPS, SLOTS, WIDE), BF16),
            pltpu.VMEM((2, 2, 3, 4, 64, WIDE), BF16),
            pltpu.VMEM((2, 2, 3, 3, 64, WIDE), BF16),
            pltpu.VMEM((2, 2, 3, 4, 16, WIDE), BF16),
            pltpu.VMEM((2, 2, 3, 3, 16, WIDE), BF16),
            pltpu.SemaphoreType.DMA((2, 2, COPIES)),
            pltpu.SemaphoreType.DMA((2, 2, COPIES)),
            pltpu.SemaphoreType.DMA((21,)),
            pltpu.SemaphoreType.DMA((21,)),
            pltpu.SemaphoreType.DMA((2,)),
        ],
        compiler_params=pltpu.CompilerParams(
            collective_id=0, has_side_effects=True, vmem_limit_bytes=60 * 1024 * 1024
        ),
    )(charges, basis, transfer, near_field, jnp.transpose(coupling, (1, 2, 0)),
      ranks.reshape(1, 12), block_source.reshape(1, BLOCKS), block_target.reshape(1, BLOCKS))


def solution(mesh):
    in_specs = (
        P("clu", None, None),
        P("clu", None, None),
        P("clu", None, None),
        P("clu", None, None, None),
        P("clu", None, None),
        P("clu"),
        P("clu"),
        P("clu"),
    )
    out_specs = (P("clu", None, None), P("clu", None, None))
    return jax.shard_map(local, mesh=mesh, in_specs=in_specs, out_specs=out_specs, check_vma=False)
```

```python
import jax
import jax.numpy as jnp
from jax import lax
from jax.experimental import pallas as pl
from jax.experimental.pallas import tpu as pltpu
from jax.sharding import PartitionSpec as P

MESH = pl.DeviceIdType.MESH
F32 = jnp.float32
BF16 = jnp.bfloat16
RMAX = 96
RHS = 32
PART = 16
LEAF = 256
STRIDE = {"x": 32, "z": 8, "y": 2}
ROUTES = (("y", "x", "z"), ("z", "y", "x"), ("x", "z", "y"))
STEPS = (2, 1, -1)
WIDE = 512
GROUPS = 8
SLOTS = 32
BLOCKS = 128

G1, G2, EX, R2, R1, HALO = 0, 9, 27, 65, 74, 83
COPIES = 85


def dot(a, b):
    return jnp.dot(a, b, preferred_element_type=F32)


def dot_nt(a, b):
    return lax.dot_general(a, b, (((1,), (1,)), ((), ())), preferred_element_type=F32)


def iota(shape, dim):
    return lax.broadcasted_iota(jnp.int32, shape, dim)


def ones_where(hit):
    return jnp.where(hit, 1.0, 0.0).astype(F32)


def merge(row, extra, u):
    return jnp.where(iota(row.shape, 1) < RMAX, row, pltpu.roll(extra, RMAX - 32 * u, 1))


def fourth(parts):
    rolled = [pltpu.roll(part, 32 + 32 * u, 1) for u, part in enumerate(parts)]
    lanes = iota(parts[0].shape, 1)
    return jnp.where(lanes < 32, rolled[0], jnp.where(lanes < 64, rolled[1], rolled[2]))


def kernel(
    charges_hbm, basis_hbm, transfer_hbm, near_hbm, coupling_hbm, ranks_hbm, source_hbm, target_hbm,
    out,
    basis, transfer, near, turned, wide_coupling, coupling, v, near_sum, ranks, block_source, block_target,
    mask, raw, raw_in, pick, scatter, unpick, place,
    small, big_in, big_out, products, gathered, outbox, inbox, sums_out, sums_in, ends_out, ends_in,
    send_sem, recv_sem, list_send, list_recv, load_sem,
):
    me = lax.axis_index("clu")
    devices = 128
    core = lax.rem(me, 2)
    pos = {a: lax.rem(lax.div(me, s), 4) for a, s in STRIDE.items()}

    def near_by(axis, step, other=0):
        base = me + (lax.rem(pos[axis] + (step + 4), 4) - pos[axis]) * STRIDE[axis]
        return base + (1 - 2 * core) if other else base

    sibling = me + (1 - 2 * core)
    before = lax.rem(me + devices - 1, devices)
    after = lax.rem(me + 1, devices)

    barrier = pltpu.get_barrier_semaphore()
    peers = [sibling, before, after]
    for axis in STRIDE:
        for step in STEPS:
            for other in (0, 1):
                peers.append(near_by(axis, step, other))
    for peer in peers:
        pl.semaphore_signal(barrier, inc=1, device_id=(peer,), device_id_type=MESH)

    loads = [pltpu.make_async_copy(src, dst, load_sem.at[k]) for k, (src, dst) in enumerate((
        (charges_hbm, v.at[0, pl.ds(1, 8)]), (basis_hbm, basis), (transfer_hbm, transfer), (ranks_hbm, ranks),
        (source_hbm, block_source), (target_hbm, block_target), (coupling_hbm, turned), (near_hbm, near)))]
    for load in loads:
        load.start()
    load_coupling, load_near = loads[6:]
    small[...] = jnp.zeros_like(small)
    raw[...] = jnp.zeros_like(raw)

    def copy_of(p, h, k, src, dst, device):
        return pltpu.make_async_remote_copy(
            src_ref=src, dst_ref=dst, send_sem=send_sem.at[p, h, k], recv_sem=recv_sem.at[p, h, k],
            device_id=(device,), device_id_type=MESH)

    def coefficients(p, h):
        rows = pl.ds(PART * h, PART)
        masks = [mask[i : i + 1, :RMAX] for i in range(12)]
        leaves = [dot_nt(v[p, 1 + i, rows], basis[i]) for i in range(8)]
        leaves = [(c * m).astype(BF16) for c, m in zip(leaves, masks)]
        lifted = [dot(c, transfer[i]) for i, c in enumerate(leaves)]
        above = [((lifted[2 * q] + lifted[2 * q + 1]) * masks[8 + q]).astype(BF16) for q in range(4)]
        for i, c in enumerate(leaves + above):
            small[h, pl.ds(i, PART, stride=16), 0:RMAX] = c.astype(F32)
        for u in range(3):
            for g in range(4):
                row = small[h, (4 * g + u) * 16 : (4 * g + u + 1) * 16, :]
                extra = small[h, (4 * g + 3) * 16 : (4 * g + 4) * 16, :]
                gathered[p, h, u, 0, 0, :, g * 128 : (g + 1) * 128] = merge(row, extra, u).astype(BF16)

    def halo_copies(p, h):
        rows = pl.ds(PART * h, PART)
        return [
            copy_of(p, h, HALO, v.at[p, 1, rows], v.at[p, 9, rows], before),
            copy_of(p, h, HALO + 1, v.at[p, 8, rows], v.at[p, 0, rows], after),
        ]

    def first_gather(p, h):
        copies = []
        for u, (first, _, _) in enumerate(ROUTES):
            block = gathered.at[p, h, u, 0]
            copies.append([copy_of(p, h, G1 + 3 * u + s, block.at[0], block.at[-step % 4], near_by(first, step))
                           for s, step in enumerate(STEPS)])
        return copies

    def second_gather(p, h, u, piece):
        second = ROUTES[u][1]
        copies = []
        for s, step in enumerate(STEPS):
            src, dst = gathered.at[p, h, u, 0], gathered.at[p, h, u, -step % 4]
            src, dst = (r.at[pl.ds(1, 3)] if piece else r.at[0] for r in (src, dst))
            copies.append(copy_of(p, h, G2 + (2 * u + piece) * 3 + s, src, dst, near_by(second, step)))
        return copies

    def begin(p, h):
        for copies in first_gather(p, h):
            for copy in copies:
                copy.start()
        for u in range(3):
            for copy in second_gather(p, h, u, 0):
                copy.start()
        for copy in halo_copies(p, h):
            copy.start()

    def near_part(p, lo, hi):
        def body(i, carry):
            s = dot(v[p, i], near[i, 0])
            s = s + dot(v[p, i + 1], near[i, 1])
            near_sum[i] = s + dot(v[p, i + 2], near[i, 2])
            return carry

        lax.fori_loop(lo, hi, body, 0)

    list_copies = []
    for u, (_, _, axis) in enumerate(ROUTES):
        targets = [(near_by(axis, step, o), -step % 4 * 2 + o) for step in STEPS for o in (0, 1)] + [(sibling, 1)]
        for k, (device, group) in enumerate(targets):
            list_copies.append(pltpu.make_async_remote_copy(
                src_ref=raw, dst_ref=raw_in.at[u, pl.ds(8 * group, 8)],
                send_sem=list_send.at[u * 7 + k], recv_sem=list_recv.at[u * 7 + k],
                device_id=(device,), device_id_type=MESH))

    def place_of(ids, route):
        first, second, axis = route
        device = lax.shift_right_logical(ids * 43691, 19)
        where = {a: (lax.shift_right_logical(device, n) + (4 - pos[a])) & 3 for a, n in (("x", 5), ("z", 3), ("y", 1))}
        group = where[axis] * 2 + ((device + core) & 1)
        return group, where[second] * 64 + where[first] * 16 + (ids - 12 * device)

    def make_selectors():
        ahead = ones_where(iota((128, 128), 0) < iota((128, 128), 1)).astype(BF16)
        number = iota((256, 128), 0).astype(F32)
        lines = iota((256, 256), 1).astype(F32)
        within = iota((SLOTS, 128), 0).astype(F32)
        for u, route in enumerate(ROUTES):
            group, _ = place_of(raw[...], route)
            slots = []
            for k in range(2):
                hit = ones_where(iota((8, 128), 0) == group[k : k + 1, :])
                rank = jnp.sum(hit * dot(hit.astype(BF16), ahead), axis=0, keepdims=True)
                slots.append(group[k : k + 1, :].astype(F32) * SLOTS + rank)
            unpick[u] = jnp.transpose(ones_where(number == slots[0]), (1, 0)).astype(BF16)
            place[u] = ones_where(number == slots[1]).astype(BF16)
            raw_in[u, 0:8, :] = raw[...]
            for k in range(2):
                ids = raw_in[u, pl.ds(k, 8, stride=8), :]
                group, row = place_of(ids, route)
                hit = ones_where(group == 0)
                rank = jnp.where(group == 0, dot(hit.astype(BF16), ahead), -1.0)
                row = row.astype(F32) + 1.0
                wanted = []
                for q in range(GROUPS):
                    mine = jnp.where(within == rank[q : q + 1, :], row[q : q + 1, :], 0.0)
                    wanted.append(jnp.sum(mine, axis=1, keepdims=True))
                wanted = jnp.concatenate(wanted, axis=0) - 1.0
                lists = ones_where(lines == wanted)
                if k == 0:
                    pick[u] = lists.astype(BF16)
                else:
                    scatter[u] = jnp.transpose(lists, (1, 0)).astype(BF16)

    def turn(lo, hi):
        same = ones_where(iota((128, 128), 0) == iota((128, 128), 1)).astype(BF16)

        def body(n, carry):
            for k in range(4):
                row = 4 * n + k
                wide_coupling[pl.ds(row, BLOCKS, stride=RMAX), 0:RMAX] = dot_nt(same, turned[row])
            return carry

        lax.fori_loop(lo // 4, hi // 4, body, 0)

    def narrow():
        def body(n, carry):
            for k in range(4):
                j = 4 * n + k
                rows = pl.ds(pl.multiple_of(j * RMAX, RMAX), RMAX)
                coupling[j] = wide_coupling[rows, 0:RMAX].astype(BF16)
            return carry

        lax.fori_loop(0, BLOCKS // 4, body, 0)

    def exchange(p, h, way, u):
        axis = ROUTES[u][2]
        base = EX + 19 * way + 6 * u
        box, to = outbox.at[p, h, way, u], inbox.at[p, h, way, u]
        copies = []
        for s, step in enumerate(STEPS):
            for o in (0, 1):
                copies.append(copy_of(p, h, base + 2 * s + o, box.at[step % 4 * 2 + o], to.at[-step % 4 * 2 + o],
                                      near_by(axis, step, o)))
        for copy in copies:
            copy.start()
        inbox[p, h, way, u, 0] = outbox[p, h, way, u, 0]
        return copies

    def exchange_sibling(p, h, way):
        copy = copy_of(p, h, EX + 19 * way + 18, outbox.at[p, h, way, pl.ds(0, 3), 1],
                       inbox.at[p, h, way, pl.ds(0, 3), 1], sibling)
        copy.start()
        return copy

    def tiles(body):
        lax.fori_loop(0, WIDE // 256, lambda n, carry: body(pl.ds(pl.multiple_of(n * 256, 256), 256), n), 0)

    def stream(p, h):
        started = []
        ring = first_gather(p, h)
        waits = []
        for u in range(3):
            for copy in ring[u]:
                copy.wait_recv()
            copies = second_gather(p, h, u, 1)
            for copy in copies:
                copy.start()
            waits.append(second_gather(p, h, u, 0) + copies)
            started += ring[u] + waits[u]
        yield
        flight = []
        for u in range(3):
            for copy in waits[u]:
                copy.wait_recv()

            def picks(cols, n, u=u):
                rows = gathered[p, h, u, :, :, :, cols].reshape(256, 256)
                outbox[p, h, 0, u, :, :, cols] = dot(pick[u], rows).astype(BF16).reshape(GROUPS, SLOTS, 256)
                return 0

            tiles(picks)
            flight.append(exchange(p, h, 0, u))
        flight.append([exchange_sibling(p, h, 0)])
        yield
        for copies in flight:
            started += copies
            for copy in copies:
                copy.wait_recv()

        def unpicks(cols, n):
            parts = [dot(unpick[u], inbox[p, h, 0, u, :, :, cols].reshape(256, 256)) for u in range(3)]
            for k in range(2):
                g = 2 * n + k
                sides = [part[:, k * 128 : (k + 1) * 128] for part in parts]
                for u in range(3):
                    big_in[h, pl.ds(pl.multiple_of((4 * g + u) * 128, 128), 128), :] = sides[u]
                big_in[h, pl.ds(pl.multiple_of((4 * g + 3) * 128, 128), 128), :] = fourth(sides)
            return 0

        tiles(unpicks)

        def blocks(b, carry):
            for k in range(16):
                j = b * 16 + k
                x = big_in[h, pl.ds(j, PART, stride=BLOCKS), 0:RMAX].astype(BF16)
                big_out[h, pl.ds(j, PART, stride=BLOCKS), 0:RMAX] = dot(x, coupling[j])
            return carry

        lax.fori_loop(0, BLOCKS // 16, blocks, 0)

        def packs(g, carry):
            cols = pl.ds(pl.multiple_of(g * 128, 128), 128)
            extra = big_out[h, pl.ds(pl.multiple_of((4 * g + 3) * 128, 128), 128), :]
            for u in range(3):
                row = big_out[h, pl.ds(pl.multiple_of((4 * g + u) * 128, 128), 128), :]
                products[h, u, :, cols] = merge(row, extra, u).astype(BF16)
            return carry

        lax.fori_loop(0, 4, packs, 0)
        flight = []
        for u in range(3):
            def places(cols, n, u=u):
                sent = dot(place[u], products[h, u, :, cols]).astype(BF16)
                outbox[p, h, 1, u, :, :, cols] = sent.reshape(GROUPS, SLOTS, 256)
                return 0

            tiles(places)
            flight.append(exchange(p, h, 1, u))
        flight.append([exchange_sibling(p, h, 1)])
        yield
        parts = []
        started += flight[3]
        flight[3][0].wait_recv()
        for u, (_, axis, _) in enumerate(ROUTES):
            started += flight[u]
            for copy in flight[u]:
                copy.wait_recv()

            def sums(cols, n, u=u):
                rows = inbox[p, h, 1, u, :, :, cols].reshape(256, 256)
                sums_out[p, h, u, :, :, cols] = dot(scatter[u], rows).astype(BF16).reshape(4, 64, 256)
                return 0

            tiles(sums)
            copies = [copy_of(p, h, R2 + 3 * u + s, sums_out.at[p, h, u, step % 4], sums_in.at[p, h, u, s],
                              near_by(axis, step)) for s, step in enumerate(STEPS)]
            for copy in copies:
                copy.start()
            parts.append(copies)
        yield
        ends = []
        for u, (axis, _, _) in enumerate(ROUTES):
            started += parts[u]
            for copy in parts[u]:
                copy.wait_recv()
            for k in range(4):
                rows = slice(16 * k, 16 * k + 16)
                s = sums_out[p, h, u, 0, rows].astype(F32)
                for n in range(3):
                    s = s + sums_in[p, h, u, n, rows].astype(F32)
                ends_out[p, h, u, k] = s.astype(BF16)
            copies = [copy_of(p, h, R1 + 3 * u + s, ends_out.at[p, h, u, step % 4], ends_in.at[p, h, u, s],
                              near_by(axis, step)) for s, step in enumerate(STEPS)]
            for copy in copies:
                copy.start()
            ends.append(copies)
        yield
        sides = []
        for u in range(3):
            started += ends[u]
            for copy in ends[u]:
                copy.wait_recv()
            s = ends_out[p, h, u, 0].astype(F32)
            for n in range(3):
                s = s + ends_in[p, h, u, n].astype(F32)
            sides.append(s)
        for g in range(4):
            here = [s[:, g * 128 : (g + 1) * 128] for s in sides]
            for u in range(3):
                small[h, (4 * g + u) * 16 : (4 * g + u + 1) * 16, :] = here[u]
            small[h, (4 * g + 3) * 16 : (4 * g + 4) * 16, :] = fourth(here)
        lines = pl.ds(PART * h, PART)
        masks = [mask[i : i + 1, :RMAX] for i in range(12)]
        fields = [(small[h, pl.ds(i, PART, stride=16), 0:RMAX] * masks[i]).astype(BF16) for i in range(12)]
        downs = [dot_nt(fields[8 + i // 2], transfer[i]) for i in range(8)]
        leaves = [((fields[i].astype(F32) + downs[i]) * masks[i]).astype(BF16) for i in range(8)]
        fars = [dot(leaves[i], basis[i]) for i in range(8)]
        fars = [(near_sum[i, lines] + fars[i]).astype(BF16) for i in range(8)]
        for i in range(8):
            v[p + 1, 1 + i, lines] = fars[i]

        @pl.when(p == 0)
        def _():
            small[h] = jnp.zeros_like(small[h])
            coefficients(p + 1, h)
            begin(p + 1, h)

        for copy in started + halo_copies(p, h):
            copy.wait_send()
        yield

    for load in loads[:6]:
        load.wait()
    raw[0:1, :] = block_source[...]
    raw[1:2, :] = block_target[...]
    for i in range(12):
        mask[i : i + 1, :] = ones_where(iota((1, 128), 1) < ranks[0:1, i : i + 1])
    coefficients(0, 0)
    coefficients(0, 1)
    pl.semaphore_wait(barrier, len(peers))
    for copy in list_copies:
        copy.start()
    begin(0, 0)
    begin(0, 1)

    def product(p, carry):
        streams = [stream(p, h) for h in (0, 1)]

        def both():
            for s in streams:
                next(s)

        @pl.when(p == 0)
        def _():
            for copy in list_copies:
                copy.wait()
            make_selectors()

        both()

        @pl.when(p == 0)
        def _():
            load_coupling.wait()
            turn(0, 32)
            load_near.wait()

        for h in (0, 1):
            for copy in halo_copies(p, h):
                copy.wait_recv()
        v[p, 0] = (v[p, 0].astype(F32) * (me > 0).astype(F32)).astype(BF16)
        v[p, 9] = (v[p, 9].astype(F32) * (me < devices - 1).astype(F32)).astype(BF16)
        near_part(p, 0, 4)
        both()

        @pl.when(p == 0)
        def _():
            turn(32, 96)
            narrow()

        near_part(p, 4, 8)
        both()
        both()
        both()
        both()
        return carry

    lax.fori_loop(0, 2, product, 0)
    out[...] = v[1:3, 1:9]


def local(charges, basis, transfer, near_field, coupling, ranks, block_source, block_target):
    vmem = pl.BlockSpec(memory_space=pltpu.VMEM)
    hbm = pl.BlockSpec(memory_space=pl.ANY)
    both = pl.pallas_call(
        kernel,
        out_shape=jax.ShapeDtypeStruct((2, 8, RHS, LEAF), BF16),
        in_specs=[hbm] * 8,
        out_specs=vmem,
        scratch_shapes=[
            pltpu.VMEM((8, RMAX, LEAF), BF16),
            pltpu.VMEM((8, RMAX, RMAX), BF16),
            pltpu.VMEM((8, 3, LEAF, LEAF), BF16),
            pltpu.VMEM((RMAX, RMAX, BLOCKS), BF16),
            pltpu.VMEM((BLOCKS * RMAX, 128), F32),
            pltpu.VMEM((BLOCKS, RMAX, RMAX), BF16),
            pltpu.VMEM((3, 10, RHS, LEAF), BF16),
            pltpu.VMEM((8, RHS, LEAF), F32),
            pltpu.VMEM((1, 12), jnp.int32),
            pltpu.VMEM((1, BLOCKS), jnp.int32),
            pltpu.VMEM((1, BLOCKS), jnp.int32),
            pltpu.VMEM((16, 128), F32),
            pltpu.VMEM((8, 128), jnp.int32),
            pltpu.VMEM((3, 64, 128), jnp.int32),
            pltpu.VMEM((3, 256, 256), BF16),
            pltpu.VMEM((3, 256, 256), BF16),
            pltpu.VMEM((3, 128, 256), BF16),
            pltpu.VMEM((3, 256, 128), BF16),
            pltpu.VMEM((2, PART * 16, 128), F32),
            pltpu.VMEM((2, PART * BLOCKS, 128), F32),
            pltpu.VMEM((2, PART * BLOCKS, 128), F32),
            pltpu.VMEM((2, 3, BLOCKS, WIDE), BF16),
            pltpu.VMEM((2, 2, 3, 4, 4, 16, WIDE), BF16),
            pltpu.VMEM((2, 2, 2, 3, GROUPS, SLOTS, WIDE), BF16),
            pltpu.VMEM((2, 2, 2, 3, GROUPS, SLOTS, WIDE), BF16),
            pltpu.VMEM((2, 2, 3, 4, 64, WIDE), BF16),
            pltpu.VMEM((2, 2, 3, 3, 64, WIDE), BF16),
            pltpu.VMEM((2, 2, 3, 4, 16, WIDE), BF16),
            pltpu.VMEM((2, 2, 3, 3, 16, WIDE), BF16),
            pltpu.SemaphoreType.DMA((2, 2, COPIES)),
            pltpu.SemaphoreType.DMA((2, 2, COPIES)),
            pltpu.SemaphoreType.DMA((21,)),
            pltpu.SemaphoreType.DMA((21,)),
            pltpu.SemaphoreType.DMA((8,)),
        ],
        compiler_params=pltpu.CompilerParams(
            collective_id=0, has_side_effects=True, vmem_limit_bytes=60 * 1024 * 1024
        ),
    )(charges, basis, transfer, near_field, jnp.transpose(coupling, (1, 2, 0)),
      ranks.reshape(1, 12), block_source.reshape(1, BLOCKS), block_target.reshape(1, BLOCKS))
    return both[0], both[1]


def solution(mesh):
    in_specs = (
        P("clu", None, None),
        P("clu", None, None),
        P("clu", None, None),
        P("clu", None, None, None),
        P("clu", None, None),
        P("clu"),
        P("clu"),
        P("clu"),
    )
    out_specs = (P("clu", None, None), P("clu", None, None))
    return jax.shard_map(local, mesh=mesh, in_specs=in_specs, out_specs=out_specs, check_vma=False)
```

```python
import jax
import jax.numpy as jnp
from jax import lax
from jax.experimental import pallas as pl
from jax.experimental.pallas import tpu as pltpu
from jax.sharding import PartitionSpec as P

MESH = pl.DeviceIdType.MESH
F32 = jnp.float32
BF16 = jnp.bfloat16
RMAX = 96
RHS = 32
PART = 16
LEAF = 256
STRIDE = {"x": 32, "z": 8, "y": 2}
ROUTES = (("y", "x", "z"), ("z", "y", "x"), ("x", "z", "y"))
STEPS = (2, 1, -1)
WIDE = 512
GROUPS = 8
SLOTS = 32
BLOCKS = 128

G1, G2, EX, R2, R1, HALO = 0, 3, 6, 12, 15, 18
GROUPS_OF_COPIES = 19


def dot(a, b):
    return jnp.dot(a, b, preferred_element_type=F32)


def dot_nt(a, b):
    return lax.dot_general(a, b, (((1,), (1,)), ((), ())), preferred_element_type=F32)


def iota(shape, dim):
    return lax.broadcasted_iota(jnp.int32, shape, dim)


def ones_where(hit):
    return jnp.where(hit, 1.0, 0.0).astype(F32)


def merge(row, extra, u):
    return jnp.where(iota(row.shape, 1) < RMAX, row, pltpu.roll(extra, RMAX - 32 * u, 1))


def fourth(parts):
    rolled = [pltpu.roll(part, 32 + 32 * u, 1) for u, part in enumerate(parts)]
    lanes = iota(parts[0].shape, 1)
    return jnp.where(lanes < 32, rolled[0], jnp.where(lanes < 64, rolled[1], rolled[2]))


def kernel(
    charges_hbm, basis_hbm, transfer_hbm, near_hbm, coupling_hbm, ranks_hbm, source_hbm, target_hbm,
    out,
    basis, transfer, near, turned, wide_coupling, coupling, v, near_sum, ranks, block_source, block_target,
    mask, raw, raw_in, pick, scatter, unpick, place,
    small, big_in, big_out, products, gathered, outbox, inbox, sums_out, sums_in, ends_out, ends_in,
    send_sem, recv_sem, list_send, list_recv, load_sem,
):
    me = lax.axis_index("clu")
    devices = 128
    core = lax.rem(me, 2)
    pos = {a: lax.rem(lax.div(me, s), 4) for a, s in STRIDE.items()}

    def near_by(axis, step, other=0):
        base = me + (lax.rem(pos[axis] + (step + 4), 4) - pos[axis]) * STRIDE[axis]
        return base + (1 - 2 * core) if other else base

    sibling = me + (1 - 2 * core)
    before = lax.rem(me + devices - 1, devices)
    after = lax.rem(me + 1, devices)

    barrier = pltpu.get_barrier_semaphore()
    peers = [sibling, before, after]
    for axis in STRIDE:
        for step in STEPS:
            for other in (0, 1):
                peers.append(near_by(axis, step, other))
    for peer in peers:
        pl.semaphore_signal(barrier, inc=1, device_id=(peer,), device_id_type=MESH)

    loads = [pltpu.make_async_copy(src, dst, load_sem.at[k]) for k, (src, dst) in enumerate((
        (charges_hbm, v.at[0, pl.ds(1, 8)]), (basis_hbm, basis), (transfer_hbm, transfer), (ranks_hbm, ranks),
        (source_hbm, block_source), (target_hbm, block_target), (coupling_hbm, turned), (near_hbm, near)))]
    for load in loads:
        load.start()
    load_coupling, load_near = loads[6:]
    small[...] = jnp.zeros_like(small)
    raw[...] = jnp.zeros_like(raw)

    def copy_of(p, h, k, src, dst, device):
        return pltpu.make_async_remote_copy(
            src_ref=src, dst_ref=dst, send_sem=send_sem.at[p, h, k], recv_sem=recv_sem.at[p, h, k],
            device_id=(device,), device_id_type=MESH)

    def arrivals(p, h, k, where):
        return copy_of(p, h, k, where, where, sibling)

    def coefficients(p, h):
        rows = pl.ds(PART * h, PART)
        masks = [mask[i : i + 1, :RMAX] for i in range(12)]
        leaves = [dot_nt(v[p, 1 + i, rows], basis[i]) for i in range(8)]
        leaves = [(c * m).astype(BF16) for c, m in zip(leaves, masks)]
        lifted = [dot(c, transfer[i]) for i, c in enumerate(leaves)]
        above = [((lifted[2 * q] + lifted[2 * q + 1]) * masks[8 + q]).astype(BF16) for q in range(4)]
        for i, c in enumerate(leaves + above):
            small[h, pl.ds(i, PART, stride=16), 0:RMAX] = c.astype(F32)
        for u in range(3):
            for g in range(4):
                row = small[h, (4 * g + u) * 16 : (4 * g + u + 1) * 16, :]
                extra = small[h, (4 * g + 3) * 16 : (4 * g + 4) * 16, :]
                gathered[p, h, u, 0, 0, :, g * 128 : (g + 1) * 128] = merge(row, extra, u).astype(BF16)

    def halo_copies(p, h):
        rows = pl.ds(PART * h, PART)
        return [
            copy_of(p, h, HALO, v.at[p, 1, rows], v.at[p, 9, rows], before),
            copy_of(p, h, HALO, v.at[p, 8, rows], v.at[p, 0, rows], after),
        ]

    def first_gather(p, h):
        copies = []
        for u, (first, _, _) in enumerate(ROUTES):
            block = gathered.at[p, h, u, 0]
            copies.append([copy_of(p, h, G1 + u, block.at[0], block.at[-step % 4], near_by(first, step))
                           for s, step in enumerate(STEPS)])
        return copies

    def second_gather(p, h, u, piece):
        second = ROUTES[u][1]
        copies = []
        for s, step in enumerate(STEPS):
            src, dst = gathered.at[p, h, u, 0], gathered.at[p, h, u, -step % 4]
            src, dst = (r.at[pl.ds(1, 3)] if piece else r.at[0] for r in (src, dst))
            copies.append(copy_of(p, h, G2 + u, src, dst, near_by(second, step)))
        return copies

    def begin(p, h):
        for copies in first_gather(p, h):
            for copy in copies:
                copy.start()
        for u in range(3):
            for copy in second_gather(p, h, u, 0):
                copy.start()
        for copy in halo_copies(p, h):
            copy.start()

    def near_part(p, lo, hi):
        for i in range(lo, hi):
            s = dot(v[p, i], near[i, 0])
            s = s + dot(v[p, i + 1], near[i, 1])
            near_sum[i] = s + dot(v[p, i + 2], near[i, 2])

    list_copies = []
    for u, (_, _, axis) in enumerate(ROUTES):
        targets = [(near_by(axis, step, o), -step % 4 * 2 + o) for step in STEPS for o in (0, 1)] + [(sibling, 1)]
        for device, group in targets:
            list_copies.append(pltpu.make_async_remote_copy(
                src_ref=raw, dst_ref=raw_in.at[u, pl.ds(8 * group, 8)],
                send_sem=list_send.at[u], recv_sem=list_recv.at[u],
                device_id=(device,), device_id_type=MESH))

    def place_of(ids, route):
        first, second, axis = route
        device = lax.shift_right_logical(ids * 43691, 19)
        where = {a: (lax.shift_right_logical(device, n) + (4 - pos[a])) & 3 for a, n in (("x", 5), ("z", 3), ("y", 1))}
        group = where[axis] * 2 + ((device + core) & 1)
        return group, where[second] * 64 + where[first] * 16 + (ids - 12 * device)

    def make_selectors():
        ahead = ones_where(iota((128, 128), 0) < iota((128, 128), 1)).astype(BF16)
        number = iota((256, 128), 0).astype(F32)
        lines = iota((256, 256), 1).astype(F32)
        within = iota((SLOTS, 128), 0).astype(F32)
        for u, route in enumerate(ROUTES):
            group, _ = place_of(raw[...], route)
            slots = []
            for k in range(2):
                hit = ones_where(iota((8, 128), 0) == group[k : k + 1, :])
                rank = jnp.sum(hit * dot(hit.astype(BF16), ahead), axis=0, keepdims=True)
                slots.append(group[k : k + 1, :].astype(F32) * SLOTS + rank)
            unpick[u] = jnp.transpose(ones_where(number == slots[0]), (1, 0)).astype(BF16)
            place[u] = ones_where(number == slots[1]).astype(BF16)
            raw_in[u, 0:8, :] = raw[...]
            for k in range(2):
                ids = raw_in[u, pl.ds(k, 8, stride=8), :]
                group, row = place_of(ids, route)
                hit = ones_where(group == 0)
                rank = jnp.where(group == 0, dot(hit.astype(BF16), ahead), -1.0)
                row = row.astype(F32) + 1.0
                wanted = []
                for q in range(GROUPS):
                    mine = jnp.where(within == rank[q : q + 1, :], row[q : q + 1, :], 0.0)
                    wanted.append(jnp.sum(mine, axis=1, keepdims=True))
                wanted = jnp.concatenate(wanted, axis=0) - 1.0
                lists = ones_where(lines == wanted)
                if k == 0:
                    pick[u] = lists.astype(BF16)
                else:
                    scatter[u] = jnp.transpose(lists, (1, 0)).astype(BF16)

    def turn():
        def body(n, carry):
            for k in range(32):
                row = 32 * n + k
                wide_coupling[pl.ds(row, BLOCKS, stride=RMAX), 0:RMAX] = jnp.transpose(turned[row].astype(F32), (1, 0))
            return carry

        lax.fori_loop(0, RMAX // 32, body, 0)

    def narrow():
        def body(n, carry):
            for k in range(8):
                j = 8 * n + k
                rows = pl.ds(pl.multiple_of(j * RMAX, RMAX), RMAX)
                coupling[j] = wide_coupling[rows, 0:RMAX].astype(BF16)
            return carry

        lax.fori_loop(0, BLOCKS // 8, body, 0)

    def exchange(p, h, way, u):
        axis = ROUTES[u][2]
        box, to = outbox.at[p, h, way, u], inbox.at[p, h, way, u]
        targets = [(near_by(axis, step, o), step % 4 * 2 + o, -step % 4 * 2 + o) for step in STEPS for o in (0, 1)]
        for device, src, dst in targets + [(sibling, 1, 1)]:
            copy_of(p, h, EX + 3 * way + u, box.at[src], to.at[dst], device).start()
        inbox[p, h, way, u, 0] = outbox[p, h, way, u, 0]

    def exchanged(p, h, way, u):
        return arrivals(p, h, EX + 3 * way + u, inbox.at[p, h, way, u, pl.ds(1, 7)])

    def tiles(body):
        for n in range(WIDE // 256):
            body(slice(256 * n, 256 * n + 256), n)

    def line_copies(p, h, k, out, into, axis):
        for s, step in enumerate(STEPS):
            copy_of(p, h, k, out.at[step % 4], into.at[s], near_by(axis, step)).start()

    def stream(p, h):
        for u in range(3):
            arrivals(p, h, G1 + u, gathered.at[p, h, u, 0, pl.ds(1, 3)]).wait_recv()
            for copy in second_gather(p, h, u, 1):
                copy.start()
        yield
        for u in range(3):
            arrivals(p, h, G2 + u, gathered.at[p, h, u, pl.ds(1, 3)]).wait_recv()

            def picks(cols, n, u=u):
                rows = gathered[p, h, u, :, :, :, cols].reshape(256, 256)
                outbox[p, h, 0, u, :, :, cols] = dot(pick[u], rows).astype(BF16).reshape(GROUPS, SLOTS, 256)

            tiles(picks)
            exchange(p, h, 0, u)
        yield
        for u in range(3):
            exchanged(p, h, 0, u).wait_recv()

        def unpicks(cols, n):
            parts = [dot(unpick[u], inbox[p, h, 0, u, :, :, cols].reshape(256, 256)) for u in range(3)]
            for k in range(2):
                g = 2 * n + k
                sides = [part[:, k * 128 : (k + 1) * 128] for part in parts]
                for u in range(3):
                    big_in[h, (4 * g + u) * 128 : (4 * g + u + 1) * 128, :] = sides[u]
                big_in[h, (4 * g + 3) * 128 : (4 * g + 4) * 128, :] = fourth(sides)

        tiles(unpicks)

        for j in range(BLOCKS):
            x = big_in[h, pl.ds(j, PART, stride=BLOCKS), 0:RMAX].astype(BF16)
            big_out[h, pl.ds(j, PART, stride=BLOCKS), 0:RMAX] = dot(x, coupling[j])
        for g in range(4):
            extra = big_out[h, (4 * g + 3) * 128 : (4 * g + 4) * 128, :]
            for u in range(3):
                row = big_out[h, (4 * g + u) * 128 : (4 * g + u + 1) * 128, :]
                products[h, u, :, g * 128 : (g + 1) * 128] = merge(row, extra, u).astype(BF16)
        for u in range(3):
            def places(cols, n, u=u):
                sent = dot(place[u], products[h, u, :, cols]).astype(BF16)
                outbox[p, h, 1, u, :, :, cols] = sent.reshape(GROUPS, SLOTS, 256)

            tiles(places)
            exchange(p, h, 1, u)
        yield
        for u, (_, axis, _) in enumerate(ROUTES):
            exchanged(p, h, 1, u).wait_recv()

            def sums(cols, n, u=u):
                rows = inbox[p, h, 1, u, :, :, cols].reshape(256, 256)
                sums_out[p, h, u, :, :, cols] = dot(scatter[u], rows).astype(BF16).reshape(4, 64, 256)

            tiles(sums)
            line_copies(p, h, R2 + u, sums_out.at[p, h, u], sums_in.at[p, h, u], axis)
        yield
        for u, (axis, _, _) in enumerate(ROUTES):
            arrivals(p, h, R2 + u, sums_in.at[p, h, u]).wait_recv()
            for k in range(4):
                rows = slice(16 * k, 16 * k + 16)
                s = sums_out[p, h, u, 0, rows].astype(F32)
                for n in range(3):
                    s = s + sums_in[p, h, u, n, rows].astype(F32)
                ends_out[p, h, u, k] = s.astype(BF16)
            line_copies(p, h, R1 + u, ends_out.at[p, h, u], ends_in.at[p, h, u], axis)
        yield
        sides = []
        for u in range(3):
            arrivals(p, h, R1 + u, ends_in.at[p, h, u]).wait_recv()
            s = ends_out[p, h, u, 0].astype(F32)
            for n in range(3):
                s = s + ends_in[p, h, u, n].astype(F32)
            sides.append(s)
        for g in range(4):
            here = [s[:, g * 128 : (g + 1) * 128] for s in sides]
            for u in range(3):
                small[h, (4 * g + u) * 16 : (4 * g + u + 1) * 16, :] = here[u]
            small[h, (4 * g + 3) * 16 : (4 * g + 4) * 16, :] = fourth(here)
        lines = pl.ds(PART * h, PART)
        masks = [mask[i : i + 1, :RMAX] for i in range(12)]
        fields = [(small[h, pl.ds(i, PART, stride=16), 0:RMAX] * masks[i]).astype(BF16) for i in range(12)]
        downs = [dot_nt(fields[8 + i // 2], transfer[i]) for i in range(8)]
        leaves = [((fields[i].astype(F32) + downs[i]) * masks[i]).astype(BF16) for i in range(8)]
        fars = [dot(leaves[i], basis[i]) for i in range(8)]
        fars = [(near_sum[i, lines] + fars[i]).astype(BF16) for i in range(8)]
        for i in range(8):
            v[p + 1, 1 + i, lines] = fars[i]

        @pl.when(p == 0)
        def _():
            small[h] = jnp.zeros_like(small[h])
            coefficients(p + 1, h)
            begin(p + 1, h)

        for u in range(3):
            arrivals(p, h, G1 + u, gathered.at[p, h, u, 0, pl.ds(1, 3)]).wait_send()
            arrivals(p, h, G2 + u, gathered.at[p, h, u, pl.ds(1, 3)]).wait_send()
            exchanged(p, h, 0, u).wait_send()
            exchanged(p, h, 1, u).wait_send()
            arrivals(p, h, R2 + u, sums_in.at[p, h, u]).wait_send()
            arrivals(p, h, R1 + u, ends_in.at[p, h, u]).wait_send()
        arrivals(p, h, HALO, v.at[p, pl.ds(0, 2), lines]).wait_send()
        yield

    for load in loads[:6]:
        load.wait()
    raw[0:1, :] = block_source[...]
    raw[1:2, :] = block_target[...]
    for i in range(12):
        mask[i : i + 1, :] = ones_where(iota((1, 128), 1) < ranks[0:1, i : i + 1])
    coefficients(0, 0)
    coefficients(0, 1)
    pl.semaphore_wait(barrier, len(peers))
    for copy in list_copies:
        copy.start()
    begin(0, 0)
    begin(0, 1)

    def product(p, carry):
        streams = [stream(p, h) for h in (0, 1)]

        def both():
            for s in streams:
                next(s)

        both()

        @pl.when(p == 0)
        def _():
            for u in range(3):
                tiles_in = raw_in.at[u, pl.ds(8, 56)]
                copy = pltpu.make_async_remote_copy(
                    src_ref=tiles_in, dst_ref=tiles_in, send_sem=list_send.at[u], recv_sem=list_recv.at[u],
                    device_id=(sibling,), device_id_type=MESH)
                copy.wait()
            make_selectors()
            load_coupling.wait()
            turn()
            load_near.wait()

        for h in (0, 1):
            arrivals(p, h, HALO, v.at[p, pl.ds(0, 2), pl.ds(PART * h, PART)]).wait_recv()
        v[p, 0] = (v[p, 0].astype(F32) * (me > 0).astype(F32)).astype(BF16)
        v[p, 9] = (v[p, 9].astype(F32) * (me < devices - 1).astype(F32)).astype(BF16)
        near_part(p, 0, 4)
        both()

        @pl.when(p == 0)
        def _():
            narrow()

        near_part(p, 4, 8)
        both()
        both()
        both()
        both()
        return carry

    lax.fori_loop(0, 2, product, 0)
    out[...] = v[1:3, 1:9]


def local(charges, basis, transfer, near_field, coupling, ranks, block_source, block_target):
    vmem = pl.BlockSpec(memory_space=pltpu.VMEM)
    hbm = pl.BlockSpec(memory_space=pl.ANY)
    both = pl.pallas_call(
        kernel,
        out_shape=jax.ShapeDtypeStruct((2, 8, RHS, LEAF), BF16),
        in_specs=[hbm] * 8,
        out_specs=vmem,
        scratch_shapes=[
            pltpu.VMEM((8, RMAX, LEAF), BF16),
            pltpu.VMEM((8, RMAX, RMAX), BF16),
            pltpu.VMEM((8, 3, LEAF, LEAF), BF16),
            pltpu.VMEM((RMAX, RMAX, BLOCKS), BF16),
            pltpu.VMEM((BLOCKS * RMAX, 128), F32),
            pltpu.VMEM((BLOCKS, RMAX, RMAX), BF16),
            pltpu.VMEM((3, 10, RHS, LEAF), BF16),
            pltpu.VMEM((8, RHS, LEAF), F32),
            pltpu.VMEM((1, 12), jnp.int32),
            pltpu.VMEM((1, BLOCKS), jnp.int32),
            pltpu.VMEM((1, BLOCKS), jnp.int32),
            pltpu.VMEM((16, 128), F32),
            pltpu.VMEM((8, 128), jnp.int32),
            pltpu.VMEM((3, 64, 128), jnp.int32),
            pltpu.VMEM((3, 256, 256), BF16),
            pltpu.VMEM((3, 256, 256), BF16),
            pltpu.VMEM((3, 128, 256), BF16),
            pltpu.VMEM((3, 256, 128), BF16),
            pltpu.VMEM((2, PART * 16, 128), F32),
            pltpu.VMEM((2, PART * BLOCKS, 128), F32),
            pltpu.VMEM((2, PART * BLOCKS, 128), F32),
            pltpu.VMEM((2, 3, BLOCKS, WIDE), BF16),
            pltpu.VMEM((2, 2, 3, 4, 4, 16, WIDE), BF16),
            pltpu.VMEM((2, 2, 2, 3, GROUPS, SLOTS, WIDE), BF16),
            pltpu.VMEM((2, 2, 2, 3, GROUPS, SLOTS, WIDE), BF16),
            pltpu.VMEM((2, 2, 3, 4, 64, WIDE), BF16),
            pltpu.VMEM((2, 2, 3, 3, 64, WIDE), BF16),
            pltpu.VMEM((2, 2, 3, 4, 16, WIDE), BF16),
            pltpu.VMEM((2, 2, 3, 3, 16, WIDE), BF16),
            pltpu.SemaphoreType.DMA((2, 2, GROUPS_OF_COPIES)),
            pltpu.SemaphoreType.DMA((2, 2, GROUPS_OF_COPIES)),
            pltpu.SemaphoreType.DMA((3,)),
            pltpu.SemaphoreType.DMA((3,)),
            pltpu.SemaphoreType.DMA((8,)),
        ],
        compiler_params=pltpu.CompilerParams(
            collective_id=0, has_side_effects=True, vmem_limit_bytes=60 * 1024 * 1024
        ),
    )(charges, basis, transfer, near_field, jnp.transpose(coupling, (1, 2, 0)),
      ranks.reshape(1, 12), block_source.reshape(1, BLOCKS), block_target.reshape(1, BLOCKS))
    return both[0], both[1]


def solution(mesh):
    in_specs = (
        P("clu", None, None),
        P("clu", None, None),
        P("clu", None, None),
        P("clu", None, None, None),
        P("clu", None, None),
        P("clu"),
        P("clu"),
        P("clu"),
    )
    out_specs = (P("clu", None, None), P("clu", None, None))
    return jax.shard_map(local, mesh=mesh, in_specs=in_specs, out_specs=out_specs, check_vma=False)
```

```python
import jax
import jax.numpy as jnp
from jax import lax
from jax.experimental import pallas as pl
from jax.experimental.pallas import tpu as pltpu
from jax.sharding import PartitionSpec as P

MESH = pl.DeviceIdType.MESH
F32 = jnp.float32
BF16 = jnp.bfloat16
RMAX = 96
RHS = 32
PART = 16
LEAF = 256
STRIDE = {"x": 32, "z": 8, "y": 2}
ROUTES = (("y", "x", "z"), ("z", "y", "x"), ("x", "z", "y"))
STEPS = (2, 1, -1)
WIDE = 512
GROUPS = 8
SLOTS = 32
BLOCKS = 128

G1, G2, EX, R2, R1, HALO = 0, 3, 6, 12, 15, 18
ARRIVALS = 19
KINDS = {G1: 0, G2: 1, EX: 2, EX + 3: 3, R2: 4, R1: 5, HALO: 6}
ROWS = 48


def dot(a, b):
    return jnp.dot(a, b, preferred_element_type=F32)


def dot_nt(a, b):
    return lax.dot_general(a, b, (((1,), (1,)), ((), ())), preferred_element_type=F32)


def iota(shape, dim):
    return lax.broadcasted_iota(jnp.int32, shape, dim)


def ones_where(hit):
    return jnp.where(hit, 1.0, 0.0).astype(F32)


def merge(row, extra, u):
    return jnp.where(iota(row.shape, 1) < RMAX, row, pltpu.roll(extra, RMAX - 32 * u, 1))


def fourth(parts):
    rolled = [pltpu.roll(part, 32 + 32 * u, 1) for u, part in enumerate(parts)]
    lanes = iota(parts[0].shape, 1)
    return jnp.where(lanes < 32, rolled[0], jnp.where(lanes < 64, rolled[1], rolled[2]))


def kernel(
    charges_hbm, basis_hbm, transfer_hbm, near_hbm, coupling_hbm, ranks_hbm, source_hbm, target_hbm,
    out,
    basis, transfer, near, turned, wide_coupling, coupling, v, near_sum, ranks, block_source, block_target,
    mask, raw, raw_in, pick, scatter, unpick, place,
    small, big_in, big_out, products, compact, expand, gathered, packed, outbox, inbox, sums_out, sums_in, ends_out, ends_in,
    send_sem, recv_sem, list_send, list_recv, load_sem,
):
    me = lax.axis_index("clu")
    devices = 128
    core = lax.rem(me, 2)
    pos = {a: lax.rem(lax.div(me, s), 4) for a, s in STRIDE.items()}

    def near_by(axis, step, other=0):
        base = me + (lax.rem(pos[axis] + (step + 4), 4) - pos[axis]) * STRIDE[axis]
        return base + (1 - 2 * core) if other else base

    sibling = me + (1 - 2 * core)
    before = lax.rem(me + devices - 1, devices)
    after = lax.rem(me + 1, devices)

    barrier = pltpu.get_barrier_semaphore()
    peers = [sibling, before, after]
    for axis in STRIDE:
        for step in STEPS:
            for other in (0, 1):
                peers.append(near_by(axis, step, other))
    for peer in peers:
        pl.semaphore_signal(barrier, inc=1, device_id=(peer,), device_id_type=MESH)

    loads = [pltpu.make_async_copy(src, dst, load_sem.at[k]) for k, (src, dst) in enumerate((
        (charges_hbm, v.at[0, pl.ds(1, 8)]), (basis_hbm, basis), (transfer_hbm, transfer), (ranks_hbm, ranks),
        (source_hbm, block_source), (target_hbm, block_target), (coupling_hbm, turned), (near_hbm, near)))]
    for load in loads:
        load.start()
    load_coupling, load_near = loads[6:]
    small[...] = jnp.zeros_like(small)
    raw[...] = jnp.zeros_like(raw)

    def copy_of(h, k, u, src, dst, device):
        return pltpu.make_async_remote_copy(
            src_ref=src, dst_ref=dst, send_sem=send_sem.at[h, KINDS[k]], recv_sem=recv_sem.at[h, k + u],
            device_id=(device,), device_id_type=MESH)

    def arrived(h, k, u, where):
        copy_of(h, k, u, where, where, sibling).wait_recv()

    def sent(h, k, where):
        copy_of(h, k, 0, where, where, sibling).wait_send()

    def coefficients(p, h):
        rows = pl.ds(PART * h, PART)
        masks = [mask[i : i + 1, :RMAX] for i in range(12)]
        leaves = [dot_nt(v[p, 1 + i, rows], basis[i]) for i in range(8)]
        leaves = [(c * m).astype(BF16) for c, m in zip(leaves, masks)]
        lifted = [dot(c, transfer[i]) for i, c in enumerate(leaves)]
        above = [((lifted[2 * q] + lifted[2 * q + 1]) * masks[8 + q]).astype(BF16) for q in range(4)]
        for i, c in enumerate(leaves + above):
            small[h, pl.ds(i, PART, stride=16), 0:RMAX] = c.astype(F32)
        for u in range(3):
            for g in range(4):
                row = small[h, (4 * g + u) * 16 : (4 * g + u + 1) * 16, :]
                extra = small[h, (4 * g + 3) * 16 : (4 * g + 4) * 16, :]
                gathered[p, h, u, 0, :, g * 128 : (g + 1) * 128] = merge(row, extra, u).astype(BF16)

    def begin(p, h):
        for u, (axis, _, _) in enumerate(ROUTES):
            block = gathered.at[p, h, u]
            for step in STEPS:
                copy_of(h, G1, u, block.at[0], block.at[-step % 4], near_by(axis, step)).start()
        rows = pl.ds(PART * h, PART)
        copy_of(h, HALO, 0, v.at[p, 1, rows], v.at[p, 9, rows], before).start()
        copy_of(h, HALO, 0, v.at[p, 8, rows], v.at[p, 0, rows], after).start()

    def near_part(p, lo, hi):
        if lo == 0:
            for h in (0, 1):
                arrived(h, HALO, 0, v.at[p, pl.ds(0, 2), pl.ds(PART * h, PART)])
            v[p, 0] = (v[p, 0].astype(F32) * (me > 0).astype(F32)).astype(BF16)
            v[p, 9] = (v[p, 9].astype(F32) * (me < devices - 1).astype(F32)).astype(BF16)
        for i in range(lo, hi):
            s = dot(v[p, i], near[i, 0])
            s = s + dot(v[p, i + 1], near[i, 1])
            near_sum[i] = s + dot(v[p, i + 2], near[i, 2])

    list_copies = []
    for u, (_, _, axis) in enumerate(ROUTES):
        targets = [(near_by(axis, step, o), -step % 4 * 2 + o) for step in STEPS for o in (0, 1)] + [(sibling, 1)]
        for device, group in targets:
            list_copies.append(pltpu.make_async_remote_copy(
                src_ref=raw, dst_ref=raw_in.at[u, pl.ds(8 * group, 8)],
                send_sem=list_send.at[u], recv_sem=list_recv.at[u],
                device_id=(device,), device_id_type=MESH))

    def place_of(ids, route):
        first, second, axis = route
        device = lax.shift_right_logical(ids * 43691, 19)
        where = {a: (lax.shift_right_logical(device, n) + (4 - pos[a])) & 3 for a, n in (("x", 5), ("z", 3), ("y", 1))}
        group = where[axis] * 2 + ((device + core) & 1)
        return group, where[second] * ROWS + where[first] * 12 + (ids - 12 * device)

    ahead = ones_where(iota((128, 128), 0) < iota((128, 128), 1)).astype(BF16)

    def rows_wanted(u, k):
        within = iota((SLOTS, 128), 0).astype(F32)
        group, row = place_of(raw_in[u, pl.ds(k, 8, stride=8), :], ROUTES[u])
        rank = jnp.where(group == 0, dot(ones_where(group == 0).astype(BF16), ahead), -1.0)
        row = row.astype(F32) + 1.0
        wanted = []
        for q in range(GROUPS):
            mine = jnp.where(within == rank[q : q + 1, :], row[q : q + 1, :], 0.0)
            wanted.append(jnp.sum(mine, axis=1, keepdims=True))
        wanted = jnp.concatenate(wanted, axis=0) - 1.0
        return ones_where(iota((256, 4 * ROWS), 1).astype(F32) == wanted)

    def make_picks():
        for u in range(3):
            raw_in[u, 0:8, :] = raw[...]
            pick[u] = rows_wanted(u, 0).astype(BF16)

    def make_others():
        number = iota((256, 128), 0).astype(F32)
        for u, route in enumerate(ROUTES):
            group, _ = place_of(raw[...], route)
            slots = []
            for k in range(2):
                hit = ones_where(iota((8, 128), 0) == group[k : k + 1, :])
                rank = jnp.sum(hit * dot(hit.astype(BF16), ahead), axis=0, keepdims=True)
                slots.append(group[k : k + 1, :].astype(F32) * SLOTS + rank)
            unpick[u] = jnp.transpose(ones_where(number == slots[0]), (1, 0)).astype(BF16)
            place[u] = ones_where(number == slots[1]).astype(BF16)
            scatter[u] = jnp.transpose(rows_wanted(u, 1), (1, 0)).astype(BF16)

    def turn():
        def body(n, carry):
            for k in range(32):
                row = 32 * n + k
                wide_coupling[pl.ds(row, BLOCKS, stride=RMAX), 0:RMAX] = jnp.transpose(turned[row].astype(F32), (1, 0))
            return carry

        lax.fori_loop(0, RMAX // 32, body, 0)

    def narrow():
        def body(n, carry):
            for k in range(8):
                j = 8 * n + k
                rows = pl.ds(pl.multiple_of(j * RMAX, RMAX), RMAX)
                coupling[j] = wide_coupling[rows, 0:RMAX].astype(BF16)
            return carry

        lax.fori_loop(0, BLOCKS // 8, body, 0)

    def exchange(p, h, way, u):
        axis = ROUTES[u][2]
        box, to = outbox.at[p, h, way, u], inbox.at[p, h, way, u]
        targets = [(near_by(axis, step, o), step % 4 * 2 + o, -step % 4 * 2 + o) for step in STEPS for o in (0, 1)]
        for device, src, dst in targets + [(sibling, 1, 1)]:
            copy_of(h, EX + 3 * way, u, box.at[src], to.at[dst], device).start()
        inbox[p, h, way, u, 0] = outbox[p, h, way, u, 0]

    def exchanged(p, h, way, u):
        arrived(h, EX + 3 * way, u, inbox.at[p, h, way, u, pl.ds(1, 7)])

    def tiles(body):
        for n in range(WIDE // 256):
            body(slice(256 * n, 256 * n + 256), n)

    def line_copies(h, k, u, out, into, axis):
        for s, step in enumerate(STEPS):
            copy_of(h, k, u, out.at[step % 4], into.at[s], near_by(axis, step)).start()

    def stream(p, h):
        for u, (_, axis, _) in enumerate(ROUTES):
            arrived(h, G1, u, gathered.at[p, h, u, pl.ds(1, 3)])
            plane = packed.at[p, h, u]
            packed[p, h, u, 0] = dot(compact[...], gathered[p, h, u].reshape(64, WIDE)).astype(BF16)
            for step in STEPS:
                copy_of(h, G2, u, plane.at[0], plane.at[-step % 4], near_by(axis, step)).start()
        yield
        for u in range(3):
            arrived(h, G2, u, packed.at[p, h, u, pl.ds(1, 3)])

            def picks(cols, n, u=u):
                rows = packed[p, h, u, :, :, cols].reshape(4 * ROWS, 256)
                outbox[p, h, 0, u, :, :, cols] = dot(pick[u], rows).astype(BF16).reshape(GROUPS, SLOTS, 256)

            tiles(picks)
            exchange(p, h, 0, u)
        yield
        for u in range(3):
            exchanged(p, h, 0, u)

        def unpicks(cols, n):
            parts = [dot(unpick[u], inbox[p, h, 0, u, :, :, cols].reshape(256, 256)) for u in range(3)]
            for k in range(2):
                g = 2 * n + k
                sides = [part[:, k * 128 : (k + 1) * 128] for part in parts]
                for u in range(3):
                    big_in[h, (4 * g + u) * 128 : (4 * g + u + 1) * 128, :] = sides[u]
                big_in[h, (4 * g + 3) * 128 : (4 * g + 4) * 128, :] = fourth(sides)

        tiles(unpicks)

        for j in range(BLOCKS):
            x = big_in[h, pl.ds(j, PART, stride=BLOCKS), 0:RMAX].astype(BF16)
            big_out[h, pl.ds(j, PART, stride=BLOCKS), 0:RMAX] = dot(x, coupling[j])
        for g in range(4):
            extra = big_out[h, (4 * g + 3) * 128 : (4 * g + 4) * 128, :]
            for u in range(3):
                row = big_out[h, (4 * g + u) * 128 : (4 * g + u + 1) * 128, :]
                products[h, u, :, g * 128 : (g + 1) * 128] = merge(row, extra, u).astype(BF16)
        for u in range(3):
            def places(cols, n, u=u):
                terms = dot(place[u], products[h, u, :, cols]).astype(BF16)
                outbox[p, h, 1, u, :, :, cols] = terms.reshape(GROUPS, SLOTS, 256)

            tiles(places)
            exchange(p, h, 1, u)
        yield
        for u, (_, axis, _) in enumerate(ROUTES):
            exchanged(p, h, 1, u)

            def sums(cols, n, u=u):
                rows = inbox[p, h, 1, u, :, :, cols].reshape(256, 256)
                sums_out[p, h, u, :, :, cols] = dot(scatter[u], rows).astype(BF16).reshape(4, ROWS, 256)

            tiles(sums)
            line_copies(h, R2, u, sums_out.at[p, h, u], sums_in.at[p, h, u], axis)
        yield
        for u, (axis, _, _) in enumerate(ROUTES):
            arrived(h, R2, u, sums_in.at[p, h, u])
            s = sums_out[p, h, u, 0].astype(F32)
            for n in range(3):
                s = s + sums_in[p, h, u, n].astype(F32)
            ends_out[p, h, u] = dot(expand[...], s.astype(BF16)).astype(BF16).reshape(4, 16, WIDE)
            line_copies(h, R1, u, ends_out.at[p, h, u], ends_in.at[p, h, u], axis)
        yield
        sides = []
        for u in range(3):
            arrived(h, R1, u, ends_in.at[p, h, u])
            s = ends_out[p, h, u, 0].astype(F32)
            for n in range(3):
                s = s + ends_in[p, h, u, n].astype(F32)
            sides.append(s)
        for g in range(4):
            here = [s[:, g * 128 : (g + 1) * 128] for s in sides]
            for u in range(3):
                small[h, (4 * g + u) * 16 : (4 * g + u + 1) * 16, :] = here[u]
            small[h, (4 * g + 3) * 16 : (4 * g + 4) * 16, :] = fourth(here)
        lines = pl.ds(PART * h, PART)
        masks = [mask[i : i + 1, :RMAX] for i in range(12)]
        fields = [(small[h, pl.ds(i, PART, stride=16), 0:RMAX] * masks[i]).astype(BF16) for i in range(12)]
        downs = [dot_nt(fields[8 + i // 2], transfer[i]) for i in range(8)]
        leaves = [((fields[i].astype(F32) + downs[i]) * masks[i]).astype(BF16) for i in range(8)]
        fars = [dot(leaves[i], basis[i]) for i in range(8)]
        fars = [(near_sum[i, lines] + fars[i]).astype(BF16) for i in range(8)]
        for i in range(8):
            v[p + 1, 1 + i, lines] = fars[i]

        sent(h, G1, gathered.at[p, h, :, pl.ds(1, 3)])
        sent(h, G2, packed.at[p, h, :, pl.ds(1, 3)])
        sent(h, EX, inbox.at[p, h, 0, :, pl.ds(1, 7)])
        sent(h, EX + 3, inbox.at[p, h, 1, :, pl.ds(1, 7)])
        sent(h, R2, sums_in.at[p, h])
        sent(h, R1, ends_in.at[p, h])
        sent(h, HALO, v.at[p, pl.ds(0, 2), lines])
        if p == 0:
            small[h] = jnp.zeros_like(small[h])
            coefficients(1, h)
            begin(1, h)
        yield

    for load in loads[:6]:
        load.wait()
    raw[0:1, :] = block_source[...]
    raw[1:2, :] = block_target[...]
    for i in range(12):
        mask[i : i + 1, :] = ones_where(iota((1, 128), 1) < ranks[0:1, i : i + 1])
    coefficients(0, 0)
    coefficients(0, 1)
    column, line = iota((ROWS, 64), 1), iota((ROWS, 64), 0)
    same = lax.shift_right_logical(column, 4) * 12 + (column & 15) == line
    compact[...] = ones_where(same & ((column & 15) < 12)).astype(BF16)
    column, line = iota((64, ROWS), 0), iota((64, ROWS), 1)
    same = lax.shift_right_logical(column, 4) * 12 + (column & 15) == line
    expand[...] = ones_where(same & ((column & 15) < 12)).astype(BF16)
    pl.semaphore_wait(barrier, len(peers))
    for copy in list_copies:
        copy.start()
    begin(0, 0)
    begin(0, 1)

    for p in range(2):
        streams = [stream(p, h) for h in (0, 1)]

        def both():
            for s in streams:
                next(s)

        both()
        if p == 0:
            for u in range(3):
                tiles_in = raw_in.at[u, pl.ds(8, 56)]
                pltpu.make_async_remote_copy(
                    src_ref=tiles_in, dst_ref=tiles_in, send_sem=list_send.at[u], recv_sem=list_recv.at[u],
                    device_id=(sibling,), device_id_type=MESH).wait()
            make_picks()
        else:
            near_part(p, 0, 4)
        both()
        if p == 0:
            make_others()
            load_coupling.wait()
            turn()
            narrow()
            load_near.wait()
            near_part(p, 0, 4)
        near_part(p, 4, 8)
        both()
        both()
        both()
        both()
    out[...] = v[1:3, 1:9]


def local(charges, basis, transfer, near_field, coupling, ranks, block_source, block_target):
    vmem = pl.BlockSpec(memory_space=pltpu.VMEM)
    hbm = pl.BlockSpec(memory_space=pl.ANY)
    both = pl.pallas_call(
        kernel,
        out_shape=jax.ShapeDtypeStruct((2, 8, RHS, LEAF), BF16),
        in_specs=[hbm] * 8,
        out_specs=vmem,
        scratch_shapes=[
            pltpu.VMEM((8, RMAX, LEAF), BF16),
            pltpu.VMEM((8, RMAX, RMAX), BF16),
            pltpu.VMEM((8, 3, LEAF, LEAF), BF16),
            pltpu.VMEM((RMAX, RMAX, BLOCKS), BF16),
            pltpu.VMEM((BLOCKS * RMAX, 128), F32),
            pltpu.VMEM((BLOCKS, RMAX, RMAX), BF16),
            pltpu.VMEM((3, 10, RHS, LEAF), BF16),
            pltpu.VMEM((8, RHS, LEAF), F32),
            pltpu.VMEM((1, 12), jnp.int32),
            pltpu.VMEM((1, BLOCKS), jnp.int32),
            pltpu.VMEM((1, BLOCKS), jnp.int32),
            pltpu.VMEM((16, 128), F32),
            pltpu.VMEM((8, 128), jnp.int32),
            pltpu.VMEM((3, 64, 128), jnp.int32),
            pltpu.VMEM((3, 256, 4 * ROWS), BF16),
            pltpu.VMEM((3, 4 * ROWS, 256), BF16),
            pltpu.VMEM((3, 128, 256), BF16),
            pltpu.VMEM((3, 256, 128), BF16),
            pltpu.VMEM((2, PART * 16, 128), F32),
            pltpu.VMEM((2, PART * BLOCKS, 128), F32),
            pltpu.VMEM((2, PART * BLOCKS, 128), F32),
            pltpu.VMEM((2, 3, BLOCKS, WIDE), BF16),
            pltpu.VMEM((ROWS, 64), BF16),
            pltpu.VMEM((64, ROWS), BF16),
            pltpu.VMEM((2, 2, 3, 4, 16, WIDE), BF16),
            pltpu.VMEM((2, 2, 3, 4, ROWS, WIDE), BF16),
            pltpu.VMEM((2, 2, 2, 3, GROUPS, SLOTS, WIDE), BF16),
            pltpu.VMEM((2, 2, 2, 3, GROUPS, SLOTS, WIDE), BF16),
            pltpu.VMEM((2, 2, 3, 4, ROWS, WIDE), BF16),
            pltpu.VMEM((2, 2, 3, 3, ROWS, WIDE), BF16),
            pltpu.VMEM((2, 2, 3, 4, 16, WIDE), BF16),
            pltpu.VMEM((2, 2, 3, 3, 16, WIDE), BF16),
            pltpu.SemaphoreType.DMA((2, len(KINDS))),
            pltpu.SemaphoreType.DMA((2, ARRIVALS)),
            pltpu.SemaphoreType.DMA((3,)),
            pltpu.SemaphoreType.DMA((3,)),
            pltpu.SemaphoreType.DMA((8,)),
        ],
        compiler_params=pltpu.CompilerParams(
            collective_id=0, has_side_effects=True, vmem_limit_bytes=60 * 1024 * 1024
        ),
    )(charges, basis, transfer, near_field, jnp.transpose(coupling, (1, 2, 0)),
      ranks.reshape(1, 12), block_source.reshape(1, BLOCKS), block_target.reshape(1, BLOCKS))
    return both[0], both[1]


def solution(mesh):
    in_specs = (
        P("clu", None, None),
        P("clu", None, None),
        P("clu", None, None),
        P("clu", None, None, None),
        P("clu", None, None),
        P("clu"),
        P("clu"),
        P("clu"),
    )
    out_specs = (P("clu", None, None), P("clu", None, None))
    return jax.shard_map(local, mesh=mesh, in_specs=in_specs, out_specs=out_specs, check_vma=False)
```

```python
import jax
import jax.numpy as jnp
from jax import lax
from jax.experimental import pallas as pl
from jax.experimental.pallas import tpu as pltpu
from jax.sharding import PartitionSpec as P

MESH = pl.DeviceIdType.MESH
F32 = jnp.float32
BF16 = jnp.bfloat16
RMAX = 96
RHS = 32
STREAMS = 2
PART = RHS // STREAMS
QUADS = PART // 4
LEAF = 256
STRIDE = {"x": 32, "z": 8, "y": 2}
ROUTES = (("y", "x", "z"), ("z", "y", "x"), ("x", "z", "y"))
STEPS = (2, 1, -1)
WIDE = 128 * QUADS
GROUPS = 8
SLOTS = 32
BLOCKS = 128

G1, G2, EX, R2, R1, HALO = 0, 1, 4, 10, 13, 14
ARRIVALS = 15
KINDS = {G1: 0, G2: 1, EX: 2, EX + 3: 3, R2: 4, R1: 5, HALO: 6}
ROWS = 48
PITCH_BLOCK, PITCH_CLUSTER, PITCH_TURN = 136, 24, 104


def dot(a, b):
    return jnp.dot(a, b, preferred_element_type=F32)


def dot_nt(a, b):
    return lax.dot_general(a, b, (((1,), (1,)), ((), ())), preferred_element_type=F32)


def iota(shape, dim):
    return lax.broadcasted_iota(jnp.int32, shape, dim)


def ones_where(hit):
    return jnp.where(hit, 1.0, 0.0).astype(F32)


def merge(row, extra, u):
    return jnp.where(iota(row.shape, 1) < RMAX, row, pltpu.roll(extra, RMAX - 32 * u, 1))


def fourth(parts):
    rolled = [pltpu.roll(part, 32 + 32 * u, 1) for u, part in enumerate(parts)]
    lanes = iota(parts[0].shape, 1)
    return jnp.where(lanes < 32, rolled[0], jnp.where(lanes < 64, rolled[1], rolled[2]))


def kernel(
    charges_hbm, basis_hbm, transfer_hbm, near_hbm, coupling_hbm, ranks_hbm, source_hbm, target_hbm,
    out,
    basis, transfer, near, turned, wide_coupling, coupling, v, lines_of, near_sum, ranks, block_source, block_target,
    mask, raw, raw_in, pick, scatter, unpick, place,
    small, big_in, big_out, products, compact, expand, gathered, packed, outbox, inbox, sums_out, sums_in, ends_out, ends_in,
    send_sem, recv_sem, list_send, list_recv, load_sem,
):
    me = lax.axis_index("clu")
    devices = 128
    core = lax.rem(me, 2)
    pos = {a: lax.rem(lax.div(me, s), 4) for a, s in STRIDE.items()}

    def near_by(axis, step, other=0):
        base = me + (lax.rem(pos[axis] + (step + 4), 4) - pos[axis]) * STRIDE[axis]
        return base + (1 - 2 * core) if other else base

    sibling = me + (1 - 2 * core)
    before = lax.rem(me + devices - 1, devices)
    after = lax.rem(me + 1, devices)

    barrier = pltpu.get_barrier_semaphore()
    peers = [sibling, before, after]
    for axis in STRIDE:
        for step in STEPS:
            for other in (0, 1):
                peers.append(near_by(axis, step, other))
    for peer in peers:
        pl.semaphore_signal(barrier, inc=1, device_id=(peer,), device_id_type=MESH)

    loads = [pltpu.make_async_copy(src, dst, load_sem.at[k]) for k, (src, dst) in enumerate((
        (charges_hbm, v.at[0, pl.ds(1, 8)]), (basis_hbm, basis), (transfer_hbm, transfer), (ranks_hbm, ranks),
        (source_hbm, block_source), (target_hbm, block_target), (coupling_hbm, turned), (near_hbm, near)))]
    for load in loads:
        load.start()
    load_coupling, load_near = loads[6:]
    small[...] = jnp.zeros_like(small)
    raw[...] = jnp.zeros_like(raw)

    def copy_of(h, k, u, src, dst, device):
        return pltpu.make_async_remote_copy(
            src_ref=src, dst_ref=dst, send_sem=send_sem.at[h, KINDS[k]], recv_sem=recv_sem.at[h, k + u],
            device_id=(device,), device_id_type=MESH)

    def arrived(h, k, u, where):
        copy_of(h, k, u, where, where, sibling).wait_recv()

    def sent(h, k, where):
        copy_of(h, k, 0, where, where, sibling).wait_send()

    def coefficients(p, h):
        masks = [mask[i : i + 1, :RMAX] for i in range(12)]
        leaves = [dot_nt(lines_of[h, i].astype(BF16), basis[i]) for i in range(8)]
        leaves = [(c * m).astype(BF16) for c, m in zip(leaves, masks)]
        lifted = [dot(c, transfer[i]) for i, c in enumerate(leaves)]
        above = [((lifted[2 * q] + lifted[2 * q + 1]) * masks[8 + q]).astype(BF16) for q in range(4)]
        for i, c in enumerate(leaves + above):
            small[h, pl.ds(i, PART, stride=PITCH_CLUSTER), 0:RMAX] = c.astype(F32)
        for u in range(3):
            for g in range(QUADS):
                row = small[h, pl.ds((4 * g + u) * PITCH_CLUSTER, 16), :]
                extra = small[h, pl.ds((4 * g + 3) * PITCH_CLUSTER, 16), :]
                gathered[p, h, u, 0, :, g * 128 : (g + 1) * 128] = merge(row, extra, u).astype(BF16)

    def halo_rows(h):
        return pl.ds(16 * (PART * h // 16), 16)

    def begin(p, h):
        for u, (axis, _, _) in enumerate(ROUTES):
            block = gathered.at[p, h, u]
            for step in STEPS:
                copy_of(h, G1, 0, block.at[0], block.at[-step % 4], near_by(axis, step)).start()
        if PART * (h + 1) % 16 == 0:
            rows = halo_rows(h)
            copy_of(h, HALO, 0, v.at[p, 1, rows], v.at[p, 9, rows], before).start()
            copy_of(h, HALO, 0, v.at[p, 8, rows], v.at[p, 0, rows], after).start()

    def near_part(p, lo, hi):
        if lo == 0:
            for h in range(STREAMS):
                if PART * (h + 1) % 16 == 0:
                    arrived(h, HALO, 0, v.at[p, pl.ds(0, 2), halo_rows(h)])
            v[p, 0] = (v[p, 0].astype(F32) * (me > 0).astype(F32)).astype(BF16)
            v[p, 9] = (v[p, 9].astype(F32) * (me < devices - 1).astype(F32)).astype(BF16)
        for i in range(lo, hi):
            s = dot(v[p, i], near[i, 0])
            s = s + dot(v[p, i + 1], near[i, 1])
            near_sum[i] = s + dot(v[p, i + 2], near[i, 2])

    list_copies = []
    for u, (_, _, axis) in enumerate(ROUTES):
        targets = [(near_by(axis, step, o), -step % 4 * 2 + o) for step in STEPS for o in (0, 1)] + [(sibling, 1)]
        for device, group in targets:
            list_copies.append(pltpu.make_async_remote_copy(
                src_ref=raw, dst_ref=raw_in.at[u, pl.ds(8 * group, 8)],
                send_sem=list_send.at[u], recv_sem=list_recv.at[u],
                device_id=(device,), device_id_type=MESH))

    def place_of(ids, route):
        first, second, axis = route
        device = lax.shift_right_logical(ids * 43691, 19)
        where = {a: (lax.shift_right_logical(device, n) + (4 - pos[a])) & 3 for a, n in (("x", 5), ("z", 3), ("y", 1))}
        group = where[axis] * 2 + ((device + core) & 1)
        return group, where[second] * ROWS + where[first] * 12 + (ids - 12 * device)

    ahead = ones_where(iota((128, 128), 0) < iota((128, 128), 1)).astype(BF16)

    def rows_wanted(u, k):
        within = iota((SLOTS, 128), 0).astype(F32)
        group, row = place_of(raw_in[u, pl.ds(k, 8, stride=8), :], ROUTES[u])
        rank = jnp.where(group == 0, dot(ones_where(group == 0).astype(BF16), ahead), -1.0)
        row = row.astype(F32) + 1.0
        wanted = []
        for q in range(GROUPS):
            mine = jnp.where(within == rank[q : q + 1, :], row[q : q + 1, :], 0.0)
            wanted.append(jnp.sum(mine, axis=1, keepdims=True))
        wanted = jnp.concatenate(wanted, axis=0) - 1.0
        return ones_where(iota((256, 4 * ROWS), 1).astype(F32) == wanted)

    def make_picks():
        for u in range(3):
            raw_in[u, 0:8, :] = raw[...]
            pick[u] = rows_wanted(u, 0).astype(BF16)

    def make_others():
        number = iota((256, 128), 0).astype(F32)
        for u, route in enumerate(ROUTES):
            group, _ = place_of(raw[...], route)
            slots = []
            for k in range(2):
                hit = ones_where(iota((8, 128), 0) == group[k : k + 1, :])
                rank = jnp.sum(hit * dot(hit.astype(BF16), ahead), axis=0, keepdims=True)
                slots.append(group[k : k + 1, :].astype(F32) * SLOTS + rank)
            unpick[u] = jnp.transpose(ones_where(number == slots[0]), (1, 0)).astype(BF16)
            place[u] = ones_where(number == slots[1]).astype(BF16)
            scatter[u] = jnp.transpose(rows_wanted(u, 1), (1, 0)).astype(BF16)

    def turn():
        def body(n, carry):
            for k in range(32):
                row = 32 * n + k
                wide_coupling[pl.ds(row, BLOCKS, stride=PITCH_TURN), 0:RMAX] = jnp.transpose(turned[row].astype(F32), (1, 0))
            return carry

        lax.fori_loop(0, RMAX // 32, body, 0)

    def narrow():
        def body(n, carry):
            for k in range(8):
                j = 8 * n + k
                rows = pl.ds(pl.multiple_of(j * PITCH_TURN, 8), RMAX)
                coupling[j] = wide_coupling[rows, 0:RMAX].astype(BF16)
            return carry

        lax.fori_loop(0, BLOCKS // 8, body, 0)

    def exchange(p, h, way, u):
        axis = ROUTES[u][2]
        box, to = outbox.at[p, h, way, u], inbox.at[p, h, way, u]
        targets = [(near_by(axis, step, o), step % 4 * 2 + o, -step % 4 * 2 + o) for step in STEPS for o in (0, 1)]
        for device, src, dst in targets + [(sibling, 1, 1)]:
            copy_of(h, EX + 3 * way, u, box.at[src], to.at[dst], device).start()
        inbox[p, h, way, u, 0] = outbox[p, h, way, u, 0]

    def exchanged(p, h, way, u):
        arrived(h, EX + 3 * way, u, inbox.at[p, h, way, u, pl.ds(1, 7)])

    def tiles(body):
        for n in range(WIDE // 256):
            body(slice(256 * n, 256 * n + 256), n)

    def line_copies(h, k, u, out, into, axis):
        for s, step in enumerate(STEPS):
            copy_of(h, k, u, out.at[step % 4], into.at[s], near_by(axis, step)).start()

    def stream(p, h):
        arrived(h, G1, 0, gathered.at[p, h, :, pl.ds(1, 3)])
        for u, (_, axis, _) in enumerate(ROUTES):
            plane = packed.at[p, h, u]
            packed[p, h, u, 0] = dot(compact[...], gathered[p, h, u].reshape(64, WIDE)).astype(BF16)
            for step in STEPS:
                copy_of(h, G2, u, plane.at[0], plane.at[-step % 4], near_by(axis, step)).start()
        yield
        for u in range(3):
            arrived(h, G2, u, packed.at[p, h, u, pl.ds(1, 3)])

            def picks(cols, n, u=u):
                rows = packed[p, h, u, :, :, cols].reshape(4 * ROWS, 256)
                outbox[p, h, 0, u, :, :, cols] = dot(pick[u], rows).astype(BF16).reshape(GROUPS, SLOTS, 256)

            tiles(picks)
            exchange(p, h, 0, u)
        yield
        for u in range(3):
            exchanged(p, h, 0, u)

        def unpicks(cols, n):
            parts = [dot(unpick[u], inbox[p, h, 0, u, :, :, cols].reshape(256, 256)) for u in range(3)]
            for k in range(2):
                g = 2 * n + k
                sides = [part[:, k * 128 : (k + 1) * 128] for part in parts]
                for u in range(3):
                    big_in[h, pl.ds((4 * g + u) * PITCH_BLOCK, BLOCKS), :] = sides[u]
                big_in[h, pl.ds((4 * g + 3) * PITCH_BLOCK, BLOCKS), :] = fourth(sides)

        tiles(unpicks)

        for j in range(BLOCKS):
            x = big_in[h, pl.ds(j, PART, stride=PITCH_BLOCK), 0:RMAX].astype(BF16)
            big_out[h, pl.ds(j, PART, stride=PITCH_BLOCK), 0:RMAX] = dot(x, coupling[j])
        for g in range(QUADS):
            extra = big_out[h, pl.ds((4 * g + 3) * PITCH_BLOCK, BLOCKS), :]
            for u in range(3):
                row = big_out[h, pl.ds((4 * g + u) * PITCH_BLOCK, BLOCKS), :]
                products[h, u, :, g * 128 : (g + 1) * 128] = merge(row, extra, u).astype(BF16)
        for u in range(3):
            def places(cols, n, u=u):
                terms = dot(place[u], products[h, u, :, cols]).astype(BF16)
                outbox[p, h, 1, u, :, :, cols] = terms.reshape(GROUPS, SLOTS, 256)

            tiles(places)
            exchange(p, h, 1, u)
        yield
        for u, (_, axis, _) in enumerate(ROUTES):
            exchanged(p, h, 1, u)

            def sums(cols, n, u=u):
                rows = inbox[p, h, 1, u, :, :, cols].reshape(256, 256)
                sums_out[p, h, u, :, :, cols] = dot(scatter[u], rows).astype(BF16).reshape(4, ROWS, 256)

            tiles(sums)
            line_copies(h, R2, u, sums_out.at[p, h, u], sums_in.at[p, h, u], axis)
        yield
        for u, (axis, _, _) in enumerate(ROUTES):
            arrived(h, R2, u, sums_in.at[p, h, u])
            s = sums_out[p, h, u, 0].astype(F32)
            for n in range(3):
                s = s + sums_in[p, h, u, n].astype(F32)
            ends_out[p, h, u] = dot(expand[...], s.astype(BF16)).astype(BF16).reshape(4, 16, WIDE)
            line_copies(h, R1, 0, ends_out.at[p, h, u], ends_in.at[p, h, u], axis)
        yield
        sides = []
        arrived(h, R1, 0, ends_in.at[p, h])
        for u in range(3):
            s = ends_out[p, h, u, 0].astype(F32)
            for n in range(3):
                s = s + ends_in[p, h, u, n].astype(F32)
            sides.append(s)
        for g in range(QUADS):
            here = [s[:, g * 128 : (g + 1) * 128] for s in sides]
            for u in range(3):
                small[h, pl.ds((4 * g + u) * PITCH_CLUSTER, 16), :] = here[u]
            small[h, pl.ds((4 * g + 3) * PITCH_CLUSTER, 16), :] = fourth(here)
        lines = pl.ds(PART * h, PART)
        masks = [mask[i : i + 1, :RMAX] for i in range(12)]
        fields = [(small[h, pl.ds(i, PART, stride=PITCH_CLUSTER), 0:RMAX] * masks[i]).astype(BF16) for i in range(12)]
        downs = [dot_nt(fields[8 + i // 2], transfer[i]) for i in range(8)]
        leaves = [((fields[i].astype(F32) + downs[i]) * masks[i]).astype(BF16) for i in range(8)]
        fars = [dot(leaves[i], basis[i]) for i in range(8)]
        fars = [(near_sum[i, lines] + fars[i]).astype(BF16) for i in range(8)]
        for i in range(8):
            lines_of[h, i] = fars[i].astype(F32)
        if PART * (h + 1) % 16 == 0:
            for i in range(8):
                parts = [lines_of[k, i] for k in range(h + 1 - 16 // PART, h + 1)]
                v[p + 1, 1 + i, halo_rows(h)] = jnp.concatenate(parts, axis=0).astype(BF16)

        sent(h, G1, gathered.at[p, h, :, pl.ds(1, 3)])
        sent(h, G2, packed.at[p, h, :, pl.ds(1, 3)])
        sent(h, EX, inbox.at[p, h, 0, :, pl.ds(1, 7)])
        sent(h, EX + 3, inbox.at[p, h, 1, :, pl.ds(1, 7)])
        sent(h, R2, sums_in.at[p, h])
        sent(h, R1, ends_in.at[p, h])
        if PART * (h + 1) % 16 == 0:
            sent(h, HALO, v.at[p, pl.ds(0, 2), halo_rows(h)])
        if p == 0:
            small[h] = jnp.zeros_like(small[h])
            coefficients(1, h)
            begin(1, h)
        yield

    for load in loads[:6]:
        load.wait()
    raw[0:1, :] = block_source[...]
    raw[1:2, :] = block_target[...]
    for i in range(12):
        mask[i : i + 1, :] = ones_where(iota((1, 128), 1) < ranks[0:1, i : i + 1])
    for i in range(8):
        whole = v[0, 1 + i].astype(F32)
        for h in range(STREAMS):
            lines_of[h, i] = whole[PART * h : PART * (h + 1)]
    coefficients(0, 0)
    column, line = iota((ROWS, 64), 1), iota((ROWS, 64), 0)
    same = lax.shift_right_logical(column, 4) * 12 + (column & 15) == line
    compact[...] = ones_where(same & ((column & 15) < 12)).astype(BF16)
    column, line = iota((64, ROWS), 0), iota((64, ROWS), 1)
    same = lax.shift_right_logical(column, 4) * 12 + (column & 15) == line
    expand[...] = ones_where(same & ((column & 15) < 12)).astype(BF16)
    pl.semaphore_wait(barrier, len(peers))
    for h in range(STREAMS):
        if h > 0:
            coefficients(0, h)
        begin(0, h)
        if h == 0:
            for copy in list_copies:
                copy.start()

    for p in range(2):
        streams = [stream(p, h) for h in range(STREAMS)]

        def both():
            for s in streams:
                next(s)

        both()
        if p == 0:
            for u in range(3):
                tiles_in = raw_in.at[u, pl.ds(8, 56)]
                pltpu.make_async_remote_copy(
                    src_ref=tiles_in, dst_ref=tiles_in, send_sem=list_send.at[u], recv_sem=list_recv.at[u],
                    device_id=(sibling,), device_id_type=MESH).wait()
            make_picks()
        else:
            near_part(p, 0, 4)
        both()
        if p == 0:
            make_others()
            load_coupling.wait()
            turn()
            narrow()
            load_near.wait()
            near_part(p, 0, 4)
        near_part(p, 4, 8)
        both()
        both()
        both()
        both()
    out[...] = v[1:3, 1:9]


def local(charges, basis, transfer, near_field, coupling, ranks, block_source, block_target):
    vmem = pl.BlockSpec(memory_space=pltpu.VMEM)
    hbm = pl.BlockSpec(memory_space=pl.ANY)
    both = pl.pallas_call(
        kernel,
        out_shape=jax.ShapeDtypeStruct((2, 8, RHS, LEAF), BF16),
        in_specs=[hbm] * 8,
        out_specs=vmem,
        scratch_shapes=[
            pltpu.VMEM((8, RMAX, LEAF), BF16),
            pltpu.VMEM((8, RMAX, RMAX), BF16),
            pltpu.VMEM((8, 3, LEAF, LEAF), BF16),
            pltpu.VMEM((RMAX, RMAX, BLOCKS), BF16),
            pltpu.VMEM((BLOCKS * PITCH_TURN, 128), F32),
            pltpu.VMEM((BLOCKS, RMAX, RMAX), BF16),
            pltpu.VMEM((3, 10, RHS, LEAF), BF16),
            pltpu.VMEM((STREAMS, 8, PART, LEAF), F32),
            pltpu.VMEM((8, RHS, LEAF), F32),
            pltpu.VMEM((1, 12), jnp.int32),
            pltpu.VMEM((1, BLOCKS), jnp.int32),
            pltpu.VMEM((1, BLOCKS), jnp.int32),
            pltpu.VMEM((16, 128), F32),
            pltpu.VMEM((8, 128), jnp.int32),
            pltpu.VMEM((3, 64, 128), jnp.int32),
            pltpu.VMEM((3, 256, 4 * ROWS), BF16),
            pltpu.VMEM((3, 4 * ROWS, 256), BF16),
            pltpu.VMEM((3, 128, 256), BF16),
            pltpu.VMEM((3, 256, 128), BF16),
            pltpu.VMEM((STREAMS, PART * PITCH_CLUSTER, 128), F32),
            pltpu.VMEM((STREAMS, PART * PITCH_BLOCK, 128), F32),
            pltpu.VMEM((STREAMS, PART * PITCH_BLOCK, 128), F32),
            pltpu.VMEM((STREAMS, 3, BLOCKS, WIDE), BF16),
            pltpu.VMEM((ROWS, 64), BF16),
            pltpu.VMEM((64, ROWS), BF16),
            pltpu.VMEM((2, STREAMS, 3, 4, 16, WIDE), BF16),
            pltpu.VMEM((2, STREAMS, 3, 4, ROWS, WIDE), BF16),
            pltpu.VMEM((2, STREAMS, 2, 3, GROUPS, SLOTS, WIDE), BF16),
            pltpu.VMEM((2, STREAMS, 2, 3, GROUPS, SLOTS, WIDE), BF16),
            pltpu.VMEM((2, STREAMS, 3, 4, ROWS, WIDE), BF16),
            pltpu.VMEM((2, STREAMS, 3, 3, ROWS, WIDE), BF16),
            pltpu.VMEM((2, STREAMS, 3, 4, 16, WIDE), BF16),
            pltpu.VMEM((2, STREAMS, 3, 3, 16, WIDE), BF16),
            pltpu.SemaphoreType.DMA((STREAMS, len(KINDS))),
            pltpu.SemaphoreType.DMA((STREAMS, ARRIVALS)),
            pltpu.SemaphoreType.DMA((3,)),
            pltpu.SemaphoreType.DMA((3,)),
            pltpu.SemaphoreType.DMA((8,)),
        ],
        compiler_params=pltpu.CompilerParams(
            collective_id=0, has_side_effects=True, vmem_limit_bytes=60 * 1024 * 1024
        ),
    )(charges, basis, transfer, near_field, jnp.transpose(coupling, (1, 2, 0)),
      ranks.reshape(1, 12), block_source.reshape(1, BLOCKS), block_target.reshape(1, BLOCKS))
    return both[0], both[1]


def solution(mesh):
    in_specs = (
        P("clu", None, None),
        P("clu", None, None),
        P("clu", None, None),
        P("clu", None, None, None),
        P("clu", None, None),
        P("clu"),
        P("clu"),
        P("clu"),
    )
    out_specs = (P("clu", None, None), P("clu", None, None))
    return jax.shard_map(local, mesh=mesh, in_specs=in_specs, out_specs=out_specs, check_vma=False)
```

```python
import jax
import jax.numpy as jnp
from jax import lax
from jax.experimental import pallas as pl
from jax.experimental.pallas import tpu as pltpu
from jax.sharding import PartitionSpec as P

MESH = pl.DeviceIdType.MESH
F32 = jnp.float32
BF16 = jnp.bfloat16
RMAX = 96
RHS = 32
STREAMS = 4
TOGETHER = 2
PART = RHS // STREAMS
QUADS = PART // 4
LEAF = 256
STRIDE = {"x": 32, "z": 8, "y": 2}
ROUTES = (("y", "x", "z"), ("z", "y", "x"), ("x", "z", "y"))
STEPS = (2, 1, -1)
WIDE = 128 * QUADS
GROUPS = 8
SLOTS = 32
BLOCKS = 128

G1, G2, EX, R2, R1, HALO = 0, 1, 4, 10, 13, 14
ARRIVALS = 15
KINDS = {G1: 0, G2: 1, EX: 2, EX + 3: 3, R2: 4, R1: 5, HALO: 6}
ROWS = 48
PITCH_BLOCK, PITCH_CLUSTER, PITCH_TURN = 136, 24, 104


def dot(a, b):
    return jnp.dot(a, b, preferred_element_type=F32)


def dot_nt(a, b):
    return lax.dot_general(a, b, (((1,), (1,)), ((), ())), preferred_element_type=F32)


def iota(shape, dim):
    return lax.broadcasted_iota(jnp.int32, shape, dim)


def ones_where(hit):
    return jnp.where(hit, 1.0, 0.0).astype(F32)


def merge(row, extra, u):
    return jnp.where(iota(row.shape, 1) < RMAX, row, pltpu.roll(extra, RMAX - 32 * u, 1))


def fourth(parts):
    rolled = [pltpu.roll(part, 32 + 32 * u, 1) for u, part in enumerate(parts)]
    lanes = iota(parts[0].shape, 1)
    return jnp.where(lanes < 32, rolled[0], jnp.where(lanes < 64, rolled[1], rolled[2]))


def kernel(
    charges_hbm, basis_hbm, transfer_hbm, near_hbm, coupling_hbm, ranks_hbm, source_hbm, target_hbm,
    out,
    basis, transfer, near, turned, wide_coupling, coupling, v, lines_of, near_sum, ranks, block_source, block_target,
    mask, raw, raw_in, pick, scatter, unpick, place,
    small, big_in, big_out, products, compact, expand, gathered, packed, outbox, inbox, sums_out, sums_in, ends_out, ends_in,
    send_sem, recv_sem, list_send, list_recv, load_sem,
):
    me = lax.axis_index("clu")
    devices = 128
    core = lax.rem(me, 2)
    pos = {a: lax.rem(lax.div(me, s), 4) for a, s in STRIDE.items()}

    def near_by(axis, step, other=0):
        base = me + (lax.rem(pos[axis] + (step + 4), 4) - pos[axis]) * STRIDE[axis]
        return base + (1 - 2 * core) if other else base

    sibling = me + (1 - 2 * core)
    before = lax.rem(me + devices - 1, devices)
    after = lax.rem(me + 1, devices)

    barrier = pltpu.get_barrier_semaphore()
    peers = [sibling, before, after]
    for axis in STRIDE:
        for step in STEPS:
            for other in (0, 1):
                peers.append(near_by(axis, step, other))
    for peer in peers:
        pl.semaphore_signal(barrier, inc=1, device_id=(peer,), device_id_type=MESH)

    loads = [pltpu.make_async_copy(src, dst, load_sem.at[k]) for k, (src, dst) in enumerate((
        (charges_hbm, v.at[0, pl.ds(1, 8)]), (basis_hbm, basis), (transfer_hbm, transfer), (ranks_hbm, ranks),
        (source_hbm, block_source), (target_hbm, block_target), (coupling_hbm, turned), (near_hbm, near)))]
    for load in loads:
        load.start()
    load_coupling, load_near = loads[6:]
    small[...] = jnp.zeros_like(small)
    raw[...] = jnp.zeros_like(raw)

    def copy_of(h, k, u, src, dst, device):
        return pltpu.make_async_remote_copy(
            src_ref=src, dst_ref=dst, send_sem=send_sem.at[h, KINDS[k]], recv_sem=recv_sem.at[h, k + u],
            device_id=(device,), device_id_type=MESH)

    def arrived(h, k, u, where):
        copy_of(h, k, u, where, where, sibling).wait_recv()

    def sent(h, k, where):
        copy_of(h, k, 0, where, where, sibling).wait_send()

    def coefficients(p, h):
        masks = [mask[i : i + 1, :RMAX] for i in range(12)]
        leaves = [dot_nt(lines_of[h, i].astype(BF16), basis[i]) for i in range(8)]
        leaves = [(c * m).astype(BF16) for c, m in zip(leaves, masks)]
        lifted = [dot(c, transfer[i]) for i, c in enumerate(leaves)]
        above = [((lifted[2 * q] + lifted[2 * q + 1]) * masks[8 + q]).astype(BF16) for q in range(4)]
        for i, c in enumerate(leaves + above):
            small[h, pl.ds(i, PART, stride=PITCH_CLUSTER), 0:RMAX] = c.astype(F32)
        for u in range(3):
            for g in range(QUADS):
                row = small[h, pl.ds((4 * g + u) * PITCH_CLUSTER, 16), :]
                extra = small[h, pl.ds((4 * g + 3) * PITCH_CLUSTER, 16), :]
                gathered[p, h, u, 0, :, g * 128 : (g + 1) * 128] = merge(row, extra, u).astype(BF16)

    def halo_rows(h):
        return pl.ds(16 * (PART * h // 16), 16)

    def begin(p, h):
        for u, (axis, _, _) in enumerate(ROUTES):
            block = gathered.at[p, h, u]
            for step in STEPS:
                copy_of(h, G1, 0, block.at[0], block.at[-step % 4], near_by(axis, step)).start()
        if PART * (h + 1) % 16 == 0:
            rows = halo_rows(h)
            copy_of(h, HALO, 0, v.at[p, 1, rows], v.at[p, 9, rows], before).start()
            copy_of(h, HALO, 0, v.at[p, 8, rows], v.at[p, 0, rows], after).start()

    def near_part(p, lo, hi):
        if lo == 0:
            for h in range(STREAMS):
                if PART * (h + 1) % 16 == 0:
                    arrived(h, HALO, 0, v.at[p, pl.ds(0, 2), halo_rows(h)])
            v[p, 0] = (v[p, 0].astype(F32) * (me > 0).astype(F32)).astype(BF16)
            v[p, 9] = (v[p, 9].astype(F32) * (me < devices - 1).astype(F32)).astype(BF16)
        for i in range(lo, hi):
            s = dot(v[p, i], near[i, 0])
            s = s + dot(v[p, i + 1], near[i, 1])
            near_sum[i] = s + dot(v[p, i + 2], near[i, 2])

    list_copies = []
    for u, (_, _, axis) in enumerate(ROUTES):
        targets = [(near_by(axis, step, o), -step % 4 * 2 + o) for step in STEPS for o in (0, 1)] + [(sibling, 1)]
        for device, group in targets:
            list_copies.append(pltpu.make_async_remote_copy(
                src_ref=raw, dst_ref=raw_in.at[u, pl.ds(8 * group, 8)],
                send_sem=list_send.at[u], recv_sem=list_recv.at[u],
                device_id=(device,), device_id_type=MESH))

    def place_of(ids, route):
        first, second, axis = route
        device = lax.shift_right_logical(ids * 43691, 19)
        where = {a: (lax.shift_right_logical(device, n) + (4 - pos[a])) & 3 for a, n in (("x", 5), ("z", 3), ("y", 1))}
        group = where[axis] * 2 + ((device + core) & 1)
        return group, where[second] * ROWS + where[first] * 12 + (ids - 12 * device)

    ahead = ones_where(iota((128, 128), 0) < iota((128, 128), 1)).astype(BF16)

    def rows_wanted(u, k):
        within = iota((SLOTS, 128), 0).astype(F32)
        group, row = place_of(raw_in[u, pl.ds(k, 8, stride=8), :], ROUTES[u])
        rank = jnp.where(group == 0, dot(ones_where(group == 0).astype(BF16), ahead), -1.0)
        row = row.astype(F32) + 1.0
        wanted = []
        for q in range(GROUPS):
            mine = jnp.where(within == rank[q : q + 1, :], row[q : q + 1, :], 0.0)
            wanted.append(jnp.sum(mine, axis=1, keepdims=True))
        wanted = jnp.concatenate(wanted, axis=0) - 1.0
        return ones_where(iota((256, 4 * ROWS), 1).astype(F32) == wanted)

    def make_picks():
        for u in range(3):
            raw_in[u, 0:8, :] = raw[...]
            pick[u] = rows_wanted(u, 0).astype(BF16)

    def make_others():
        number = iota((256, 128), 0).astype(F32)
        for u, route in enumerate(ROUTES):
            group, _ = place_of(raw[...], route)
            slots = []
            for k in range(2):
                hit = ones_where(iota((8, 128), 0) == group[k : k + 1, :])
                rank = jnp.sum(hit * dot(hit.astype(BF16), ahead), axis=0, keepdims=True)
                slots.append(group[k : k + 1, :].astype(F32) * SLOTS + rank)
            unpick[u] = jnp.transpose(ones_where(number == slots[0]), (1, 0)).astype(BF16)
            place[u] = ones_where(number == slots[1]).astype(BF16)
            scatter[u] = jnp.transpose(rows_wanted(u, 1), (1, 0)).astype(BF16)

    def turn():
        def body(n, carry):
            for k in range(32):
                row = 32 * n + k
                wide_coupling[pl.ds(row, BLOCKS, stride=PITCH_TURN), 0:RMAX] = jnp.transpose(turned[row].astype(F32), (1, 0))
            return carry

        lax.fori_loop(0, RMAX // 32, body, 0)

    def narrow():
        def body(n, carry):
            for k in range(8):
                j = 8 * n + k
                rows = pl.ds(pl.multiple_of(j * PITCH_TURN, 8), RMAX)
                coupling[j] = wide_coupling[rows, 0:RMAX].astype(BF16)
            return carry

        lax.fori_loop(0, BLOCKS // 8, body, 0)

    def exchange(p, h, way, u):
        axis = ROUTES[u][2]
        box, to = outbox.at[p, h, way, u], inbox.at[p, h, way, u]
        targets = [(near_by(axis, step, o), step % 4 * 2 + o, -step % 4 * 2 + o) for step in STEPS for o in (0, 1)]
        for device, src, dst in targets + [(sibling, 1, 1)]:
            copy_of(h, EX + 3 * way, u, box.at[src], to.at[dst], device).start()

    def fill_boxes(p, h, way, u, selector, rows):
        for n in range(0, WIDE, 256):
            cols = slice(n, n + 256)
            boxes = dot(selector, rows[:, cols]).astype(BF16).reshape(GROUPS, SLOTS, 256)
            outbox[p, h, way, u, 1:GROUPS, :, cols] = boxes[1:GROUPS]
            inbox[p, h, way, u, 0, :, cols] = boxes[0]

    def exchanged(p, h, way, u):
        arrived(h, EX + 3 * way, u, inbox.at[p, h, way, u, pl.ds(1, 7)])

    def line_copies(h, k, u, out, into, axis):
        for s, step in enumerate(STEPS):
            copy_of(h, k, u, out.at[step % 4], into.at[s], near_by(axis, step)).start()

    def stream(p, h):
        arrived(h, G1, 0, gathered.at[p, h, :, pl.ds(1, 3)])
        for u in range(3):
            packed[p, h, u, 0] = dot(compact[...], gathered[p, h, u].reshape(64, WIDE)).astype(BF16)
        for u, (_, axis, _) in enumerate(ROUTES):
            plane = packed.at[p, h, u]
            for step in STEPS:
                copy_of(h, G2, u, plane.at[0], plane.at[-step % 4], near_by(axis, step)).start()
        yield
        for u in range(3):
            arrived(h, G2, u, packed.at[p, h, u, pl.ds(1, 3)])
        for u in range(3):
            fill_boxes(p, h, 0, u, pick[u], packed[p, h, u].reshape(4 * ROWS, WIDE))
        for u in range(3):
            exchange(p, h, 0, u)
        yield
        batch, first_row = h // TOGETHER, PART * (h % TOGETHER)
        for u in range(3):
            exchanged(p, h, 0, u)

        for n in range(0, WIDE, 256):
            parts = [dot(unpick[u], inbox[p, h, 0, u, :, :, n : n + 256].reshape(256, 256)) for u in range(3)]
            for k in range(2):
                g = n // 128 + k
                sides = [part[:, k * 128 : (k + 1) * 128] for part in parts]
                for k, side in enumerate(sides + [fourth(sides)]):
                    big_in[batch, pl.ds((first_row + 4 * g + k) * PITCH_BLOCK, BLOCKS), :] = side

        if (h + 1) % TOGETHER == 0:
            lines_at_once = PART * TOGETHER
            for j in range(BLOCKS):
                x = big_in[batch, pl.ds(j, lines_at_once, stride=PITCH_BLOCK), 0:RMAX].astype(BF16)
                big_out[batch, pl.ds(j, lines_at_once, stride=PITCH_BLOCK), 0:RMAX] = dot(x, coupling[j])
            for k in range(h + 1 - TOGETHER, h + 1):
                for g in range(QUADS):
                    row = PART * (k % TOGETHER) + 4 * g
                    parts = [big_out[batch, pl.ds((row + u) * PITCH_BLOCK, BLOCKS), :] for u in range(4)]
                    for u in range(3):
                        products[k, u, :, g * 128 : (g + 1) * 128] = merge(parts[u], parts[3], u).astype(BF16)
                for u in range(3):
                    fill_boxes(p, k, 1, u, place[u], products[k, u])
                for u in range(3):
                    exchange(p, k, 1, u)
        yield
        for u in range(3):
            exchanged(p, h, 1, u)
        for u in range(3):
            for n in range(0, WIDE, 256):
                rows = inbox[p, h, 1, u, :, :, n : n + 256].reshape(256, 256)
                sums_out[p, h, u, :, :, n : n + 256] = dot(scatter[u], rows).astype(BF16).reshape(4, ROWS, 256)
        for u, (_, axis, _) in enumerate(ROUTES):
            line_copies(h, R2, u, sums_out.at[p, h, u], sums_in.at[p, h, u], axis)
        yield
        for u in range(3):
            arrived(h, R2, u, sums_in.at[p, h, u])
        for u in range(3):
            s = sums_out[p, h, u, 0].astype(F32)
            for n in range(3):
                s = s + sums_in[p, h, u, n].astype(F32)
            ends_out[p, h, u] = dot(expand[...], s.astype(BF16)).astype(BF16).reshape(4, 16, WIDE)
        for u, (axis, _, _) in enumerate(ROUTES):
            line_copies(h, R1, 0, ends_out.at[p, h, u], ends_in.at[p, h, u], axis)
        yield
        sides = []
        arrived(h, R1, 0, ends_in.at[p, h])
        for u in range(3):
            s = ends_out[p, h, u, 0].astype(F32)
            for n in range(3):
                s = s + ends_in[p, h, u, n].astype(F32)
            sides.append(s)
        for g in range(QUADS):
            here = [s[:, g * 128 : (g + 1) * 128] for s in sides]
            for u in range(3):
                small[h, pl.ds((4 * g + u) * PITCH_CLUSTER, 16), :] = here[u]
            small[h, pl.ds((4 * g + 3) * PITCH_CLUSTER, 16), :] = fourth(here)
        lines = pl.ds(PART * h, PART)
        masks = [mask[i : i + 1, :RMAX] for i in range(12)]
        fields = [(small[h, pl.ds(i, PART, stride=PITCH_CLUSTER), 0:RMAX] * masks[i]).astype(BF16) for i in range(12)]
        downs = [dot_nt(fields[8 + i // 2], transfer[i]) for i in range(8)]
        leaves = [((fields[i].astype(F32) + downs[i]) * masks[i]).astype(BF16) for i in range(8)]
        fars = [dot(leaves[i], basis[i]) for i in range(8)]
        fars = [(near_sum[i, lines] + fars[i]).astype(BF16) for i in range(8)]
        for i in range(8):
            lines_of[h, i] = fars[i].astype(F32)
        if PART * (h + 1) % 16 == 0:
            for i in range(8):
                parts = [lines_of[k, i] for k in range(h + 1 - 16 // PART, h + 1)]
                v[p + 1, 1 + i, halo_rows(h)] = jnp.concatenate(parts, axis=0).astype(BF16)

        sent(h, G1, gathered.at[p, h, :, pl.ds(1, 3)])
        sent(h, G2, packed.at[p, h, :, pl.ds(1, 3)])
        sent(h, EX, inbox.at[p, h, 0, :, pl.ds(1, 7)])
        sent(h, EX + 3, inbox.at[p, h, 1, :, pl.ds(1, 7)])
        sent(h, R2, sums_in.at[p, h])
        sent(h, R1, ends_in.at[p, h])
        if PART * (h + 1) % 16 == 0:
            sent(h, HALO, v.at[p, pl.ds(0, 2), halo_rows(h)])
        if p == 0:
            small[h] = jnp.zeros_like(small[h])
            coefficients(1, h)
            begin(1, h)
        yield

    for load in loads[:6]:
        load.wait()
    raw[0:1, :] = block_source[...]
    raw[1:2, :] = block_target[...]
    for i in range(12):
        mask[i : i + 1, :] = ones_where(iota((1, 128), 1) < ranks[0:1, i : i + 1])
    for i in range(8):
        whole = v[0, 1 + i].astype(F32)
        for h in range(STREAMS):
            lines_of[h, i] = whole[PART * h : PART * (h + 1)]
    coefficients(0, 0)
    column, line = iota((ROWS, 64), 1), iota((ROWS, 64), 0)
    same = lax.shift_right_logical(column, 4) * 12 + (column & 15) == line
    compact[...] = ones_where(same & ((column & 15) < 12)).astype(BF16)
    column, line = iota((64, ROWS), 0), iota((64, ROWS), 1)
    same = lax.shift_right_logical(column, 4) * 12 + (column & 15) == line
    expand[...] = ones_where(same & ((column & 15) < 12)).astype(BF16)
    pl.semaphore_wait(barrier, len(peers))
    for h in range(STREAMS):
        if h > 0:
            coefficients(0, h)
        begin(0, h)
        if h == 0:
            for copy in list_copies:
                copy.start()

    for p in range(2):
        streams = [stream(p, h) for h in range(STREAMS)]

        def both():
            for s in streams:
                next(s)

        both()
        if p == 0:
            for u in range(3):
                tiles_in = raw_in.at[u, pl.ds(8, 56)]
                pltpu.make_async_remote_copy(
                    src_ref=tiles_in, dst_ref=tiles_in, send_sem=list_send.at[u], recv_sem=list_recv.at[u],
                    device_id=(sibling,), device_id_type=MESH).wait()
            make_picks()
        else:
            near_part(p, 0, 4)
        both()
        if p == 0:
            make_others()
            load_coupling.wait()
            turn()
            narrow()
            load_near.wait()
            near_part(p, 0, 4)
        near_part(p, 4, 8)
        both()
        both()
        both()
        both()
    out[...] = v[1:3, 1:9]


def local(charges, basis, transfer, near_field, coupling, ranks, block_source, block_target):
    vmem = pl.BlockSpec(memory_space=pltpu.VMEM)
    hbm = pl.BlockSpec(memory_space=pl.ANY)
    both = pl.pallas_call(
        kernel,
        out_shape=jax.ShapeDtypeStruct((2, 8, RHS, LEAF), BF16),
        in_specs=[hbm] * 8,
        out_specs=vmem,
        scratch_shapes=[
            pltpu.VMEM((8, RMAX, LEAF), BF16),
            pltpu.VMEM((8, RMAX, RMAX), BF16),
            pltpu.VMEM((8, 3, LEAF, LEAF), BF16),
            pltpu.VMEM((RMAX, RMAX, BLOCKS), BF16),
            pltpu.VMEM((BLOCKS * PITCH_TURN, 128), F32),
            pltpu.VMEM((BLOCKS, RMAX, RMAX), BF16),
            pltpu.VMEM((3, 10, RHS, LEAF), BF16),
            pltpu.VMEM((STREAMS, 8, PART, LEAF), F32),
            pltpu.VMEM((8, RHS, LEAF), F32),
            pltpu.VMEM((1, 12), jnp.int32),
            pltpu.VMEM((1, BLOCKS), jnp.int32),
            pltpu.VMEM((1, BLOCKS), jnp.int32),
            pltpu.VMEM((16, 128), F32),
            pltpu.VMEM((8, 128), jnp.int32),
            pltpu.VMEM((3, 64, 128), jnp.int32),
            pltpu.VMEM((3, 256, 4 * ROWS), BF16),
            pltpu.VMEM((3, 4 * ROWS, 256), BF16),
            pltpu.VMEM((3, 128, 256), BF16),
            pltpu.VMEM((3, 256, 128), BF16),
            pltpu.VMEM((STREAMS, PART * PITCH_CLUSTER, 128), F32),
            pltpu.VMEM((STREAMS // TOGETHER, PART * TOGETHER * PITCH_BLOCK, 128), F32),
            pltpu.VMEM((STREAMS // TOGETHER, PART * TOGETHER * PITCH_BLOCK, 128), F32),
            pltpu.VMEM((STREAMS, 3, BLOCKS, WIDE), BF16),
            pltpu.VMEM((ROWS, 64), BF16),
            pltpu.VMEM((64, ROWS), BF16),
            pltpu.VMEM((2, STREAMS, 3, 4, 16, WIDE), BF16),
            pltpu.VMEM((2, STREAMS, 3, 4, ROWS, WIDE), BF16),
            pltpu.VMEM((2, STREAMS, 2, 3, GROUPS, SLOTS, WIDE), BF16),
            pltpu.VMEM((2, STREAMS, 2, 3, GROUPS, SLOTS, WIDE), BF16),
            pltpu.VMEM((2, STREAMS, 3, 4, ROWS, WIDE), BF16),
            pltpu.VMEM((2, STREAMS, 3, 3, ROWS, WIDE), BF16),
            pltpu.VMEM((2, STREAMS, 3, 4, 16, WIDE), BF16),
            pltpu.VMEM((2, STREAMS, 3, 3, 16, WIDE), BF16),
            pltpu.SemaphoreType.DMA((STREAMS, len(KINDS))),
            pltpu.SemaphoreType.DMA((STREAMS, ARRIVALS)),
            pltpu.SemaphoreType.DMA((3,)),
            pltpu.SemaphoreType.DMA((3,)),
            pltpu.SemaphoreType.DMA((8,)),
        ],
        compiler_params=pltpu.CompilerParams(
            collective_id=0, has_side_effects=True, vmem_limit_bytes=60 * 1024 * 1024
        ),
    )(charges, basis, transfer, near_field, jnp.transpose(coupling, (1, 2, 0)),
      ranks.reshape(1, 12), block_source.reshape(1, BLOCKS), block_target.reshape(1, BLOCKS))
    return both[0], both[1]


def solution(mesh):
    in_specs = (
        P("clu", None, None),
        P("clu", None, None),
        P("clu", None, None),
        P("clu", None, None, None),
        P("clu", None, None),
        P("clu"),
        P("clu"),
        P("clu"),
    )
    out_specs = (P("clu", None, None), P("clu", None, None))
    return jax.shard_map(local, mesh=mesh, in_specs=in_specs, out_specs=out_specs, check_vma=False)
```

```python
import jax
import jax.numpy as jnp
from jax import lax
from jax.experimental import pallas as pl
from jax.experimental.pallas import tpu as pltpu
from jax.sharding import PartitionSpec as P

MESH = pl.DeviceIdType.MESH
F32 = jnp.float32
BF16 = jnp.bfloat16
RMAX = 96
RHS = 32
STREAMS = 4
TOGETHER = 2
PART = RHS // STREAMS
QUADS = PART // 4
LEAF = 256
STRIDE = {"x": 32, "z": 8, "y": 2}
ROUTES = (("y", "x", "z"), ("z", "y", "x"), ("x", "z", "y"))
STEPS = (2, 1, -1)
WIDE = 128 * QUADS
GROUPS = 8
SLOTS = 32
BLOCKS = 128

G1, G2, EX, BACK, R2, R1, HALO = range(7)
ROWS = 48
PITCH_BLOCK, PITCH_CLUSTER, PITCH_TURN = 136, 24, 104


def dot(a, b):
    return jnp.dot(a, b, preferred_element_type=F32)


def dot_nt(a, b):
    return lax.dot_general(a, b, (((1,), (1,)), ((), ())), preferred_element_type=F32)


def iota(shape, dim):
    return lax.broadcasted_iota(jnp.int32, shape, dim)


def ones_where(hit):
    return jnp.where(hit, 1.0, 0.0).astype(F32)


def merge(row, extra, u):
    return jnp.where(iota(row.shape, 1) < RMAX, row, pltpu.roll(extra, RMAX - 32 * u, 1))


def fourth(parts):
    rolled = [pltpu.roll(part, 32 + 32 * u, 1) for u, part in enumerate(parts)]
    lanes = iota(parts[0].shape, 1)
    return jnp.where(lanes < 32, rolled[0], jnp.where(lanes < 64, rolled[1], rolled[2]))


def kernel(
    charges_hbm, basis_hbm, transfer_hbm, near_hbm, coupling_hbm, ranks_hbm, source_hbm, target_hbm,
    out,
    basis, transfer, near, turned, wide_coupling, coupling, v, lines_of, near_sum, ranks, block_source, block_target,
    mask, raw, raw_in, pick, scatter, unpick, place,
    small, big_in, big_out, products, compact, expand, gathered, packed, outbox, inbox, sums_out, sums_in, ends_out, ends_in,
    send_sem, recv_sem, list_send, list_recv, load_sem,
):
    me = lax.axis_index("clu")
    devices = 128
    core = lax.rem(me, 2)
    pos = {a: lax.rem(lax.div(me, s), 4) for a, s in STRIDE.items()}

    def near_by(axis, step, other=0):
        base = me + (lax.rem(pos[axis] + (step + 4), 4) - pos[axis]) * STRIDE[axis]
        return base + (1 - 2 * core) if other else base

    sibling = me + (1 - 2 * core)
    before = lax.rem(me + devices - 1, devices)
    after = lax.rem(me + 1, devices)

    barrier = pltpu.get_barrier_semaphore()
    peers = [sibling, before, after]
    for axis in STRIDE:
        for step in STEPS:
            for other in (0, 1):
                peers.append(near_by(axis, step, other))
    for peer in peers:
        pl.semaphore_signal(barrier, inc=1, device_id=(peer,), device_id_type=MESH)

    loads = [pltpu.make_async_copy(src, dst, load_sem.at[k]) for k, (src, dst) in enumerate((
        (charges_hbm, v.at[0, pl.ds(1, 8)]), (basis_hbm, basis), (transfer_hbm, transfer), (ranks_hbm, ranks),
        (source_hbm, block_source), (target_hbm, block_target), (coupling_hbm, turned), (near_hbm, near)))]
    for load in loads:
        load.start()
    load_coupling, load_near = loads[6:]
    small[...] = jnp.zeros_like(small)
    raw[...] = jnp.zeros_like(raw)

    def copy_of(h, k, src, dst, device):
        return pltpu.make_async_remote_copy(
            src_ref=src, dst_ref=dst, send_sem=send_sem.at[k], recv_sem=recv_sem.at[h, k],
            device_id=(device,), device_id_type=MESH)

    def arrived(h, k, where):
        copy_of(h, k, where, where, sibling).wait_recv()

    def sent(k, where):
        copy_of(0, k, where, where, sibling).wait_send()

    def coefficients(p, streams):
        masks = [mask[i : i + 1, :RMAX] for i in range(12)]
        fields = [jnp.concatenate([lines_of[h, i] for h in streams], axis=0).astype(BF16) for i in range(8)]
        leaves = [dot_nt(fields[i], basis[i]) for i in range(8)]
        leaves = [(c * m).astype(BF16) for c, m in zip(leaves, masks)]
        lifted = [dot(c, transfer[i]) for i, c in enumerate(leaves)]
        above = [((lifted[2 * q] + lifted[2 * q + 1]) * masks[8 + q]).astype(BF16) for q in range(4)]
        for i, c in enumerate(leaves + above):
            c = c.astype(F32)
            for k, h in enumerate(streams):
                small[h, pl.ds(i, PART, stride=PITCH_CLUSTER), 0:RMAX] = c[PART * k : PART * (k + 1)]
        for h in streams:
            for u in range(3):
                for g in range(QUADS):
                    row = small[h, pl.ds((4 * g + u) * PITCH_CLUSTER, 16), :]
                    extra = small[h, pl.ds((4 * g + 3) * PITCH_CLUSTER, 16), :]
                    gathered[p, h, u, 0, :, g * 128 : (g + 1) * 128] = merge(row, extra, u).astype(BF16)

    def halo_rows(h):
        return pl.ds(16 * (PART * h // 16), 16)

    def begin(p, h):
        for u, (axis, _, _) in enumerate(ROUTES):
            block = gathered.at[p, h, u]
            for step in STEPS:
                copy_of(h, G1, block.at[0], block.at[-step % 4], near_by(axis, step)).start()
        if PART * (h + 1) % 16 == 0:
            rows = halo_rows(h)
            copy_of(h, HALO, v.at[p, 1, rows], v.at[p, 9, rows], before).start()
            copy_of(h, HALO, v.at[p, 8, rows], v.at[p, 0, rows], after).start()

    def near_part(p, lo, hi):
        if lo == 0:
            for h in range(STREAMS):
                if PART * (h + 1) % 16 == 0:
                    arrived(h, HALO, v.at[p, pl.ds(0, 2), halo_rows(h)])
            v[p, 0] = (v[p, 0].astype(F32) * (me > 0).astype(F32)).astype(BF16)
            v[p, 9] = (v[p, 9].astype(F32) * (me < devices - 1).astype(F32)).astype(BF16)
        for i in range(lo, hi):
            s = dot(v[p, i], near[i, 0])
            s = s + dot(v[p, i + 1], near[i, 1])
            near_sum[i] = s + dot(v[p, i + 2], near[i, 2])

    list_copies = []
    for u, (_, _, axis) in enumerate(ROUTES):
        targets = [(near_by(axis, step, o), -step % 4 * 2 + o) for step in STEPS for o in (0, 1)] + [(sibling, 1)]
        for device, group in targets:
            list_copies.append(pltpu.make_async_remote_copy(
                src_ref=raw, dst_ref=raw_in.at[u, pl.ds(8 * group, 8)],
                send_sem=list_send.at[0], recv_sem=list_recv.at[0],
                device_id=(device,), device_id_type=MESH))

    def place_of(ids, route):
        first, second, axis = route
        device = lax.shift_right_logical(ids * 43691, 19)
        where = {a: (lax.shift_right_logical(device, n) + (4 - pos[a])) & 3 for a, n in (("x", 5), ("z", 3), ("y", 1))}
        group = where[axis] * 2 + ((device + core) & 1)
        return group, where[second] * ROWS + where[first] * 12 + (ids - 12 * device)

    ahead = ones_where(iota((128, 128), 0) < iota((128, 128), 1)).astype(BF16)

    def rows_wanted(u, k):
        within = iota((SLOTS, 128), 0).astype(F32)
        group, row = place_of(raw_in[u, pl.ds(k, 8, stride=8), :], ROUTES[u])
        rank = jnp.where(group == 0, dot(ones_where(group == 0).astype(BF16), ahead), -1.0)
        row = row.astype(F32) + 1.0
        wanted = []
        for q in range(GROUPS):
            mine = jnp.where(within == rank[q : q + 1, :], row[q : q + 1, :], 0.0)
            wanted.append(jnp.sum(mine, axis=1, keepdims=True))
        wanted = jnp.concatenate(wanted, axis=0) - 1.0
        return ones_where(iota((256, 4 * ROWS), 1).astype(F32) == wanted)

    def make_picks():
        for u in range(3):
            raw_in[u, 0:8, :] = raw[...]
            pick[u] = rows_wanted(u, 0).astype(BF16)

    def make_own():
        number = iota((256, 128), 0).astype(F32)
        for u, route in enumerate(ROUTES):
            group, _ = place_of(raw[...], route)
            slots = []
            for k in range(2):
                hit = ones_where(iota((8, 128), 0) == group[k : k + 1, :])
                rank = jnp.sum(hit * dot(hit.astype(BF16), ahead), axis=0, keepdims=True)
                slots.append(group[k : k + 1, :].astype(F32) * SLOTS + rank)
            unpick[u] = jnp.transpose(ones_where(number == slots[0]), (1, 0)).astype(BF16)
            place[u] = ones_where(number == slots[1]).astype(BF16)

    def make_sums():
        for u in range(3):
            scatter[u] = jnp.transpose(rows_wanted(u, 1), (1, 0)).astype(BF16)

    def turn():
        def body(n, carry):
            for k in range(32):
                row = 32 * n + k
                wide_coupling[pl.ds(row, BLOCKS, stride=PITCH_TURN), 0:RMAX] = jnp.transpose(turned[row].astype(F32), (1, 0))
            return carry

        lax.fori_loop(0, RMAX // 32, body, 0)

    def narrow():
        def body(n, carry):
            for k in range(8):
                j = 8 * n + k
                rows = pl.ds(pl.multiple_of(j * PITCH_TURN, 8), RMAX)
                coupling[j] = wide_coupling[rows, 0:RMAX].astype(BF16)
            return carry

        lax.fori_loop(0, BLOCKS // 8, body, 0)

    def exchange(p, h, way, u):
        axis = ROUTES[u][2]
        box, to = outbox.at[p, h, way, u], inbox.at[p, h, way, u]
        targets = [(near_by(axis, step, o), step % 4 * 2 + o, -step % 4 * 2 + o) for step in STEPS for o in (0, 1)]
        for device, src, dst in targets + [(sibling, 1, 1)]:
            copy_of(h, BACK if way else EX, box.at[src], to.at[dst], device).start()

    def fill_boxes(p, h, way, u, selector, rows):
        for n in range(0, WIDE, 256):
            cols = slice(n, n + 256)
            boxes = dot(selector, rows[:, cols]).astype(BF16).reshape(GROUPS, SLOTS, 256)
            outbox[p, h, way, u, 1:GROUPS, :, cols] = boxes[1:GROUPS]
            inbox[p, h, way, u, 0, :, cols] = boxes[0]

    def exchanged(p, h, way):
        arrived(h, BACK if way else EX, inbox.at[p, h, way, :, pl.ds(1, 7)])

    def line_copies(h, k, out, into, axis):
        for s, step in enumerate(STEPS):
            copy_of(h, k, out.at[step % 4], into.at[s], near_by(axis, step)).start()

    def stream(p, h):
        arrived(h, G1, gathered.at[p, h, :, pl.ds(1, 3)])
        for u in range(3):
            packed[p, h, u, 0] = dot(compact[...], gathered[p, h, u].reshape(64, WIDE)).astype(BF16)
        for u, (_, axis, _) in enumerate(ROUTES):
            plane = packed.at[p, h, u]
            for step in STEPS:
                copy_of(h, G2, plane.at[0], plane.at[-step % 4], near_by(axis, step)).start()
        yield
        arrived(h, G2, packed.at[p, h, :, pl.ds(1, 3)])
        for u in range(3):
            fill_boxes(p, h, 0, u, pick[u], packed[p, h, u].reshape(4 * ROWS, WIDE))
        for u in range(3):
            exchange(p, h, 0, u)
        yield
        batch, first_row = h // TOGETHER, PART * (h % TOGETHER)
        exchanged(p, h, 0)

        for n in range(0, WIDE, 256):
            parts = [dot(unpick[u], inbox[p, h, 0, u, :, :, n : n + 256].reshape(256, 256)) for u in range(3)]
            for k in range(2):
                g = n // 128 + k
                sides = [part[:, k * 128 : (k + 1) * 128] for part in parts]
                for k, side in enumerate(sides + [fourth(sides)]):
                    big_in[batch, pl.ds((first_row + 4 * g + k) * PITCH_BLOCK, BLOCKS), :] = side

        if (h + 1) % TOGETHER == 0:
            lines_at_once = PART * TOGETHER
            for j in range(BLOCKS):
                x = big_in[batch, pl.ds(j, lines_at_once, stride=PITCH_BLOCK), 0:RMAX].astype(BF16)
                big_out[batch, pl.ds(j, lines_at_once, stride=PITCH_BLOCK), 0:RMAX] = dot(x, coupling[j])
            for k in range(h + 1 - TOGETHER, h + 1):
                for g in range(QUADS):
                    row = PART * (k % TOGETHER) + 4 * g
                    parts = [big_out[batch, pl.ds((row + u) * PITCH_BLOCK, BLOCKS), :] for u in range(4)]
                    for u in range(3):
                        products[k, u, :, g * 128 : (g + 1) * 128] = merge(parts[u], parts[3], u).astype(BF16)
                for u in range(3):
                    fill_boxes(p, k, 1, u, place[u], products[k, u])
                for u in range(3):
                    exchange(p, k, 1, u)
        yield
        exchanged(p, h, 1)
        for u in range(3):
            for n in range(0, WIDE, 256):
                rows = inbox[p, h, 1, u, :, :, n : n + 256].reshape(256, 256)
                sums_out[p, h, u, :, :, n : n + 256] = dot(scatter[u], rows).astype(BF16).reshape(4, ROWS, 256)
        for u, (_, axis, _) in enumerate(ROUTES):
            line_copies(h, R2, sums_out.at[p, h, u], sums_in.at[p, h, u], axis)
        yield
        arrived(h, R2, sums_in.at[p, h])
        for u in range(3):
            s = sums_out[p, h, u, 0].astype(F32)
            for n in range(3):
                s = s + sums_in[p, h, u, n].astype(F32)
            ends_out[p, h, u] = dot(expand[...], s.astype(BF16)).astype(BF16).reshape(4, 16, WIDE)
        for u, (axis, _, _) in enumerate(ROUTES):
            line_copies(h, R1, ends_out.at[p, h, u], ends_in.at[p, h, u], axis)
        yield
        sides = []
        arrived(h, R1, ends_in.at[p, h])
        for u in range(3):
            s = ends_out[p, h, u, 0].astype(F32)
            for n in range(3):
                s = s + ends_in[p, h, u, n].astype(F32)
            sides.append(s)
        for g in range(QUADS):
            here = [s[:, g * 128 : (g + 1) * 128] for s in sides]
            for u in range(3):
                small[h, pl.ds((4 * g + u) * PITCH_CLUSTER, 16), :] = here[u]
            small[h, pl.ds((4 * g + 3) * PITCH_CLUSTER, 16), :] = fourth(here)
        lines = pl.ds(PART * h, PART)
        masks = [mask[i : i + 1, :RMAX] for i in range(12)]
        fields = [(small[h, pl.ds(i, PART, stride=PITCH_CLUSTER), 0:RMAX] * masks[i]).astype(BF16) for i in range(12)]
        downs = [dot_nt(fields[8 + i // 2], transfer[i]) for i in range(8)]
        leaves = [((fields[i].astype(F32) + downs[i]) * masks[i]).astype(BF16) for i in range(8)]
        fars = [dot(leaves[i], basis[i]) for i in range(8)]
        fars = [(near_sum[i, lines] + fars[i]).astype(BF16) for i in range(8)]
        for i in range(8):
            lines_of[h, i] = fars[i].astype(F32)
        if PART * (h + 1) % 16 == 0:
            for i in range(8):
                parts = [lines_of[k, i] for k in range(h + 1 - 16 // PART, h + 1)]
                v[p + 1, 1 + i, halo_rows(h)] = jnp.concatenate(parts, axis=0).astype(BF16)

        if p == 0:
            coefficients(1, [h])
            begin(1, h)
        yield

    for load in loads[:6]:
        load.wait()
    raw[0:1, :] = block_source[...]
    raw[1:2, :] = block_target[...]
    for i in range(12):
        mask[i : i + 1, :] = ones_where(iota((1, 128), 1) < ranks[0:1, i : i + 1])
    for i in range(8):
        whole = v[0, 1 + i].astype(F32)
        for h in range(STREAMS):
            lines_of[h, i] = whole[PART * h : PART * (h + 1)]
    coefficients(0, range(STREAMS))
    column, line = iota((ROWS, 64), 1), iota((ROWS, 64), 0)
    same = lax.shift_right_logical(column, 4) * 12 + (column & 15) == line
    compact[...] = ones_where(same & ((column & 15) < 12)).astype(BF16)
    column, line = iota((64, ROWS), 0), iota((64, ROWS), 1)
    same = lax.shift_right_logical(column, 4) * 12 + (column & 15) == line
    expand[...] = ones_where(same & ((column & 15) < 12)).astype(BF16)
    pl.semaphore_wait(barrier, len(peers))
    for h in range(STREAMS):
        begin(0, h)
    for copy in list_copies:
        copy.start()
    make_own()
    load_coupling.wait()
    turn()

    for p in range(2):
        streams = [stream(p, h) for h in range(STREAMS)]

        def both():
            for s in streams:
                next(s)

        both()
        if p == 0:
            tiles_in = raw_in.at[:, pl.ds(8, 56)]
            pltpu.make_async_remote_copy(
                src_ref=tiles_in, dst_ref=tiles_in, send_sem=list_send.at[0], recv_sem=list_recv.at[0],
                device_id=(sibling,), device_id_type=MESH).wait()
            make_picks()
        else:
            near_part(p, 0, 4)
        both()
        if p == 0:
            make_sums()
            narrow()
            load_near.wait()
            near_part(p, 0, 4)
        near_part(p, 4, 8)
        both()
        both()
        both()
        both()
    out[...] = v[1:3, 1:9]
    sent(G1, gathered.at[:, :, :, pl.ds(1, 3)])
    sent(G2, packed.at[:, :, :, pl.ds(1, 3)])
    sent(EX, inbox.at[:, :, 0, :, pl.ds(1, 7)])
    sent(BACK, inbox.at[:, :, 1, :, pl.ds(1, 7)])
    sent(R2, sums_in)
    sent(R1, ends_in)
    sent(HALO, v.at[0, pl.ds(0, 4)])


def local(charges, basis, transfer, near_field, coupling, ranks, block_source, block_target):
    vmem = pl.BlockSpec(memory_space=pltpu.VMEM)
    hbm = pl.BlockSpec(memory_space=pl.ANY)
    both = pl.pallas_call(
        kernel,
        out_shape=jax.ShapeDtypeStruct((2, 8, RHS, LEAF), BF16),
        in_specs=[hbm] * 8,
        out_specs=vmem,
        scratch_shapes=[
            pltpu.VMEM((8, RMAX, LEAF), BF16),
            pltpu.VMEM((8, RMAX, RMAX), BF16),
            pltpu.VMEM((8, 3, LEAF, LEAF), BF16),
            pltpu.VMEM((RMAX, RMAX, BLOCKS), BF16),
            pltpu.VMEM((BLOCKS * PITCH_TURN, 128), F32),
            pltpu.VMEM((BLOCKS, RMAX, RMAX), BF16),
            pltpu.VMEM((3, 10, RHS, LEAF), BF16),
            pltpu.VMEM((STREAMS, 8, PART, LEAF), F32),
            pltpu.VMEM((8, RHS, LEAF), F32),
            pltpu.VMEM((1, 12), jnp.int32),
            pltpu.VMEM((1, BLOCKS), jnp.int32),
            pltpu.VMEM((1, BLOCKS), jnp.int32),
            pltpu.VMEM((16, 128), F32),
            pltpu.VMEM((8, 128), jnp.int32),
            pltpu.VMEM((3, 64, 128), jnp.int32),
            pltpu.VMEM((3, 256, 4 * ROWS), BF16),
            pltpu.VMEM((3, 4 * ROWS, 256), BF16),
            pltpu.VMEM((3, 128, 256), BF16),
            pltpu.VMEM((3, 256, 128), BF16),
            pltpu.VMEM((STREAMS, PART * PITCH_CLUSTER, 128), F32),
            pltpu.VMEM((STREAMS // TOGETHER, PART * TOGETHER * PITCH_BLOCK, 128), F32),
            pltpu.VMEM((STREAMS // TOGETHER, PART * TOGETHER * PITCH_BLOCK, 128), F32),
            pltpu.VMEM((STREAMS, 3, BLOCKS, WIDE), BF16),
            pltpu.VMEM((ROWS, 64), BF16),
            pltpu.VMEM((64, ROWS), BF16),
            pltpu.VMEM((2, STREAMS, 3, 4, 16, WIDE), BF16),
            pltpu.VMEM((2, STREAMS, 3, 4, ROWS, WIDE), BF16),
            pltpu.VMEM((2, STREAMS, 2, 3, GROUPS, SLOTS, WIDE), BF16),
            pltpu.VMEM((2, STREAMS, 2, 3, GROUPS, SLOTS, WIDE), BF16),
            pltpu.VMEM((2, STREAMS, 3, 4, ROWS, WIDE), BF16),
            pltpu.VMEM((2, STREAMS, 3, 3, ROWS, WIDE), BF16),
            pltpu.VMEM((2, STREAMS, 3, 4, 16, WIDE), BF16),
            pltpu.VMEM((2, STREAMS, 3, 3, 16, WIDE), BF16),
            pltpu.SemaphoreType.DMA((HALO + 1,)),
            pltpu.SemaphoreType.DMA((STREAMS, HALO + 1)),
            pltpu.SemaphoreType.DMA((1,)),
            pltpu.SemaphoreType.DMA((1,)),
            pltpu.SemaphoreType.DMA((8,)),
        ],
        compiler_params=pltpu.CompilerParams(
            collective_id=0, has_side_effects=True, vmem_limit_bytes=60 * 1024 * 1024
        ),
    )(charges, basis, transfer, near_field, jnp.transpose(coupling, (1, 2, 0)),
      ranks.reshape(1, 12), block_source.reshape(1, BLOCKS), block_target.reshape(1, BLOCKS))
    return both[0], both[1]


def solution(mesh):
    in_specs = (
        P("clu", None, None),
        P("clu", None, None),
        P("clu", None, None),
        P("clu", None, None, None),
        P("clu", None, None),
        P("clu"),
        P("clu"),
        P("clu"),
    )
    out_specs = (P("clu", None, None), P("clu", None, None))
    return jax.shard_map(local, mesh=mesh, in_specs=in_specs, out_specs=out_specs, check_vma=False)
```

```python
import jax
import jax.numpy as jnp
from jax import lax
from jax.experimental import pallas as pl
from jax.experimental.pallas import tpu as pltpu
from jax.sharding import PartitionSpec as P

MESH = pl.DeviceIdType.MESH
F32 = jnp.float32
BF16 = jnp.bfloat16
RMAX = 96
RHS = 32
STREAMS = 4
TOGETHER = 2
PART = RHS // STREAMS
QUADS = PART // 4
LEAF = 256
STRIDE = {"x": 32, "z": 8, "y": 2}
ROUTES = (("y", "x", "z"), ("z", "y", "x"), ("x", "z", "y"))
STEPS = (2, 1, -1)
WIDE = 128 * QUADS
GROUPS = 8
SLOTS = 32
BLOCKS = 128

G1, G2, EX, BACK, R2, R1, HALO = range(7)
ROWS = 48
PITCH_BLOCK, PITCH_CLUSTER, PITCH_TURN = 136, 24, 104


def dot(a, b):
    return jnp.dot(a, b, preferred_element_type=F32)


def dot_nt(a, b):
    return lax.dot_general(a, b, (((1,), (1,)), ((), ())), preferred_element_type=F32)


def iota(shape, dim):
    return lax.broadcasted_iota(jnp.int32, shape, dim)


def ones_where(hit):
    return jnp.where(hit, 1.0, 0.0).astype(F32)


def merge(row, extra, u):
    return jnp.where(iota(row.shape, 1) < RMAX, row, pltpu.roll(extra, RMAX - 32 * u, 1))


def fourth(parts):
    rolled = [pltpu.roll(part, 32 + 32 * u, 1) for u, part in enumerate(parts)]
    lanes = iota(parts[0].shape, 1)
    return jnp.where(lanes < 32, rolled[0], jnp.where(lanes < 64, rolled[1], rolled[2]))


def kernel(
    charges_hbm, basis_hbm, transfer_hbm, near_hbm, coupling_hbm, ranks_hbm, source_hbm, target_hbm,
    out,
    basis, transfer, near, turned, wide_coupling, coupling, v, lines_of, near_sum, ranks, block_source, block_target,
    mask, raw, raw_in, pick, scatter, unpick, place,
    small, big_in, big_out, products, compact, expand, gathered, packed, outbox, inbox, sums_out, sums_in, ends_out, ends_in,
    send_sem, recv_sem, list_send, list_recv, load_sem,
):
    me = lax.axis_index("clu")
    devices = 128
    core = lax.rem(me, 2)
    pos = {a: lax.rem(lax.div(me, s), 4) for a, s in STRIDE.items()}

    def near_by(axis, step, other=0):
        base = me + (lax.rem(pos[axis] + (step + 4), 4) - pos[axis]) * STRIDE[axis]
        return base + (1 - 2 * core) if other else base

    sibling = me + (1 - 2 * core)
    before = lax.rem(me + devices - 1, devices)
    after = lax.rem(me + 1, devices)

    barrier = pltpu.get_barrier_semaphore()
    peers = [sibling, before, after]
    for axis in STRIDE:
        for step in STEPS:
            for other in (0, 1):
                peers.append(near_by(axis, step, other))
    for peer in peers:
        pl.semaphore_signal(barrier, inc=1, device_id=(peer,), device_id_type=MESH)

    loads = [pltpu.make_async_copy(src, dst, load_sem.at[k]) for k, (src, dst) in enumerate((
        (charges_hbm, v.at[0, pl.ds(1, 8)]), (basis_hbm, basis), (transfer_hbm, transfer), (ranks_hbm, ranks),
        (source_hbm, block_source), (target_hbm, block_target), (coupling_hbm, turned), (near_hbm, near)))]
    for load in loads:
        load.start()
    load_coupling, load_near = loads[6:]
    small[...] = jnp.zeros_like(small)
    raw[...] = jnp.zeros_like(raw)

    def copy_of(h, k, src, dst, device):
        return pltpu.make_async_remote_copy(
            src_ref=src, dst_ref=dst, send_sem=send_sem.at[k], recv_sem=recv_sem.at[h, k],
            device_id=(device,), device_id_type=MESH)

    def arrived(h, k, where):
        copy_of(h, k, where, where, sibling).wait_recv()

    def sent(k, where):
        copy_of(0, k, where, where, sibling).wait_send()

    def coefficients(p, streams):
        masks = [mask[i : i + 1, :RMAX] for i in range(12)]
        fields = [jnp.concatenate([lines_of[h, i] for h in streams], axis=0).astype(BF16) for i in range(8)]
        leaves = [dot_nt(fields[i], basis[i]) for i in range(8)]
        leaves = [(c * m).astype(BF16) for c, m in zip(leaves, masks)]
        lifted = [dot(c, transfer[i]) for i, c in enumerate(leaves)]
        above = [((lifted[2 * q] + lifted[2 * q + 1]) * masks[8 + q]).astype(BF16) for q in range(4)]
        for i, c in enumerate(leaves + above):
            c = c.astype(F32)
            for k, h in enumerate(streams):
                small[h, pl.ds(i, PART, stride=PITCH_CLUSTER), 0:RMAX] = c[PART * k : PART * (k + 1)]
        for h in streams:
            for u in range(3):
                for g in range(QUADS):
                    row = small[h, pl.ds((4 * g + u) * PITCH_CLUSTER, 16), :]
                    extra = small[h, pl.ds((4 * g + 3) * PITCH_CLUSTER, 16), :]
                    gathered[p, h, u, 0, :, g * 128 : (g + 1) * 128] = merge(row, extra, u).astype(BF16)

    def halo_rows(h):
        return pl.ds(16 * (PART * h // 16), 16)

    def begin(p, h):
        for u, (axis, _, _) in enumerate(ROUTES):
            block = gathered.at[p, h, u]
            for step in STEPS:
                copy_of(h, G1, block.at[0], block.at[-step % 4], near_by(axis, step)).start()
        if PART * (h + 1) % 16 == 0:
            rows = halo_rows(h)
            copy_of(h, HALO, v.at[p, 1, rows], v.at[p, 9, rows], before).start()
            copy_of(h, HALO, v.at[p, 8, rows], v.at[p, 0, rows], after).start()

    def near_part(p, lo, hi):
        if lo == 0:
            for h in range(STREAMS):
                if PART * (h + 1) % 16 == 0:
                    arrived(h, HALO, v.at[p, pl.ds(0, 2), halo_rows(h)])
            v[p, 0] = (v[p, 0].astype(F32) * (me > 0).astype(F32)).astype(BF16)
            v[p, 9] = (v[p, 9].astype(F32) * (me < devices - 1).astype(F32)).astype(BF16)
        for i in range(lo, hi):
            s = dot(v[p, i], near[i, 0])
            s = s + dot(v[p, i + 1], near[i, 1])
            near_sum[i] = s + dot(v[p, i + 2], near[i, 2])

    list_copies = []
    for u, (_, _, axis) in enumerate(ROUTES):
        targets = [(near_by(axis, step, o), -step % 4 * 2 + o) for step in STEPS for o in (0, 1)] + [(sibling, 1)]
        for device, group in targets:
            list_copies.append(pltpu.make_async_remote_copy(
                src_ref=raw, dst_ref=raw_in.at[u, pl.ds(8 * group, 8)],
                send_sem=list_send.at[0], recv_sem=list_recv.at[0],
                device_id=(device,), device_id_type=MESH))

    def place_of(ids, route):
        first, second, axis = route
        device = lax.shift_right_logical(ids * 43691, 19)
        where = {a: (lax.shift_right_logical(device, n) + (4 - pos[a])) & 3 for a, n in (("x", 5), ("z", 3), ("y", 1))}
        group = where[axis] * 2 + ((device + core) & 1)
        return group, where[second] * ROWS + where[first] * 12 + (ids - 12 * device)

    ahead = ones_where(iota((128, 128), 0) < iota((128, 128), 1)).astype(BF16)

    def rows_wanted(u, k):
        within = iota((SLOTS, 128), 0).astype(F32)
        group, row = place_of(raw_in[u, pl.ds(k, 8, stride=8), :], ROUTES[u])
        rank = jnp.where(group == 0, dot(ones_where(group == 0).astype(BF16), ahead), -1.0)
        row = row.astype(F32) + 1.0
        wanted = []
        for q in range(GROUPS):
            mine = jnp.where(within == rank[q : q + 1, :], row[q : q + 1, :], 0.0)
            wanted.append(jnp.sum(mine, axis=1, keepdims=True))
        wanted = jnp.concatenate(wanted, axis=0) - 1.0
        return ones_where(iota((256, 4 * ROWS), 1).astype(F32) == wanted)

    def make_picks():
        for u in range(3):
            raw_in[u, 0:8, :] = raw[...]
            pick[u] = rows_wanted(u, 0).astype(BF16)

    def make_own():
        number = iota((256, 128), 0).astype(F32)
        for u, route in enumerate(ROUTES):
            group, _ = place_of(raw[...], route)
            slots = []
            for k in range(2):
                hit = ones_where(iota((8, 128), 0) == group[k : k + 1, :])
                rank = jnp.sum(hit * dot(hit.astype(BF16), ahead), axis=0, keepdims=True)
                slots.append(group[k : k + 1, :].astype(F32) * SLOTS + rank)
            unpick[u] = jnp.transpose(ones_where(number == slots[0]), (1, 0)).astype(BF16)
            place[u] = ones_where(number == slots[1]).astype(BF16)

    def make_sums():
        for u in range(3):
            scatter[u] = jnp.transpose(rows_wanted(u, 1), (1, 0)).astype(BF16)

    def turn():
        def body(n, carry):
            for k in range(32):
                row = 32 * n + k
                wide_coupling[pl.ds(row, BLOCKS, stride=PITCH_TURN), 0:RMAX] = jnp.transpose(turned[row].astype(F32), (1, 0))
            return carry

        lax.fori_loop(0, RMAX // 32, body, 0)

    def narrow():
        def body(n, carry):
            for k in range(8):
                j = 8 * n + k
                rows = pl.ds(pl.multiple_of(j * PITCH_TURN, 8), RMAX)
                coupling[j] = wide_coupling[rows, 0:RMAX].astype(BF16)
            return carry

        lax.fori_loop(0, BLOCKS // 8, body, 0)

    def exchange(p, h, way, u):
        axis = ROUTES[u][2]
        box, to = outbox.at[p, h, way, u], inbox.at[p, h, way, u]
        targets = [(near_by(axis, step, o), step % 4 * 2 + o, -step % 4 * 2 + o) for step in STEPS for o in (0, 1)]
        for device, src, dst in targets + [(sibling, 1, 1)]:
            copy_of(h, BACK if way else EX, box.at[src], to.at[dst], device).start()

    def fill_boxes(p, h, way, u, selector, rows):
        for n in range(0, WIDE, 256):
            cols = slice(n, n + 256)
            boxes = dot(selector, rows[:, cols]).astype(BF16).reshape(GROUPS, SLOTS, 256)
            outbox[p, h, way, u, 1:GROUPS, :, cols] = boxes[1:GROUPS]
            inbox[p, h, way, u, 0, :, cols] = boxes[0]

    def exchanged(p, h, way):
        arrived(h, BACK if way else EX, inbox.at[p, h, way, :, pl.ds(1, 7)])

    def line_copies(h, k, out, into, axis):
        for s, step in enumerate(STEPS):
            copy_of(h, k, out.at[step % 4], into.at[s], near_by(axis, step)).start()

    def stream(p, h):
        arrived(h, G1, gathered.at[p, h, :, pl.ds(1, 3)])
        for u in range(3):
            packed[p, h, u, 0] = dot(compact[...], gathered[p, h, u].reshape(64, WIDE)).astype(BF16)
        for u, (_, axis, _) in enumerate(ROUTES):
            plane = packed.at[p, h, u]
            for step in STEPS:
                copy_of(h, G2, plane.at[0], plane.at[-step % 4], near_by(axis, step)).start()
        yield
        arrived(h, G2, packed.at[p, h, :, pl.ds(1, 3)])
        for u in range(3):
            fill_boxes(p, h, 0, u, pick[u], packed[p, h, u].reshape(4 * ROWS, WIDE))
        for u in range(3):
            exchange(p, h, 0, u)
        yield
        batch, first_row = h // TOGETHER, PART * (h % TOGETHER)
        exchanged(p, h, 0)

        for n in range(0, WIDE, 256):
            parts = [dot(unpick[u], inbox[p, h, 0, u, :, :, n : n + 256].reshape(256, 256)) for u in range(3)]
            for k in range(2):
                g = n // 128 + k
                sides = [part[:, k * 128 : (k + 1) * 128] for part in parts]
                for k, side in enumerate(sides + [fourth(sides)]):
                    big_in[batch, pl.ds((first_row + 4 * g + k) * PITCH_BLOCK, BLOCKS), :] = side

        if (h + 1) % TOGETHER == 0:
            lines_at_once = PART * TOGETHER
            for j in range(BLOCKS):
                x = big_in[batch, pl.ds(j, lines_at_once, stride=PITCH_BLOCK), 0:RMAX].astype(BF16)
                big_out[batch, pl.ds(j, lines_at_once, stride=PITCH_BLOCK), 0:RMAX] = dot(x, coupling[j])
            for k in range(h + 1 - TOGETHER, h + 1):
                for g in range(QUADS):
                    row = PART * (k % TOGETHER) + 4 * g
                    parts = [big_out[batch, pl.ds((row + u) * PITCH_BLOCK, BLOCKS), :] for u in range(4)]
                    for u in range(3):
                        products[k, u, :, g * 128 : (g + 1) * 128] = merge(parts[u], parts[3], u).astype(BF16)
                for u in range(3):
                    fill_boxes(p, k, 1, u, place[u], products[k, u])
                for u in range(3):
                    exchange(p, k, 1, u)
        yield
        exchanged(p, h, 1)
        for u in range(3):
            for n in range(0, WIDE, 256):
                rows = inbox[p, h, 1, u, :, :, n : n + 256].reshape(256, 256)
                sums_out[p, h, u, :, :, n : n + 256] = dot(scatter[u], rows).astype(BF16).reshape(4, ROWS, 256)
        for u, (_, axis, _) in enumerate(ROUTES):
            line_copies(h, R2, sums_out.at[p, h, u], sums_in.at[p, h, u], axis)
        yield
        arrived(h, R2, sums_in.at[p, h])
        for u in range(3):
            s = sums_out[p, h, u, 0].astype(F32)
            for n in range(3):
                s = s + sums_in[p, h, u, n].astype(F32)
            ends_out[p, h, u] = dot(expand[...], s.astype(BF16)).astype(BF16).reshape(4, 16, WIDE)
        for u, (axis, _, _) in enumerate(ROUTES):
            line_copies(h, R1, ends_out.at[p, h, u], ends_in.at[p, h, u], axis)
        yield
        sides = []
        arrived(h, R1, ends_in.at[p, h])
        for u in range(3):
            s = ends_out[p, h, u, 0].astype(F32)
            for n in range(3):
                s = s + ends_in[p, h, u, n].astype(F32)
            sides.append(s)
        for g in range(QUADS):
            here = [s[:, g * 128 : (g + 1) * 128] for s in sides]
            for u in range(3):
                small[h, pl.ds((4 * g + u) * PITCH_CLUSTER, 16), :] = here[u]
            small[h, pl.ds((4 * g + 3) * PITCH_CLUSTER, 16), :] = fourth(here)
        lines = pl.ds(PART * h, PART)
        masks = [mask[i : i + 1, :RMAX] for i in range(12)]
        fields = [(small[h, pl.ds(i, PART, stride=PITCH_CLUSTER), 0:RMAX] * masks[i]).astype(BF16) for i in range(12)]
        downs = [dot_nt(fields[8 + i // 2], transfer[i]) for i in range(8)]
        leaves = [((fields[i].astype(F32) + downs[i]) * masks[i]).astype(BF16) for i in range(8)]
        fars = [dot(leaves[i], basis[i]) for i in range(8)]
        fars = [(near_sum[i, lines] + fars[i]).astype(BF16) for i in range(8)]
        for i in range(8):
            lines_of[h, i] = fars[i].astype(F32)
        if PART * (h + 1) % 16 == 0:
            for i in range(8):
                parts = [lines_of[k, i] for k in range(h + 1 - 16 // PART, h + 1)]
                v[p + 1, 1 + i, halo_rows(h)] = jnp.concatenate(parts, axis=0).astype(BF16)

        if p == 0:
            coefficients(1, [h])
            begin(1, h)
        yield

    for load in loads[:6]:
        load.wait()
    raw[0:1, :] = block_source[...]
    raw[1:2, :] = block_target[...]
    for i in range(12):
        mask[i : i + 1, :] = ones_where(iota((1, 128), 1) < ranks[0:1, i : i + 1])
    for i in range(8):
        whole = v[0, 1 + i].astype(F32)
        for h in range(STREAMS):
            lines_of[h, i] = whole[PART * h : PART * (h + 1)]
    coefficients(0, range(STREAMS))
    column, line = iota((ROWS, 64), 1), iota((ROWS, 64), 0)
    same = lax.shift_right_logical(column, 4) * 12 + (column & 15) == line
    compact[...] = ones_where(same & ((column & 15) < 12)).astype(BF16)
    column, line = iota((64, ROWS), 0), iota((64, ROWS), 1)
    same = lax.shift_right_logical(column, 4) * 12 + (column & 15) == line
    expand[...] = ones_where(same & ((column & 15) < 12)).astype(BF16)
    pl.semaphore_wait(barrier, len(peers))
    for h in range(STREAMS):
        begin(0, h)
    for copy in list_copies:
        copy.start()
    make_own()
    load_coupling.wait()
    turn()

    for p in range(2):
        streams = [stream(p, h) for h in range(STREAMS)]

        def both():
            for s in streams:
                next(s)

        both()
        if p == 0:
            tiles_in = raw_in.at[:, pl.ds(8, 56)]
            pltpu.make_async_remote_copy(
                src_ref=tiles_in, dst_ref=tiles_in, send_sem=list_send.at[0], recv_sem=list_recv.at[0],
                device_id=(sibling,), device_id_type=MESH).wait()
            make_picks()
        else:
            near_part(p, 0, 4)
        both()
        if p == 0:
            make_sums()
            narrow()
            load_near.wait()
            near_part(p, 0, 4)
        near_part(p, 4, 8)
        both()
        both()
        both()
        both()
    out[...] = v[1:3, 1:9]
    sent(G1, gathered.at[:, :, :, pl.ds(1, 3)])
    sent(G2, packed.at[:, :, :, pl.ds(1, 3)])
    sent(EX, inbox.at[:, :, 0, :, pl.ds(1, 7)])
    sent(BACK, inbox.at[:, :, 1, :, pl.ds(1, 7)])
    sent(R2, sums_in)
    sent(R1, ends_in)
    sent(HALO, v.at[0, pl.ds(0, 4)])


def local(charges, basis, transfer, near_field, coupling, ranks, block_source, block_target):
    vmem = pl.BlockSpec(memory_space=pltpu.VMEM)
    hbm = pl.BlockSpec(memory_space=pl.ANY)
    both = pl.pallas_call(
        kernel,
        out_shape=jax.ShapeDtypeStruct((2, 8, RHS, LEAF), BF16),
        in_specs=[hbm] * 8,
        out_specs=vmem,
        scratch_shapes=[
            pltpu.VMEM((8, RMAX, LEAF), BF16),
            pltpu.VMEM((8, RMAX, RMAX), BF16),
            pltpu.VMEM((8, 3, LEAF, LEAF), BF16),
            pltpu.VMEM((RMAX, RMAX, BLOCKS), BF16),
            pltpu.VMEM(((BLOCKS + 1) * PITCH_TURN, 128), F32),
            pltpu.VMEM((BLOCKS, RMAX, RMAX), BF16),
            pltpu.VMEM((3, 10, RHS, LEAF), BF16),
            pltpu.VMEM((STREAMS, 8, PART, LEAF), F32),
            pltpu.VMEM((8, RHS, LEAF), F32),
            pltpu.VMEM((1, 12), jnp.int32),
            pltpu.VMEM((1, BLOCKS), jnp.int32),
            pltpu.VMEM((1, BLOCKS), jnp.int32),
            pltpu.VMEM((16, 128), F32),
            pltpu.VMEM((8, 128), jnp.int32),
            pltpu.VMEM((3, 72, 128), jnp.int32),
            pltpu.VMEM((3, 256, 4 * ROWS), BF16),
            pltpu.VMEM((3, 4 * ROWS, 256), BF16),
            pltpu.VMEM((3, 128, 256), BF16),
            pltpu.VMEM((3, 256, 128), BF16),
            pltpu.VMEM((STREAMS, (PART + 1) * PITCH_CLUSTER, 128), F32),
            pltpu.VMEM((STREAMS // TOGETHER, (PART * TOGETHER + 1) * PITCH_BLOCK, 128), F32),
            pltpu.VMEM((STREAMS // TOGETHER, (PART * TOGETHER + 1) * PITCH_BLOCK, 128), F32),
            pltpu.VMEM((STREAMS, 3, BLOCKS, WIDE), BF16),
            pltpu.VMEM((ROWS, 64), BF16),
            pltpu.VMEM((64, ROWS), BF16),
            pltpu.VMEM((2, STREAMS, 3, 4, 16, WIDE), BF16),
            pltpu.VMEM((2, STREAMS, 3, 4, ROWS, WIDE), BF16),
            pltpu.VMEM((2, STREAMS, 2, 3, GROUPS, SLOTS, WIDE), BF16),
            pltpu.VMEM((2, STREAMS, 2, 3, GROUPS, SLOTS, WIDE), BF16),
            pltpu.VMEM((2, STREAMS, 3, 4, ROWS, WIDE), BF16),
            pltpu.VMEM((2, STREAMS, 3, 3, ROWS, WIDE), BF16),
            pltpu.VMEM((2, STREAMS, 3, 4, 16, WIDE), BF16),
            pltpu.VMEM((2, STREAMS, 3, 3, 16, WIDE), BF16),
            pltpu.SemaphoreType.DMA((HALO + 1,)),
            pltpu.SemaphoreType.DMA((STREAMS, HALO + 1)),
            pltpu.SemaphoreType.DMA((1,)),
            pltpu.SemaphoreType.DMA((1,)),
            pltpu.SemaphoreType.DMA((8,)),
        ],
        compiler_params=pltpu.CompilerParams(
            collective_id=0, has_side_effects=True, vmem_limit_bytes=60 * 1024 * 1024
        ),
    )(charges, basis, transfer, near_field, jnp.transpose(coupling, (1, 2, 0)),
      ranks.reshape(1, 12), block_source.reshape(1, BLOCKS), block_target.reshape(1, BLOCKS))
    return both[0], both[1]


def solution(mesh):
    in_specs = (
        P("clu", None, None),
        P("clu", None, None),
        P("clu", None, None),
        P("clu", None, None, None),
        P("clu", None, None),
        P("clu"),
        P("clu"),
        P("clu"),
    )
    out_specs = (P("clu", None, None), P("clu", None, None))
    return jax.shard_map(local, mesh=mesh, in_specs=in_specs, out_specs=out_specs, check_vma=False)
```

```python
import jax
import jax.numpy as jnp
from jax import lax
from jax.experimental import pallas as pl
from jax.experimental.pallas import tpu as pltpu
from jax.sharding import PartitionSpec as P

MESH = pl.DeviceIdType.MESH
F32 = jnp.float32
BF16 = jnp.bfloat16
RMAX = 96
RHS = 32
STREAMS = 4
TOGETHER = 2
PART = RHS // STREAMS
QUADS = PART // 4
LEAF = 256
STRIDE = {"x": 32, "z": 8, "y": 2}
ROUTES = (("y", "x", "z"), ("z", "y", "x"), ("x", "z", "y"))
STEPS = (2, 1, -1)
WIDE = 128 * QUADS
GROUPS = 8
SLOTS = 32
BLOCKS = 128

G1, G2, EX, BACK, R2, R1, HALO = range(7)
ROWS = 48
PITCH_BLOCK, PITCH_CLUSTER, PITCH_TURN = 136, 24, 104


def dot(a, b):
    return jnp.dot(a, b, preferred_element_type=F32)


def dot_nt(a, b):
    return lax.dot_general(a, b, (((1,), (1,)), ((), ())), preferred_element_type=F32)


def iota(shape, dim):
    return lax.broadcasted_iota(jnp.int32, shape, dim)


def ones_where(hit):
    return jnp.where(hit, 1.0, 0.0).astype(F32)


def merge(row, extra, u):
    return jnp.where(iota(row.shape, 1) < RMAX, row, pltpu.roll(extra, RMAX - 32 * u, 1))


def fourth(parts):
    rolled = [pltpu.roll(part, 32 + 32 * u, 1) for u, part in enumerate(parts)]
    lanes = iota(parts[0].shape, 1)
    return jnp.where(lanes < 32, rolled[0], jnp.where(lanes < 64, rolled[1], rolled[2]))


def kernel(
    charges_hbm, basis_hbm, transfer_hbm, near_hbm, coupling_hbm, ranks_hbm, source_hbm, target_hbm,
    out,
    basis, transfer, near, turned, wide_coupling, coupling, v, lines_of, near_sum, ranks, block_source, block_target,
    mask, raw, raw_in, pick, scatter, unpick, place,
    small, big_in, big_out, products, compact, expand, gathered, packed, outbox, inbox, sums_out, sums_in, ends_out, ends_in,
    send_sem, recv_sem, list_send, list_recv, load_sem,
):
    me = lax.axis_index("clu")
    devices = 128
    core = lax.rem(me, 2)
    pos = {a: lax.rem(lax.div(me, s), 4) for a, s in STRIDE.items()}

    def near_by(axis, step, other=0):
        base = me + (lax.rem(pos[axis] + (step + 4), 4) - pos[axis]) * STRIDE[axis]
        return base + (1 - 2 * core) if other else base

    sibling = me + (1 - 2 * core)
    before = lax.rem(me + devices - 1, devices)
    after = lax.rem(me + 1, devices)

    barrier = pltpu.get_barrier_semaphore()
    peers = [sibling, before, after]
    for axis in STRIDE:
        for step in STEPS:
            for other in (0, 1):
                peers.append(near_by(axis, step, other))
    for peer in peers:
        pl.semaphore_signal(barrier, inc=1, device_id=(peer,), device_id_type=MESH)

    loads = [pltpu.make_async_copy(src, dst, load_sem.at[k]) for k, (src, dst) in enumerate((
        (charges_hbm, v.at[0, pl.ds(1, 8)]), (basis_hbm, basis), (transfer_hbm, transfer), (ranks_hbm, ranks),
        (source_hbm, block_source), (target_hbm, block_target), (coupling_hbm, turned), (near_hbm, near)))]
    for load in loads:
        load.start()
    load_coupling, load_near = loads[6:]
    small[...] = jnp.zeros_like(small)
    raw[...] = jnp.zeros_like(raw)

    def copy_of(h, k, src, dst, device):
        return pltpu.make_async_remote_copy(
            src_ref=src, dst_ref=dst, send_sem=send_sem.at[k], recv_sem=recv_sem.at[h, k],
            device_id=(device,), device_id_type=MESH)

    def arrived(h, k, where):
        copy_of(h, k, where, where, sibling).wait_recv()

    def sent(k, where):
        copy_of(0, k, where, where, sibling).wait_send()

    def coefficients(p, streams):
        masks = [mask[i : i + 1, :RMAX] for i in range(12)]
        fields = [jnp.concatenate([lines_of[h, i] for h in streams], axis=0).astype(BF16) for i in range(8)]
        leaves = [dot_nt(fields[i], basis[i]) for i in range(8)]
        leaves = [(c * m).astype(BF16) for c, m in zip(leaves, masks)]
        lifted = [dot(c, transfer[i]) for i, c in enumerate(leaves)]
        above = [((lifted[2 * q] + lifted[2 * q + 1]) * masks[8 + q]).astype(BF16) for q in range(4)]
        for i, c in enumerate(leaves + above):
            c = c.astype(F32)
            for k, h in enumerate(streams):
                small[h, pl.ds(i, PART, stride=PITCH_CLUSTER), 0:RMAX] = c[PART * k : PART * (k + 1)]
        for h in streams:
            for u in range(3):
                for g in range(QUADS):
                    row = small[h, pl.ds((4 * g + u) * PITCH_CLUSTER, 16), :]
                    extra = small[h, pl.ds((4 * g + 3) * PITCH_CLUSTER, 16), :]
                    gathered[p, h, u, 0, :, g * 128 : (g + 1) * 128] = merge(row, extra, u).astype(BF16)

    def halo_rows(h):
        return pl.ds(16 * (PART * h // 16), 16)

    def begin(p, h):
        for u, (axis, _, _) in enumerate(ROUTES):
            block = gathered.at[p, h, u]
            for step in STEPS:
                copy_of(h, G1, block.at[0], block.at[-step % 4], near_by(axis, step)).start()
        if PART * (h + 1) % 16 == 0:
            rows = halo_rows(h)
            copy_of(h, HALO, v.at[p, 1, rows], v.at[p, 9, rows], before).start()
            copy_of(h, HALO, v.at[p, 8, rows], v.at[p, 0, rows], after).start()

    def near_part(p, lo, hi):
        if lo == 0:
            for h in range(STREAMS):
                if PART * (h + 1) % 16 == 0:
                    arrived(h, HALO, v.at[p, pl.ds(0, 2), halo_rows(h)])
            v[p, 0] = (v[p, 0].astype(F32) * (me > 0).astype(F32)).astype(BF16)
            v[p, 9] = (v[p, 9].astype(F32) * (me < devices - 1).astype(F32)).astype(BF16)
        for i in range(lo, hi):
            s = dot(v[p, i], near[i, 0])
            s = s + dot(v[p, i + 1], near[i, 1])
            near_sum[i] = s + dot(v[p, i + 2], near[i, 2])

    list_copies = []
    for u, (_, _, axis) in enumerate(ROUTES):
        targets = [(near_by(axis, step, o), -step % 4 * 2 + o) for step in STEPS for o in (0, 1)] + [(sibling, 1)]
        for device, group in targets:
            list_copies.append(pltpu.make_async_remote_copy(
                src_ref=raw, dst_ref=raw_in.at[u, pl.ds(8 * group, 8)],
                send_sem=list_send.at[0], recv_sem=list_recv.at[0],
                device_id=(device,), device_id_type=MESH))

    def place_of(ids, route):
        first, second, axis = route
        device = lax.shift_right_logical(ids * 43691, 19)
        where = {a: (lax.shift_right_logical(device, n) + (4 - pos[a])) & 3 for a, n in (("x", 5), ("z", 3), ("y", 1))}
        group = where[axis] * 2 + ((device + core) & 1)
        return group, where[second] * ROWS + where[first] * 12 + (ids - 12 * device)

    ahead = ones_where(iota((128, 128), 0) < iota((128, 128), 1)).astype(BF16)

    def rows_wanted(u, k):
        within = iota((SLOTS, 128), 0).astype(F32)
        group, row = place_of(raw_in[u, pl.ds(k, 8, stride=8), :], ROUTES[u])
        rank = jnp.where(group == 0, dot(ones_where(group == 0).astype(BF16), ahead), -1.0)
        row = row.astype(F32) + 1.0
        wanted = []
        for q in range(GROUPS):
            mine = jnp.where(within == rank[q : q + 1, :], row[q : q + 1, :], 0.0)
            wanted.append(jnp.sum(mine, axis=1, keepdims=True))
        wanted = jnp.concatenate(wanted, axis=0) - 1.0
        return ones_where(iota((256, 4 * ROWS), 1).astype(F32) == wanted)

    def make_picks():
        for u in range(3):
            raw_in[u, 0:8, :] = raw[...]
            pick[u] = rows_wanted(u, 0).astype(BF16)

    def make_own():
        number = iota((256, 128), 0).astype(F32)
        for u, route in enumerate(ROUTES):
            group, _ = place_of(raw[...], route)
            slots = []
            for k in range(2):
                hit = ones_where(iota((8, 128), 0) == group[k : k + 1, :])
                rank = jnp.sum(hit * dot(hit.astype(BF16), ahead), axis=0, keepdims=True)
                slots.append(group[k : k + 1, :].astype(F32) * SLOTS + rank)
            unpick[u] = jnp.transpose(ones_where(number == slots[0]), (1, 0)).astype(BF16)
            place[u] = ones_where(number == slots[1]).astype(BF16)

    def make_sums():
        for u in range(3):
            scatter[u] = jnp.transpose(rows_wanted(u, 1), (1, 0)).astype(BF16)

    def turn():
        def body(n, carry):
            for k in range(32):
                row = 32 * n + k
                wide_coupling[pl.ds(row, BLOCKS, stride=PITCH_TURN), 0:RMAX] = jnp.transpose(turned[row].astype(F32), (1, 0))
            return carry

        lax.fori_loop(0, RMAX // 32, body, 0)

    def narrow():
        def body(n, carry):
            for k in range(8):
                j = 8 * n + k
                rows = pl.ds(pl.multiple_of(j * PITCH_TURN, 8), RMAX)
                coupling[j] = wide_coupling[rows, 0:RMAX].astype(BF16)
            return carry

        lax.fori_loop(0, BLOCKS // 8, body, 0)

    def exchange(p, h, way, u):
        axis = ROUTES[u][2]
        box, to = outbox.at[p, h, way, u], inbox.at[p, h, way, u]
        targets = [(near_by(axis, step, o), step % 4 * 2 + o, -step % 4 * 2 + o) for step in STEPS for o in (0, 1)]
        for device, src, dst in targets + [(sibling, 1, 1)]:
            copy_of(h, BACK if way else EX, box.at[src], to.at[dst], device).start()

    def fill_boxes(p, h, way, u, selector, rows):
        for n in range(0, WIDE, 256):
            cols = slice(n, n + 256)
            boxes = dot(selector, rows[:, cols]).astype(BF16).reshape(GROUPS, SLOTS, 256)
            outbox[p, h, way, u, 1:GROUPS, :, cols] = boxes[1:GROUPS]
            inbox[p, h, way, u, 0, :, cols] = boxes[0]

    def exchanged(p, h, way):
        arrived(h, BACK if way else EX, inbox.at[p, h, way, :, pl.ds(1, 7)])

    def line_copies(h, k, out, into, axis):
        for s, step in enumerate(STEPS):
            copy_of(h, k, out.at[step % 4], into.at[s], near_by(axis, step)).start()

    def stream(p, h):
        arrived(h, G1, gathered.at[p, h, :, pl.ds(1, 3)])
        for u in range(3):
            packed[p, h, u, 0] = dot(compact[...], gathered[p, h, u].reshape(64, WIDE)).astype(BF16)
        for u, (_, axis, _) in enumerate(ROUTES):
            plane = packed.at[p, h, u]
            for step in STEPS:
                copy_of(h, G2, plane.at[0], plane.at[-step % 4], near_by(axis, step)).start()
        yield
        arrived(h, G2, packed.at[p, h, :, pl.ds(1, 3)])
        for u in range(3):
            fill_boxes(p, h, 0, u, pick[u], packed[p, h, u].reshape(4 * ROWS, WIDE))
        for u in range(3):
            exchange(p, h, 0, u)
        yield
        batch, first_row = h // TOGETHER, PART * (h % TOGETHER)
        exchanged(p, h, 0)

        for n in range(0, WIDE, 256):
            parts = [dot(unpick[u], inbox[p, h, 0, u, :, :, n : n + 256].reshape(256, 256)) for u in range(3)]
            for k in range(2):
                g = n // 128 + k
                sides = [part[:, k * 128 : (k + 1) * 128] for part in parts]
                for k, side in enumerate(sides + [fourth(sides)]):
                    big_in[batch, pl.ds((first_row + 4 * g + k) * PITCH_BLOCK, BLOCKS), :] = side

        if (h + 1) % TOGETHER == 0:
            lines_at_once = PART * TOGETHER
            for j in range(BLOCKS):
                x = big_in[batch, pl.ds(j, lines_at_once, stride=PITCH_BLOCK), 0:RMAX].astype(BF16)
                big_out[batch, pl.ds(j, lines_at_once, stride=PITCH_BLOCK), 0:RMAX] = dot(x, coupling[j])
            for k in range(h + 1 - TOGETHER, h + 1):
                for g in range(QUADS):
                    row = PART * (k % TOGETHER) + 4 * g
                    parts = [big_out[batch, pl.ds((row + u) * PITCH_BLOCK, BLOCKS), :] for u in range(4)]
                    for u in range(3):
                        products[k, u, :, g * 128 : (g + 1) * 128] = merge(parts[u], parts[3], u).astype(BF16)
                for u in range(3):
                    fill_boxes(p, k, 1, u, place[u], products[k, u])
                for u in range(3):
                    exchange(p, k, 1, u)
        yield
        exchanged(p, h, 1)
        for u in range(3):
            for n in range(0, WIDE, 256):
                rows = inbox[p, h, 1, u, :, :, n : n + 256].reshape(256, 256)
                sums_out[p, h, u, :, :, n : n + 256] = dot(scatter[u], rows).astype(BF16).reshape(4, ROWS, 256)
        for u, (_, axis, _) in enumerate(ROUTES):
            line_copies(h, R2, sums_out.at[p, h, u], sums_in.at[p, h, u], axis)
        yield
        arrived(h, R2, sums_in.at[p, h])
        for u in range(3):
            s = sums_out[p, h, u, 0].astype(F32)
            for n in range(3):
                s = s + sums_in[p, h, u, n].astype(F32)
            ends_out[p, h, u] = dot(expand[...], s.astype(BF16)).astype(BF16).reshape(4, 16, WIDE)
        for u, (axis, _, _) in enumerate(ROUTES):
            line_copies(h, R1, ends_out.at[p, h, u], ends_in.at[p, h, u], axis)
        yield
        sides = []
        arrived(h, R1, ends_in.at[p, h])
        for u in range(3):
            s = ends_out[p, h, u, 0].astype(F32)
            for n in range(3):
                s = s + ends_in[p, h, u, n].astype(F32)
            sides.append(s)
        for g in range(QUADS):
            here = [s[:, g * 128 : (g + 1) * 128] for s in sides]
            for u in range(3):
                small[h, pl.ds((4 * g + u) * PITCH_CLUSTER, 16), :] = here[u]
            small[h, pl.ds((4 * g + 3) * PITCH_CLUSTER, 16), :] = fourth(here)
        lines = pl.ds(PART * h, PART)
        masks = [mask[i : i + 1, :RMAX] for i in range(12)]
        fields = [(small[h, pl.ds(i, PART, stride=PITCH_CLUSTER), 0:RMAX] * masks[i]).astype(BF16) for i in range(12)]
        downs = [dot_nt(fields[8 + i // 2], transfer[i]) for i in range(8)]
        leaves = [((fields[i].astype(F32) + downs[i]) * masks[i]).astype(BF16) for i in range(8)]
        fars = [dot(leaves[i], basis[i]) for i in range(8)]
        fars = [(near_sum[i, lines] + fars[i]).astype(BF16) for i in range(8)]
        for i in range(8):
            lines_of[h, i] = fars[i].astype(F32)
        if PART * (h + 1) % 16 == 0:
            for i in range(8):
                parts = [lines_of[k, i] for k in range(h + 1 - 16 // PART, h + 1)]
                v[p + 1, 1 + i, halo_rows(h)] = jnp.concatenate(parts, axis=0).astype(BF16)

        if p == 0:
            coefficients(1, [h])
            begin(1, h)
        yield

    for load in loads[:6]:
        load.wait()
    raw[0:1, :] = block_source[...]
    raw[1:2, :] = block_target[...]
    for i in range(12):
        mask[i : i + 1, :] = ones_where(iota((1, 128), 1) < ranks[0:1, i : i + 1])
    for i in range(8):
        whole = v[0, 1 + i].astype(F32)
        for h in range(STREAMS):
            lines_of[h, i] = whole[PART * h : PART * (h + 1)]
    coefficients(0, range(STREAMS))
    column, line = iota((ROWS, 64), 1), iota((ROWS, 64), 0)
    same = lax.shift_right_logical(column, 4) * 12 + (column & 15) == line
    compact[...] = ones_where(same & ((column & 15) < 12)).astype(BF16)
    column, line = iota((64, ROWS), 0), iota((64, ROWS), 1)
    same = lax.shift_right_logical(column, 4) * 12 + (column & 15) == line
    expand[...] = ones_where(same & ((column & 15) < 12)).astype(BF16)
    pl.semaphore_wait(barrier, len(peers))
    for h in range(STREAMS):
        begin(0, h)
    for copy in list_copies:
        copy.start()
    make_own()
    load_coupling.wait()
    turn()
    narrow()
    load_near.wait()

    for p in range(2):
        streams = [stream(p, h) for h in range(STREAMS)]

        def both():
            for s in streams:
                next(s)

        both()
        if p == 0:
            tiles_in = raw_in.at[:, pl.ds(8, 56)]
            pltpu.make_async_remote_copy(
                src_ref=tiles_in, dst_ref=tiles_in, send_sem=list_send.at[0], recv_sem=list_recv.at[0],
                device_id=(sibling,), device_id_type=MESH).wait()
            make_picks()
        near_part(p, 0, 4)
        both()
        if p == 0:
            make_sums()
        near_part(p, 4, 8)
        both()
        both()
        both()
        both()
    out[...] = v[1:3, 1:9]
    sent(G1, gathered.at[:, :, :, pl.ds(1, 3)])
    sent(G2, packed.at[:, :, :, pl.ds(1, 3)])
    sent(EX, inbox.at[:, :, 0, :, pl.ds(1, 7)])
    sent(BACK, inbox.at[:, :, 1, :, pl.ds(1, 7)])
    sent(R2, sums_in)
    sent(R1, ends_in)
    sent(HALO, v.at[0, pl.ds(0, 4)])


def local(charges, basis, transfer, near_field, coupling, ranks, block_source, block_target):
    vmem = pl.BlockSpec(memory_space=pltpu.VMEM)
    hbm = pl.BlockSpec(memory_space=pl.ANY)
    both = pl.pallas_call(
        kernel,
        out_shape=jax.ShapeDtypeStruct((2, 8, RHS, LEAF), BF16),
        in_specs=[hbm] * 8,
        out_specs=vmem,
        scratch_shapes=[
            pltpu.VMEM((8, RMAX, LEAF), BF16),
            pltpu.VMEM((8, RMAX, RMAX), BF16),
            pltpu.VMEM((8, 3, LEAF, LEAF), BF16),
            pltpu.VMEM((RMAX, RMAX, BLOCKS), BF16),
            pltpu.VMEM(((BLOCKS + 1) * PITCH_TURN, 128), F32),
            pltpu.VMEM((BLOCKS, RMAX, RMAX), BF16),
            pltpu.VMEM((3, 10, RHS, LEAF), BF16),
            pltpu.VMEM((STREAMS, 8, PART, LEAF), F32),
            pltpu.VMEM((8, RHS, LEAF), F32),
            pltpu.VMEM((1, 12), jnp.int32),
            pltpu.VMEM((1, BLOCKS), jnp.int32),
            pltpu.VMEM((1, BLOCKS), jnp.int32),
            pltpu.VMEM((16, 128), F32),
            pltpu.VMEM((8, 128), jnp.int32),
            pltpu.VMEM((3, 72, 128), jnp.int32),
            pltpu.VMEM((3, 256, 4 * ROWS), BF16),
            pltpu.VMEM((3, 4 * ROWS, 256), BF16),
            pltpu.VMEM((3, 128, 256), BF16),
            pltpu.VMEM((3, 256, 128), BF16),
            pltpu.VMEM((STREAMS, (PART + 1) * PITCH_CLUSTER, 128), F32),
            pltpu.VMEM((STREAMS // TOGETHER, (PART * TOGETHER + 1) * PITCH_BLOCK, 128), F32),
            pltpu.VMEM((STREAMS // TOGETHER, (PART * TOGETHER + 1) * PITCH_BLOCK, 128), F32),
            pltpu.VMEM((STREAMS, 3, BLOCKS, WIDE), BF16),
            pltpu.VMEM((ROWS, 64), BF16),
            pltpu.VMEM((64, ROWS), BF16),
            pltpu.VMEM((2, STREAMS, 3, 4, 16, WIDE), BF16),
            pltpu.VMEM((2, STREAMS, 3, 4, ROWS, WIDE), BF16),
            pltpu.VMEM((2, STREAMS, 2, 3, GROUPS, SLOTS, WIDE), BF16),
            pltpu.VMEM((2, STREAMS, 2, 3, GROUPS, SLOTS, WIDE), BF16),
            pltpu.VMEM((2, STREAMS, 3, 4, ROWS, WIDE), BF16),
            pltpu.VMEM((2, STREAMS, 3, 3, ROWS, WIDE), BF16),
            pltpu.VMEM((2, STREAMS, 3, 4, 16, WIDE), BF16),
            pltpu.VMEM((2, STREAMS, 3, 3, 16, WIDE), BF16),
            pltpu.SemaphoreType.DMA((HALO + 1,)),
            pltpu.SemaphoreType.DMA((STREAMS, HALO + 1)),
            pltpu.SemaphoreType.DMA((1,)),
            pltpu.SemaphoreType.DMA((1,)),
            pltpu.SemaphoreType.DMA((8,)),
        ],
        compiler_params=pltpu.CompilerParams(
            collective_id=0, has_side_effects=True, vmem_limit_bytes=60 * 1024 * 1024
        ),
    )(charges, basis, transfer, near_field, jnp.transpose(coupling, (1, 2, 0)),
      ranks.reshape(1, 12), block_source.reshape(1, BLOCKS), block_target.reshape(1, BLOCKS))
    return both[0], both[1]


def solution(mesh):
    in_specs = (
        P("clu", None, None),
        P("clu", None, None),
        P("clu", None, None),
        P("clu", None, None, None),
        P("clu", None, None),
        P("clu"),
        P("clu"),
        P("clu"),
    )
    out_specs = (P("clu", None, None), P("clu", None, None))
    return jax.shard_map(local, mesh=mesh, in_specs=in_specs, out_specs=out_specs, check_vma=False)
```
